32 devices in a mesh: dp: 4 (over x, core), ctx: 2 (over y), tensor: 4 (over z).
Axes of the slice: x: 2, y: 2, z: 4, core: 2. Of those that a mesh axis runs over, the one named last changes fastest.
Arguments:
- hidden_in: bfloat16 [4, 1024, 1536], P('dp', 'ctx'), may hold values from -6 to 6
- segment_ids: int32 [4, 1024], P('dp'), may hold values from 0 to 5, never falling along the last dimension, each value on 1 to 512 neighbouring positions
- out_grad: bfloat16 [4, 1024, 1536], P('dp', 'ctx'), may hold values from -6 to 6
- norm_gains: bfloat16 [2, 2, 1536], P(None, None, ('dp', 'ctx')), may hold values from 0.5 to 1.5
- query_weight: bfloat16 [2, 1536, 1536], P(None, ('dp', 'ctx'), 'tensor'), may hold values from -0.15625 to 0.15625
- query_bias: bfloat16 [2, 12, 128], P(None, 'tensor', ('dp', 'ctx')), may hold values from -3 to 3
- kv_weight: bfloat16 [2, 1536, 512], P(None, ('dp', 'ctx')), may hold values from -0.15625 to 0.15625
- kv_bias: bfloat16 [2, 512], P(None, ('dp', 'ctx')), may hold values from -3 to 3
- out_weight: bfloat16 [2, 1536, 1536], P(None, 'tensor', ('dp', 'ctx')), may hold values from -1.25 to 1.25
- gate_up_weight: bfloat16 [2, 1536, 2, 8960], P(None, ('dp', 'ctx'), None, 'tensor'), may hold values from -0.15625 to 0.15625
- down_weight: bfloat16 [2, 8960, 1536], P(None, 'tensor', ('dp', 'ctx')), may hold values from -0.0625 to 0.0625
- norm_gains_first: float32 [2, 2, 1536], P(None, None, ('dp', 'ctx')), may hold values from -235.15102 to 235.15102
- query_weight_first: float32 [2, 1536, 1536], P(None, ('dp', 'ctx'), 'tensor'), may hold values from -71.55418 to 71.55418
- query_bias_first: float32 [2, 12, 128], P(None, 'tensor', ('dp', 'ctx')), may hold values from -71.55418 to 71.55418
- kv_weight_first: float32 [2, 1536, 512], P(None, ('dp', 'ctx')), may hold values from -175.27122 to 175.27122
- kv_bias_first: float32 [2, 512], P(None, ('dp', 'ctx')), may hold values from -175.27122 to 175.27122
- out_weight_first: float32 [2, 1536, 1536], P(None, 'tensor', ('dp', 'ctx')), may hold values from -39.191837 to 39.191837
- gate_up_weight_first: float32 [2, 1536, 2, 8960], P(None, ('dp', 'ctx'), None, 'tensor'), may hold values from -10.119288 to 10.119288
- down_weight_first: float32 [2, 8960, 1536], P(None, 'tensor', ('dp', 'ctx')), may hold values from -30.357866 to 30.357866
- norm_gains_second: float32 [2, 2, 1536], P(None, None, ('dp', 'ctx')), may hold values from 1105.92 to 17694.72
- query_weight_second: float32 [2, 1536, 1536], P(None, ('dp', 'ctx'), 'tensor'), may hold values from 102.4 to 1638.4
- query_bias_second: float32 [2, 12, 128], P(None, 'tensor', ('dp', 'ctx')), may hold values from 102.4 to 1638.4
- kv_weight_second: float32 [2, 1536, 512], P(None, ('dp', 'ctx')), may hold values from 614.4 to 9830.4
- kv_bias_second: float32 [2, 512], P(None, ('dp', 'ctx')), may hold values from 614.4 to 9830.4
- out_weight_second: float32 [2, 1536, 1536], P(None, 'tensor', ('dp', 'ctx')), may hold values from 30.72 to 491.52
- gate_up_weight_second: float32 [2, 1536, 2, 8960], P(None, ('dp', 'ctx'), None, 'tensor'), may hold values from 2.048 to 32.768
- down_weight_second: float32 [2, 8960, 1536], P(None, 'tensor', ('dp', 'ctx')), may hold values from 18.432 to 294.912
Outputs:
- block_out: bfloat16 [4, 1024, 1536], P('dp', 'ctx')
- input_grad: float32 [4, 1024, 1536], P('dp', 'ctx')
- norm_gains_grad: float32 [2, 2, 1536], P(None, None, ('dp', 'ctx'))
- query_weight_grad: float32 [2, 1536, 1536], P(None, ('dp', 'ctx'), 'tensor')
- query_bias_grad: float32 [2, 12, 128], P(None, 'tensor', ('dp', 'ctx'))
- kv_weight_grad: float32 [2, 1536, 512], P(None, ('dp', 'ctx'))
- kv_bias_grad: float32 [2, 512], P(None, ('dp', 'ctx'))
- out_weight_grad: float32 [2, 1536, 1536], P(None, 'tensor', ('dp', 'ctx'))
- gate_up_weight_grad: float32 [2, 1536, 2, 8960], P(None, ('dp', 'ctx'), None, 'tensor')
- down_weight_grad: float32 [2, 8960, 1536], P(None, 'tensor', ('dp', 'ctx'))
- norm_gains_first_new: float32 [2, 2, 1536], P(None, None, ('dp', 'ctx'))
- query_weight_first_new: float32 [2, 1536, 1536], P(None, ('dp', 'ctx'), 'tensor')
- query_bias_first_new: float32 [2, 12, 128], P(None, 'tensor', ('dp', 'ctx'))
- kv_weight_first_new: float32 [2, 1536, 512], P(None, ('dp', 'ctx'))
- kv_bias_first_new: float32 [2, 512], P(None, ('dp', 'ctx'))
- out_weight_first_new: float32 [2, 1536, 1536], P(None, 'tensor', ('dp', 'ctx'))
- gate_up_weight_first_new: float32 [2, 1536, 2, 8960], P(None, ('dp', 'ctx'), None, 'tensor')
- down_weight_first_new: float32 [2, 8960, 1536], P(None, 'tensor', ('dp', 'ctx'))
- norm_gains_second_new: float32 [2, 2, 1536], P(None, None, ('dp', 'ctx'))
- query_weight_second_new: float32 [2, 1536, 1536], P(None, ('dp', 'ctx'), 'tensor')
- query_bias_second_new: float32 [2, 12, 128], P(None, 'tensor', ('dp', 'ctx'))
- kv_weight_second_new: float32 [2, 1536, 512], P(None, ('dp', 'ctx'))
- kv_bias_second_new: float32 [2, 512], P(None, ('dp', 'ctx'))
- out_weight_second_new: float32 [2, 1536, 1536], P(None, 'tensor', ('dp', 'ctx'))
- gate_up_weight_second_new: float32 [2, 1536, 2, 8960], P(None, ('dp', 'ctx'), None, 'tensor')
- down_weight_second_new: float32 [2, 8960, 1536], P(None, 'tensor', ('dp', 'ctx'))
- norm_gains_new: float32 [2, 2, 1536], P(None, None, ('dp', 'ctx'))
- query_weight_new: float32 [2, 1536, 1536], P(None, ('dp', 'ctx'), 'tensor')
- query_bias_new: float32 [2, 12, 128], P(None, 'tensor', ('dp', 'ctx'))
- kv_weight_new: float32 [2, 1536, 512], P(None, ('dp', 'ctx'))
- kv_bias_new: float32 [2, 512], P(None, ('dp', 'ctx'))
- out_weight_new: float32 [2, 1536, 1536], P(None, 'tensor', ('dp', 'ctx'))
- gate_up_weight_new: float32 [2, 1536, 2, 8960], P(None, ('dp', 'ctx'), None, 'tensor')
- down_weight_new: float32 [2, 8960, 1536], P(None, 'tensor', ('dp', 'ctx'))
The draws below stay inside these ranges and needn't reach their ends.
Inputs may be any that keep to these rules, and one draw needn't show every extreme that they name: `segment_ids`: within each sequence the numbers never fall; each document holds 1 to 512 tokens, and one holds exactly that many.
All inputs are finite; a program needn't handle non-finite values.
Results may differ from the reference program's by a relative error of at most 0.03.
Values may be sent and summed in bfloat16 or wider, within the bound.
A program may use at most 320 MiB of HBM per device.

```python
import math
import jax
import jax.numpy as jnp
import numpy as np
from jax import lax

D = 1536
H = 12
KV = 2
HD = 128
FF = 8960
LAYERS = 2
DOCS = 6
SEQ_LEN = 1024
SEQS = 4


def shard_levels(stream_key, shape, cuts, smallest, largest):
    def one(dim, shards_of):
        steps = jax.random.uniform(jax.random.fold_in(jax.random.fold_in(stream_key, 6), dim), (shards_of,), jnp.float32, smallest / len(cuts), largest / len(cuts))
        return jnp.repeat(jnp.exp(steps), shape[dim] // shards_of).reshape((-1,) + (1,) * (len(shape) - dim - 1))

    level = one(*cuts[0])
    for cut in cuts[1:]:
        level = level * one(*cut)
    return level


def profile(number_of, total, bound, slope):
    weights = [(1 << 20) // math.isqrt(standing ** slope) + 1 for standing in range(2, number_of + 1)]
    surplus, counts = total - bound - (number_of - 1), [1] * (number_of - 1)
    while surplus > 0:
        candidates = [i for i in range(number_of - 1) if counts[i] < bound]
        mass, left = sum([weights[i] for i in candidates]), surplus
        for i in candidates:
            extra = min(bound - counts[i], max(1, left * weights[i] // mass), surplus)
            counts[i] = counts[i] + extra
            surplus = surplus - extra
    return np.array([bound] + counts)


def uneven(key, amount, total, bound, lean):
    if amount == 2:
        one = jax.random.randint(key, (), max(1, total - bound), min(bound, total - 1) + 1)
        return jnp.stack([one, total - one])
    lengths = jnp.asarray(profile(amount, total, bound, lean), jnp.int32)
    pairs = (amount - 1) // 2
    giver, taker = lengths[1:1 + 2 * pairs:2], lengths[2:2 + 2 * pairs:2]
    margin = jnp.minimum(giver - 1, bound - taker)
    shifted = jax.random.randint(jax.random.fold_in(key, 1), (pairs,), 0, 1 << 20) % (margin + 1)
    lengths = lengths.at[1:1 + 2 * pairs:2].set(giver - shifted).at[2:2 + 2 * pairs:2].set(taker + shifted)
    return lengths[jax.random.permutation(jax.random.fold_in(key, 2), amount)]


def noise(key, dims, spread, limit, cuts=(), held_as=jnp.bfloat16):
    array = jax.random.normal(key, dims, jnp.float32) * spread
    if len(cuts) > 0:
        array = shard_levels(key, dims, cuts, -0.22, 0.18) * array
    return jnp.clip(array, min=-limit, max=limit).astype(held_as)


def setup_inputs(seed: int = 0) -> dict:
    seeds = jax.random.split(jax.random.key(seed), 28)
    return {
        "hidden_in": noise(seeds[0], (SEQS, SEQ_LEN, D), 1.0, 6.0, ((0, 4), (1, 2))),
        "segment_ids": jax.vmap(lambda own: jnp.searchsorted(jnp.cumsum(uneven(own, DOCS, SEQ_LEN, SEQ_LEN // 2, 2)), jnp.arange(SEQ_LEN), side="right"))(jax.random.split(seeds[1], SEQS)).reshape((SEQS, SEQ_LEN)).astype(jnp.int32),
        "out_grad": noise(seeds[2], (SEQS, SEQ_LEN, D), 1.0, 6.0, ((0, 4), (1, 2))),
        "norm_gains": jnp.clip(1.0 + 0.1 * jax.random.normal(seeds[3], (LAYERS, 2, D), jnp.float32), 0.5, 1.5).astype(jnp.bfloat16),
        "query_weight": noise(seeds[4], (LAYERS, D, H * HD), D ** -0.5, 0.15625, ((1, 8), (2, 4))),
        "query_bias": noise(seeds[5], (LAYERS, H, HD), 0.5, 3.0, ((1, 4), (2, 8))),
        "kv_weight": noise(seeds[6], (LAYERS, D, 2 * KV * HD), D ** -0.5, 0.15625, ((1, 8),)),
        "kv_bias": noise(seeds[7], (LAYERS, 2 * KV * HD), 0.5, 3.0, ((1, 8),)),
        "out_weight": noise(seeds[8], (LAYERS, H * HD, D), (H * HD // 64) ** -0.5, 1.25, ((1, 4), (2, 8))),
        "gate_up_weight": noise(seeds[9], (LAYERS, D, 2, FF), D ** -0.5, 0.15625, ((1, 8), (3, 4))),
        "down_weight": noise(seeds[10], (LAYERS, FF, D), FF ** -0.5, 0.0625, ((1, 4), (2, 8))),
        "norm_gains_first": noise(seeds[11], (LAYERS, 2, D), ((54.0 * SEQS * SEQ_LEN) ** 0.5 / 12), 235.15102, ((2, 8),), jnp.float32),
        "query_weight_first": noise(seeds[12], (LAYERS, D, H * HD), ((5.0 * SEQS * SEQ_LEN) ** 0.5 / 12), 71.55418, ((1, 8), (2, 4)), jnp.float32),
        "query_bias_first": noise(seeds[13], (LAYERS, H, HD), ((5.0 * SEQS * SEQ_LEN) ** 0.5 / 12), 71.55418, ((1, 4), (2, 8)), jnp.float32),
        "kv_weight_first": noise(seeds[14], (LAYERS, D, 2 * KV * HD), ((30.0 * SEQS * SEQ_LEN) ** 0.5 / 12), 175.27122, ((1, 8),), jnp.float32),
        "kv_bias_first": noise(seeds[15], (LAYERS, 2 * KV * HD), ((30.0 * SEQS * SEQ_LEN) ** 0.5 / 12), 175.27122, ((1, 8),), jnp.float32),
        "out_weight_first": noise(seeds[16], (LAYERS, H * HD, D), ((1.5 * SEQS * SEQ_LEN) ** 0.5 / 12), 39.191837, ((1, 4), (2, 8)), jnp.float32),
        "gate_up_weight_first": noise(seeds[17], (LAYERS, D, 2, FF), ((0.1 * SEQS * SEQ_LEN) ** 0.5 / 12), 10.119288, ((1, 8), (3, 4)), jnp.float32),
        "down_weight_first": noise(seeds[18], (LAYERS, FF, D), ((0.9 * SEQS * SEQ_LEN) ** 0.5 / 12), 30.357866, ((1, 4), (2, 8)), jnp.float32),
        "norm_gains_second": jnp.clip(jnp.exp(math.log(17694.72) - 2.7725887 * jax.random.uniform(seeds[19], (LAYERS, 2, D), jnp.float32) ** shard_levels(seeds[19], (LAYERS, 2, D), ((2, 8),), -0.2, 0.2)), 1105.92, 17694.72),
        "query_weight_second": jnp.clip(jnp.exp(math.log(1638.4) - 2.7725887 * jax.random.uniform(seeds[20], (LAYERS, D, H * HD), jnp.float32) ** shard_levels(seeds[20], (LAYERS, D, H * HD), ((1, 8), (2, 4)), -0.2, 0.2)), 102.4, 1638.4),
        "query_bias_second": jnp.clip(jnp.exp(math.log(1638.4) - 2.7725887 * jax.random.uniform(seeds[21], (LAYERS, H, HD), jnp.float32) ** shard_levels(seeds[21], (LAYERS, H, HD), ((1, 4), (2, 8)), -0.2, 0.2)), 102.4, 1638.4),
        "kv_weight_second": jnp.clip(jnp.exp(math.log(9830.4) - 2.7725887 * jax.random.uniform(seeds[22], (LAYERS, D, 2 * KV * HD), jnp.float32) ** shard_levels(seeds[22], (LAYERS, D, 2 * KV * HD), ((1, 8),), -0.2, 0.2)), 614.4, 9830.4),
        "kv_bias_second": jnp.clip(jnp.exp(math.log(9830.4) - 2.7725887 * jax.random.uniform(seeds[23], (LAYERS, 2 * KV * HD), jnp.float32) ** shard_levels(seeds[23], (LAYERS, 2 * KV * HD), ((1, 8),), -0.2, 0.2)), 614.4, 9830.4),
        "out_weight_second": jnp.clip(jnp.exp(math.log(491.52) - 2.7725887 * jax.random.uniform(seeds[24], (LAYERS, H * HD, D), jnp.float32) ** shard_levels(seeds[24], (LAYERS, H * HD, D), ((1, 4), (2, 8)), -0.2, 0.2)), 30.72, 491.52),
        "gate_up_weight_second": jnp.clip(jnp.exp(math.log(32.768) - 2.7725887 * jax.random.uniform(seeds[25], (LAYERS, D, 2, FF), jnp.float32) ** shard_levels(seeds[25], (LAYERS, D, 2, FF), ((1, 8), (3, 4)), -0.2, 0.2)), 2.048, 32.768),
        "down_weight_second": jnp.clip(jnp.exp(math.log(294.912) - 2.7725887 * jax.random.uniform(seeds[26], (LAYERS, FF, D), jnp.float32) ** shard_levels(seeds[26], (LAYERS, FF, D), ((1, 4), (2, 8)), -0.2, 0.2)), 18.432, 294.912),
    }


@jax.custom_vjp
def low(v):
    return lax.optimization_barrier(v.astype(jnp.bfloat16)).astype(jnp.float32)

@jax.custom_vjp
def low_back(v):
    return v

def low_keep(v):
    return (low(v), None)

def low_pass(kept, grad):
    return (grad,)

def back_keep(v):
    return (v, None)

def back_low(kept, grad):
    return (low(grad),)
low.defvjp(low_keep, low_pass)
low_back.defvjp(back_keep, back_low)
NORM_EPS = 1e-06
ROPE_BASE = 1000000.0
MASK_FILL = -1e+30
beta_first = 0.9
beta_second = 0.95
adam_eps = 1e-08
decay_rate = 0.1
adam_step = 3.0

def linear(values, weight):
    return jnp.einsum('...d,de->...e', values, weight, precision=lax.Precision.HIGHEST)

def rms_norm(values, gain):
    norm_scale = lax.rsqrt(lax.optimization_barrier(jnp.mean(values * values, axis=-1, keepdims=True)) + NORM_EPS)
    return values * norm_scale * gain

def rotate(values, cosine, sine):
    half_width = values.shape[-1] // 2
    first_half = values[..., :half_width]
    second_half = values[..., half_width:]
    return jnp.concatenate([first_half * cosine - second_half * sine, second_half * cosine + first_half * sine], axis=-1)

def rope_tables(segments):
    length = segments.shape[-1]
    earlier = lax.optimization_barrier(jnp.sum((segments[:, None, :] < segments[:, :, None]).astype(jnp.int32), axis=-1))
    position = (jnp.arange(length, dtype=jnp.int32)[None, :] - earlier).astype(jnp.float32)
    frequency = ROPE_BASE ** (-jnp.arange(HD // 2, dtype=jnp.float32) / (HD // 2))
    angles = position[..., None] * frequency
    return (jnp.cos(angles), jnp.sin(angles))

def attend_one(sequence_item):
    queries, key_rows, value_rows, segment_row = sequence_item
    length = segment_row.shape[0]
    group_size = H // KV
    wide_keys = jnp.repeat(key_rows, group_size, axis=1)
    wide_values = jnp.repeat(value_rows, group_size, axis=1)
    scores = low_back(jnp.einsum('qhd,khd->hqk', queries, wide_keys, precision=lax.Precision.HIGHEST) * HD ** (-0.5))
    token_index = jnp.arange(length, dtype=jnp.int32)
    allowed = (segment_row[:, None] == segment_row[None, :]) & (token_index[None, :] <= token_index[:, None])
    scores = jnp.where(allowed[None], scores, MASK_FILL)
    row_max = lax.optimization_barrier(jnp.max(scores, axis=-1, keepdims=True))
    exp_scores = jnp.exp(scores - row_max)
    weights = exp_scores / lax.optimization_barrier(jnp.sum(exp_scores, axis=-1, keepdims=True))
    return jnp.einsum('hqk,khd->qhd', low(weights), wide_values, precision=lax.Precision.HIGHEST)

def forward_block(hidden, segments, cosine, sine, params):
    norm_gains, query_weight, query_bias, kv_weight, kv_bias, out_weight, gate_up_weight, down_weight = params
    seq_count, length = segments.shape
    cos_heads = cosine[:, :, None, :]
    sin_heads = sine[:, :, None, :]
    for layer_index in range(LAYERS):
        normed = low(rms_norm(hidden, norm_gains[layer_index, 0]))
        query_lin = low_back(linear(normed, query_weight[layer_index]) + query_bias[layer_index].reshape(H * HD))
        kv_lin = low_back(linear(normed, kv_weight[layer_index]) + kv_bias[layer_index])
        queries = low(rotate(query_lin.reshape(seq_count, length, H, HD), cos_heads, sin_heads))
        key_rows = low(rotate(kv_lin[..., :KV * HD].reshape(seq_count, length, KV, HD), cos_heads, sin_heads))
        value_rows = low(kv_lin[..., KV * HD:].reshape(seq_count, length, KV, HD))
        mixture = lax.map(jax.checkpoint(attend_one), (queries, key_rows, value_rows, segments))
        mixture = low(low_back(mixture.reshape(seq_count, length, H * HD)))
        middle = hidden + low_back(linear(mixture, out_weight[layer_index]))
        normed_two = low(rms_norm(middle, norm_gains[layer_index, 1]))
        gate_up = low_back(jnp.einsum('bsd,dgf->bsgf', normed_two, gate_up_weight[layer_index], precision=lax.Precision.HIGHEST))
        inner_low = low(jax.nn.silu(gate_up[:, :, 0]) * gate_up[:, :, 1])
        hidden = middle + low_back(linear(inner_low, down_weight[layer_index]))
    return hidden

def adam_update(weight, gradient, first_old, second_old, decayed, step_rate):
    first_new = beta_first * first_old + (1.0 - beta_first) * gradient
    second_new = beta_second * second_old + (1.0 - beta_second) * gradient * gradient
    mean_hat = first_new / (1.0 - beta_first ** adam_step)
    square_hat = second_new / (1.0 - beta_second ** adam_step)
    new_weight = weight - step_rate * (mean_hat / (jnp.sqrt(square_hat) + adam_eps) + decayed * decay_rate * weight)
    return (first_new, second_new, new_weight)

def reference(hidden_in, segment_ids, out_grad, norm_gains, query_weight, query_bias, kv_weight, kv_bias, out_weight, gate_up_weight, down_weight, norm_gains_first, query_weight_first, query_bias_first, kv_weight_first, kv_bias_first, out_weight_first, gate_up_weight_first, down_weight_first, norm_gains_second, query_weight_second, query_bias_second, kv_weight_second, kv_bias_second, out_weight_second, gate_up_weight_second, down_weight_second):
    params = (norm_gains.astype(jnp.float32), query_weight.astype(jnp.float32), query_bias.astype(jnp.float32), kv_weight.astype(jnp.float32), kv_bias.astype(jnp.float32), out_weight.astype(jnp.float32), gate_up_weight.astype(jnp.float32), down_weight.astype(jnp.float32))
    cosine, sine = rope_tables(segment_ids)

    def run_block(hidden, weights):
        return forward_block(hidden, segment_ids, cosine, sine, weights)
    result, pullback = jax.vjp(run_block, hidden_in.astype(jnp.float32), params)
    input_grad, grads = pullback(out_grad.astype(jnp.float32))
    firsts = (norm_gains_first, query_weight_first, query_bias_first, kv_weight_first, kv_bias_first, out_weight_first, gate_up_weight_first, down_weight_first)
    seconds = (norm_gains_second, query_weight_second, query_bias_second, kv_weight_second, kv_bias_second, out_weight_second, gate_up_weight_second, down_weight_second)
    decays = (0.0, 1.0, 0.0, 1.0, 0.0, 1.0, 1.0, 1.0)
    rates = (0.5, 0.02, 0.5, 0.02, 0.5, 0.1, 0.02, 0.02)
    moved = [adam_update(params[param_index], grads[param_index], firsts[param_index], seconds[param_index], decays[param_index], rates[param_index]) for param_index in range(8)]
    return (result.astype(jnp.bfloat16), input_grad, grads[0], grads[1], grads[2], grads[3], grads[4], grads[5], grads[6], grads[7], moved[0][0], moved[1][0], moved[2][0], moved[3][0], moved[4][0], moved[5][0], moved[6][0], moved[7][0], moved[0][1], moved[1][1], moved[2][1], moved[3][1], moved[4][1], moved[5][1], moved[6][1], moved[7][1], moved[0][2], moved[1][2], moved[2][2], moved[3][2], moved[4][2], moved[5][2], moved[6][2], moved[7][2])
```

```python
import functools

import jax
import jax.numpy as jnp
from jax import lax
from jax.experimental import pallas as pl
from jax.experimental.pallas import tpu as pltpu
from jax.sharding import PartitionSpec as P

H = 12
KV = 2
HD = 128
LAYERS = 2

NORM_EPS = 1e-06
ROPE_BASE = 1000000.0
MASK_FILL = -1e30
beta_first = 0.9
beta_second = 0.95
adam_eps = 1e-08
decay_rate = 0.1
adam_step = 3.0

MESH = pl.DeviceIdType.MESH
ROW_TILE = 16
Z_CHUNKS = 8


class Place:
    def __init__(self, sizes):
        self.dps, self.ctxs, self.tensors = sizes
        self.xs = self.dps // 2
        self.dp = lax.axis_index("dp")
        self.ctx = lax.axis_index("ctx")
        self.tensor = lax.axis_index("tensor")
        self.x = self.dp // 2
        self.core = self.dp % 2

    def x_at(self, step):
        return lax.rem(self.x + step, self.xs)

    def ctx_at(self, step):
        return lax.rem(self.ctx + step, self.ctxs)

    def shard(self, x, core, ctx):
        return (x * 2 + core) * self.ctxs + ctx

    def to_x(self, x):
        return {"dp": x * 2 + self.core}

    def to_ctx(self, ctx):
        return {"ctx": ctx}

    def to_core(self):
        return {"dp": self.x * 2 + 1 - self.core}

    def to_tensor(self, tensor):
        return {"tensor": tensor}


class Sems:
    def __init__(self, send, recv):
        self.send, self.recv, self.used = send, recv, 0

    def take(self, count=1):
        first = self.used
        self.used += count
        return first

    def remote(self, src, dst, device, slot=None):
        slot = self.take() if slot is None else slot
        return pltpu.make_async_remote_copy(
            src_ref=src,
            dst_ref=dst,
            send_sem=self.send.at[slot],
            recv_sem=self.recv.at[slot],
            device_id=device,
            device_id_type=MESH,
        )

    def local(self, src, dst):
        return pltpu.make_async_copy(src, dst, self.send.at[self.take()])


def half_rows(rows):
    return min(rows, (rows // 2 + ROW_TILE - 1) // ROW_TILE * ROW_TILE)


def gather_steps(place, sems, shard, whole):
    rows = shard.shape[0]
    cut = half_rows(rows)
    spans = [(0, cut), (cut, rows - cut)]
    xs, ctxs = range(1, place.xs), range(1, place.ctxs)
    me = place.shard(place.x, place.core, place.ctx)
    sent, kept = [], {}

    def part(index, span):
        return whole.at[index, pl.ds(span[0], span[1])]

    def first():
        for step in xs:
            kept["x", step] = sems.remote(shard, whole.at[me], place.to_x(place.x_at(step)))
        for step in ctxs:
            kept["ctx", step] = sems.remote(shard, whole.at[me], place.to_ctx(place.ctx_at(step)))
        kept["core"] = sems.remote(shard, whole.at[me], place.to_core())
        kept["own"] = sems.local(shard, whole.at[me])
        for copy in kept.values():
            copy.start()

    def forward(index, span, device):
        copy = sems.remote(part(index, span), part(index, span), device)
        copy.start()
        sent.append(copy)
        return copy

    def second():
        for step in xs:
            kept["x", step].wait_recv()
            index = place.shard(place.x_at(place.xs - step), place.core, place.ctx)
            for other in ctxs:
                kept["far", step, other, 0] = forward(index, spans[0], place.to_ctx(place.ctx_at(other)))
            forward(index, (0, rows), place.to_core())
        for step in ctxs:
            kept["ctx", step].wait_recv()
            index = place.shard(place.x, place.core, place.ctx_at(place.ctxs - step))
            if spans[1][1] > 0:
                for other in xs:
                    kept["far", other, step, 1] = forward(
                        index, spans[1], place.to_x(place.x_at(other))
                    )
            forward(index, (0, rows), place.to_core())

    def third():
        for step in xs:
            for other in ctxs:
                index = place.shard(
                    place.x_at(place.xs - step), place.core, place.ctx_at(place.ctxs - other)
                )
                kept["far", step, other, 0].wait_recv()
                if spans[1][1] > 0:
                    kept["far", step, other, 1].wait_recv()
                forward(index, (0, rows), place.to_core())

    def last():
        for name, copy in kept.items():
            if name == "own":
                copy.wait()
            elif name[0] in ("x", "ctx"):
                copy.wait_send()
        kept["core"].wait()
        far = [copy for name, copy in kept.items() if name[0] == "far"]
        for copy in sent:
            if any(copy is other for other in far):
                copy.wait_send()
            else:
                copy.wait()

    return [first, second, third, last]


def gather_sems(sizes):
    xs, ctxs = sizes[0] // 2 - 1, sizes[1] - 1
    return 2 + 2 * (xs + ctxs) + 3 * xs * ctxs


def add_rows(rows, body):
    @pl.loop(0, rows // ROW_TILE)
    def _(block):
        body(pl.ds(pl.multiple_of(block * ROW_TILE, ROW_TILE), ROW_TILE))


def scatter_buffers(sizes, shape, dtype):
    n, rows, cols = shape
    xs, ctxs = sizes[0] // 2, sizes[1]
    cut = half_rows(rows)
    far = max(1, (xs - 1) * (ctxs - 1))
    return [
        pltpu.VMEM((xs, ctxs, rows, cols), dtype),
        pltpu.VMEM((xs, ctxs, rows, cols), dtype),
        pltpu.VMEM((far, cut, cols), dtype),
        pltpu.VMEM((far, max(ROW_TILE, rows - cut), cols), dtype),
        pltpu.VMEM((max(1, xs - 1 + ctxs - 1), rows, cols), dtype),
    ]


def scatter_sems(sizes):
    xs, ctxs = sizes[0] // 2 - 1, sizes[1] - 1
    return 2 * (xs + 1) + (xs + ctxs) + 2 * xs * ctxs


def scatter_steps(place, sems, whole, out, mine, other, far_x, far_ctx, near):
    rows = out.shape[0]
    cut = half_rows(rows)
    xs, ctxs = range(1, place.xs), range(1, place.ctxs)
    ahead = lambda step, turn: (step - 1) * len(ctxs) + turn - 1
    loads, swaps, sent = {}, {}, []
    far, close = {}, {}
    wide = lambda ref, *at: ref[at].astype(jnp.float32)

    def first():
        for step in list(xs) + [0]:
            to = place.x_at(step)
            at = place.shard(to, 1 - place.core, 0)
            swaps[step] = sems.remote(
                whole.at[pl.ds(at, place.ctxs)], other.at[step], place.to_core()
            )
            swaps[step].start()
            at = place.shard(to, place.core, 0)
            loads[step] = sems.local(whole.at[pl.ds(at, place.ctxs)], mine.at[step])
            loads[step].start()

    def second():
        for step in xs:
            loads[step].wait()
            swaps[step].wait_recv()
            for turn in ctxs:
                ctx = place.ctx_at(turn)

                def add(span):
                    total = wide(mine, step, ctx, span) + wide(other, step, ctx, span)
                    mine[step, ctx, span] = total.astype(mine.dtype)

                add_rows(rows, add)
                slot = ahead(step, turn)
                far[step, turn, 0] = sems.remote(
                    mine.at[step, ctx, pl.ds(0, cut)], far_x.at[slot], place.to_ctx(ctx)
                )
                far[step, turn, 0].start()
                if rows > cut:
                    far[step, turn, 1] = sems.remote(
                        mine.at[step, ctx, pl.ds(cut, rows - cut)],
                        far_ctx.at[slot],
                        place.to_x(place.x_at(step)),
                    )
                    far[step, turn, 1].start()
        loads[0].wait()
        swaps[0].wait_recv()

    def third():
        for turn in ctxs:
            ctx = place.ctx_at(turn)
            if rows > cut:
                for step in xs:
                    far[step, turn, 1].wait_recv()

            def add_near(span):
                total = wide(mine, 0, ctx, span) + wide(other, 0, ctx, span)
                mine[0, ctx, span] = total.astype(mine.dtype)

            def add_far(block):
                span = pl.ds(pl.multiple_of(cut + block * ROW_TILE, ROW_TILE), ROW_TILE)
                here = pl.ds(pl.multiple_of(block * ROW_TILE, ROW_TILE), ROW_TILE)
                total = wide(mine, 0, ctx, span) + wide(other, 0, ctx, span)
                for step in xs:
                    total = total + wide(far_ctx, ahead(step, turn), here)
                mine[0, ctx, span] = total.astype(mine.dtype)

            add_rows(cut, add_near)
            if rows > cut:
                pl.loop(0, (rows - cut) // ROW_TILE)(add_far)
            slot = len(xs) + turn - 1
            close["ctx", turn] = sems.remote(mine.at[0, ctx], near.at[slot], place.to_ctx(ctx))
            close["ctx", turn].start()
        for step in xs:
            for turn in ctxs:
                far[step, turn, 0].wait_recv()

            def add_cut(span):
                total = wide(mine, step, place.ctx, span) + wide(other, step, place.ctx, span)
                for turn in ctxs:
                    total = total + wide(far_x, ahead(step, turn), span)
                mine[step, place.ctx, span] = total.astype(mine.dtype)

            def add_rest(block):
                span = pl.ds(pl.multiple_of(cut + block * ROW_TILE, ROW_TILE), ROW_TILE)
                total = wide(mine, step, place.ctx, span) + wide(other, step, place.ctx, span)
                mine[step, place.ctx, span] = total.astype(mine.dtype)

            add_rows(cut, add_cut)
            if rows > cut:
                pl.loop(0, (rows - cut) // ROW_TILE)(add_rest)
            close["x", step] = sems.remote(
                mine.at[step, place.ctx], near.at[step - 1], place.to_x(place.x_at(step))
            )
            close["x", step].start()

    def last():
        for copy in close.values():
            copy.wait_recv()

        def add_own(span):
            total = wide(mine, 0, place.ctx, span) + wide(other, 0, place.ctx, span)
            for slot in range(len(xs) + len(ctxs)):
                total = total + wide(near, slot, span)
            out[span] = total.astype(out.dtype)

        add_rows(rows, add_own)
        for copy in (*far.values(), *close.values(), *swaps.values()):
            copy.wait_send()

    return [first, second, third, last]


def line_steps(place, sems, part, out, recv, acc):
    rows = part.shape[0]
    size = rows // (2 * Z_CHUNKS)
    line = place.tensors
    me = place.tensor
    left = me < (line + 1) // 2
    hops = jnp.where(left, me, line - 1 - me)
    ahead = jnp.where(left, 1, -1)
    near = jnp.where(left, 0, 1)
    far = 1 - near
    onward = place.to_tensor(lax.clamp(0, me + ahead, line - 1))
    back = place.to_tensor(lax.clamp(0, me - ahead, line - 1))
    base = sems.take(4 * Z_CHUNKS)
    inner = hops > 0

    def span(flow, chunk):
        return pl.ds(pl.multiple_of((flow * Z_CHUNKS + chunk) * size, size), size)

    def summing(flow, chunk, src, device):
        return sems.remote(
            src.at[span(flow, chunk)],
            recv.at[span(flow, chunk)],
            device,
            base + flow * Z_CHUNKS + chunk,
        )

    def sharing(flow, chunk, device):
        return sems.remote(
            out.at[span(flow, chunk)],
            out.at[span(flow, chunk)],
            device,
            base + (2 + flow) * Z_CHUNKS + chunk,
        )

    def add(flow, chunk, into):
        at = span(flow, chunk)
        total = part[at].astype(jnp.float32) + recv[at].astype(jnp.float32)
        into[at] = total.astype(into.dtype)

    def begin():
        @pl.when(hops == 0)
        def _():
            for chunk in range(Z_CHUNKS):
                summing(near, chunk, part, onward).start()

    def step(turn):
        def run():
            chunk = turn
            if chunk < Z_CHUNKS:

                @pl.when(inner)
                def _():
                    summing(near, chunk, part, onward).wait_recv()
                    add(near, chunk, acc)
                    summing(near, chunk, acc, onward).start()

                summing(far, chunk, acc, back).wait_recv()

                @pl.when(inner)
                def _():
                    add(far, chunk, acc)
                    summing(far, chunk, acc, back).start()

                @pl.when(hops == 0)
                def _():
                    add(far, chunk, out)
                    sharing(far, chunk, onward).start()

            chunk = turn - 2
            if 0 <= chunk < Z_CHUNKS:

                @pl.when(inner)
                def _():
                    sharing(far, chunk, onward).wait_recv()
                    sharing(far, chunk, onward).start()

            chunk = turn - 3
            if 0 <= chunk < Z_CHUNKS:
                sharing(near, chunk, back).wait_recv()

                @pl.when(inner)
                def _():
                    sharing(near, chunk, back).start()

        return run

    def end():
        for chunk in range(Z_CHUNKS):
            summing(near, chunk, acc, onward).wait_send()
            sharing(far, chunk, onward).wait_send()

            @pl.when(inner)
            def _():
                summing(far, chunk, acc, back).wait_send()
                sharing(near, chunk, back).wait_send()

    return [begin] + [step(turn) for turn in range(Z_CHUNKS + 3)] + [end]


def transfer_kernel(sizes, counts, plan, *refs):
    z_count, g_count, s_count, p_count, w_count = counts
    inputs = sum(counts)
    ins, outs, rest = refs[:inputs], refs[inputs : 2 * inputs], list(refs[2 * inputs :])
    place = Place(sizes)
    sems = Sems(rest.pop(), rest.pop())

    barrier = pltpu.get_barrier_semaphore()
    partners = []
    arrived = 0
    if g_count or s_count:
        partners.append(place.to_core())
        partners += [place.to_x(place.x_at(step)) for step in range(1, place.xs)]
    if g_count or s_count or p_count or w_count:
        partners += [place.to_ctx(place.ctx_at(step)) for step in range(1, place.ctxs)]
    for partner in partners:
        pl.semaphore_signal(barrier, inc=1, device_id=partner, device_id_type=MESH)
    arrived = len(partners)
    if z_count:
        above = place.tensor < place.tensors - 1
        below = place.tensor > 0

        @pl.when(above)
        def _():
            pl.semaphore_signal(
                barrier, inc=1, device_id=place.to_tensor(place.tensor + 1), device_id_type=MESH
            )

        @pl.when(below)
        def _():
            pl.semaphore_signal(
                barrier, inc=1, device_id=place.to_tensor(place.tensor - 1), device_id_type=MESH
            )

        arrived = arrived + above.astype(jnp.int32) + below.astype(jnp.int32)
    pl.semaphore_wait(barrier, arrived)

    ins, outs = list(ins), list(outs)
    lines, planes, ends = [], [], []
    for _ in range(z_count):
        lines.append(line_steps(place, sems, ins.pop(0), outs.pop(0), rest.pop(0), rest.pop(0)))
    for _ in range(g_count):
        planes.append(gather_steps(place, sems, ins.pop(0), outs.pop(0)))
    for _ in range(s_count):
        buffers = [rest.pop(0) for _ in range(5)]
        planes.append(scatter_steps(place, sems, ins.pop(0), outs.pop(0), *buffers))
    small = []
    for index in range(p_count + w_count):
        src, dst = ins.pop(0), outs.pop(0)
        mine = place.ctx
        for step in range(1, place.ctxs):
            to = place.ctx_at(step)
            block = src if index < p_count else src.at[to]
            small.append(sems.remote(block, dst.at[mine], place.to_ctx(to)))
        block = src if index < p_count else src.at[mine]
        small.append(sems.local(block, dst.at[mine]))
    for copy in small:
        copy.start()
    stages = [[plane[stage] for plane in planes] for stage in range(4)]
    for run in stages[0]:
        run()
    turns = max([len(line) for line in lines], default=0)
    for turn in range(turns + 1):
        for stage in (1, 2):
            if (plan[stage - 1] == turn) or (turn == turns and plan[stage - 1] > turns):
                for run in stages[stage]:
                    run()
        for line in lines:
            if turn < len(line):
                line[turn]()
    for run in stages[3]:
        run()
    for copy in small:
        copy.wait()


def transfer(sizes, number, z_sums=(), gathers=(), scatters=(), pieces=(), swaps=(), plan=(99, 99)):
    n = sizes[0] * sizes[1]
    any_space = pl.BlockSpec(memory_space=pl.ANY)
    in_vmem = pl.BlockSpec(memory_space=pltpu.VMEM)
    args = (*z_sums, *gathers, *scatters, *pieces, *swaps)
    in_specs = [in_vmem] * len(z_sums) + [any_space] * (len(args) - len(z_sums))
    out_specs = (
        [in_vmem] * len(z_sums)
        + [any_space] * len(gathers)
        + [in_vmem] * len(scatters)
        + [any_space] * (len(pieces) + len(swaps))
    )
    out_shape = (
        [jax.ShapeDtypeStruct(a.shape, a.dtype) for a in z_sums]
        + [jax.ShapeDtypeStruct((n, *a.shape), a.dtype) for a in gathers]
        + [jax.ShapeDtypeStruct(a.shape[1:], jnp.float32) for a in scatters]
        + [jax.ShapeDtypeStruct((sizes[1], *a.shape), a.dtype) for a in pieces]
        + [jax.ShapeDtypeStruct(a.shape, a.dtype) for a in swaps]
    )
    scratch = []
    for a in z_sums:
        scratch += [pltpu.VMEM(a.shape, a.dtype)] * 2
    for a in scatters:
        scratch += scatter_buffers(sizes, a.shape, a.dtype)
    count = (
        4 * Z_CHUNKS * len(z_sums)
        + gather_sems(sizes) * len(gathers)
        + scatter_sems(sizes) * len(scatters)
        + sizes[1] * (len(pieces) + len(swaps))
    )
    scratch += [pltpu.SemaphoreType.DMA((count,)), pltpu.SemaphoreType.DMA((count,))]
    counts = (len(z_sums), len(gathers), len(scatters), len(pieces), len(swaps))
    return pl.pallas_call(
        functools.partial(transfer_kernel, sizes, counts, plan),
        out_shape=out_shape,
        in_specs=in_specs,
        out_specs=out_specs,
        scratch_shapes=scratch,
        compiler_params=pltpu.CompilerParams(
            collective_id=number, has_side_effects=True, vmem_limit_bytes=56 << 20
        ),
        name="transfer%d" % number,
    )(*args)


def rotate(values, cosine, sine):
    half_width = values.shape[-1] // 2
    first_half = values[..., :half_width]
    second_half = values[..., half_width:]
    return jnp.concatenate(
        [first_half * cosine - second_half * sine, second_half * cosine + first_half * sine],
        axis=-1,
    )


def rotate_back(grad_rows, cosine, sine):
    return rotate(grad_rows, cosine, -sine)


def norm_back(values, norm_scale, gain, grad_rows):
    weighted = grad_rows * gain
    inner_mean = jnp.mean(weighted * values, axis=-1, keepdims=True)
    grad_values = (
        norm_scale * weighted - values * (norm_scale * norm_scale * norm_scale) * inner_mean
    )
    return (grad_values, jnp.sum(grad_rows * values * norm_scale, axis=0))


def adam_update(weight, gradient, first_old, second_old, decayed, step_rate):
    first_new = beta_first * first_old + (1.0 - beta_first) * gradient
    second_new = beta_second * second_old + (1.0 - beta_second) * gradient * gradient
    mean_hat = first_new / (1.0 - beta_first**adam_step)
    square_hat = second_new / (1.0 - beta_second**adam_step)
    new_weight = weight - step_rate * (
        mean_hat / (jnp.sqrt(square_hat) + adam_eps) + decayed * decay_rate * weight
    )
    return (first_new, second_new, new_weight)


def dot(lhs, rhs, over):
    return lax.dot_general(lhs, rhs, ((over[0:1], over[1:2]), ((), ())), preferred_element_type=jnp.float32)


def masked_scores(queries, all_keys, allowed, score_scale):
    scores = (
        jnp.einsum("sqhd,skd->shqk", queries, all_keys, preferred_element_type=jnp.float32)
        * score_scale
    )
    return jnp.where(allowed, scores, MASK_FILL)


def local(
    sizes,
    hidden_in,
    segment_ids,
    out_grad,
    norm_gains,
    query_weight,
    query_bias,
    kv_weight,
    kv_bias,
    out_weight,
    gate_up_weight,
    down_weight,
    *moments,
):
    low = jnp.bfloat16
    wide = jnp.float32
    dps, ctxs, tensors = sizes
    n = dps * ctxs
    seq_count, local_len, model_width = hidden_in.shape
    seq_length = segment_ids.shape[1]
    row_count = seq_count * local_len
    shard_rows = query_weight.shape[1]
    heads_here = query_weight.shape[2] // HD
    q_width = heads_here * HD
    hidden_units = down_weight.shape[1]
    local_start = lax.axis_index("ctx") * local_len
    kv_head = lax.axis_index("tensor") * heads_here // (H // KV)
    score_scale = HD ** (-0.5)
    numbers = iter(range(1, 100))

    def move(**what):
        return transfer(sizes, next(numbers), **what)

    attention_shards = [
        jnp.concatenate(
            [
                query_weight[layer],
                lax.dynamic_slice_in_dim(kv_weight[layer], kv_head * HD, HD, 1),
                lax.dynamic_slice_in_dim(kv_weight[layer], (KV + kv_head) * HD, HD, 1),
                out_weight[layer].T,
            ],
            axis=1,
        )
        for layer in range(LAYERS)
    ]
    gate_shards = [gate_up_weight[layer, :, 0] for layer in range(LAYERS)]
    up_shards = [gate_up_weight[layer, :, 1] for layer in range(LAYERS)]
    down_shards = [down_weight[layer].T for layer in range(LAYERS)]

    bias_part = kv_bias.shape[1]
    head_part = query_bias.shape[2]
    small_width = -(-max(shard_rows, bias_part) // 128) * 128
    pad = lambda a: jnp.pad(a, ((0, 0), (0, small_width - a.shape[1])))
    small_rows = LAYERS * (2 + heads_here + 1)
    small_shard = jnp.pad(
        jnp.concatenate(
            [
                pad(norm_gains.reshape(LAYERS * 2, shard_rows)),
                pad(query_bias.reshape(LAYERS * heads_here, head_part)),
                pad(kv_bias),
            ],
            axis=0,
        ),
        ((0, -small_rows % ROW_TILE), (0, 0)),
    )

    small, attention_weights = move(gathers=[small_shard, attention_shards[0]])
    at = LAYERS * 2
    gains = (
        small[:, :at, :shard_rows]
        .transpose(1, 0, 2)
        .reshape(LAYERS, 2, model_width)
        .astype(wide)
    )
    q_biases = (
        small[:, at : at + LAYERS * heads_here, :head_part]
        .transpose(1, 0, 2)
        .reshape(LAYERS, q_width)
        .astype(wide)
    )
    at += LAYERS * heads_here
    kv_biases = small[:, at : at + LAYERS, :bias_part].transpose(1, 0, 2).reshape(LAYERS, 2 * KV, HD)
    kv_biases = jnp.concatenate(
        [
            lax.dynamic_slice_in_dim(kv_biases, kv_head, 1, 1)[:, 0],
            lax.dynamic_slice_in_dim(kv_biases, KV + kv_head, 1, 1)[:, 0],
        ],
        axis=1,
    ).astype(wide)

    own_segments = lax.dynamic_slice_in_dim(segment_ids, local_start, local_len, 1)
    earlier = jnp.sum(
        (segment_ids[:, None, :] < own_segments[:, :, None]).astype(jnp.int32), axis=-1
    )
    token_index = local_start + jnp.arange(local_len, dtype=jnp.int32)
    position = (token_index[None, :] - earlier).astype(wide)
    frequency = ROPE_BASE ** (-jnp.arange(HD // 2, dtype=wide) / (HD // 2))
    angles = position[..., None] * frequency
    cosine = jnp.cos(angles).reshape(row_count, 1, HD // 2)
    sine = jnp.sin(angles).reshape(row_count, 1, HD // 2)
    key_index = jnp.arange(seq_length, dtype=jnp.int32)
    allowed = (own_segments[:, :, None] == segment_ids[:, None, :]) & (
        key_index[None, None, :] <= token_index[None, :, None]
    )
    allowed = allowed[:, None]

    hidden = hidden_in.astype(wide).reshape(row_count, model_width)
    stored = []
    gate_weights = up_weights = down_weights = None
    for layer in range(LAYERS):
        w_attention = attention_weights.reshape(model_width, q_width + 2 * HD + q_width)
        w_in = w_attention[:, : q_width + 2 * HD]
        w_out = w_attention[:, q_width + 2 * HD :]
        scale_one = lax.rsqrt(jnp.mean(hidden * hidden, axis=-1, keepdims=True) + NORM_EPS)
        normed = (hidden * scale_one * gains[layer, 0]).astype(low)
        lin = dot(normed, w_in, (1, 0)) + jnp.concatenate([q_biases[layer], kv_biases[layer]])
        lin_heads = lin[:, : q_width + HD].reshape(row_count, heads_here + 1, HD)
        turned = rotate(lin_heads, cosine, sine).astype(low)
        queries = turned[:, :heads_here].reshape(seq_count, local_len, heads_here, HD)
        pair = jnp.concatenate([turned[:, heads_here], lin[:, q_width + HD :].astype(low)], axis=1)
        if layer == 0:
            down_weights, pairs = move(gathers=[down_shards[0]], pieces=[pair])
        else:
            (pairs,) = move(pieces=[pair])
        pairs = (
            pairs.reshape(ctxs, seq_count, local_len, 2 * HD)
            .transpose(1, 0, 2, 3)
            .reshape(seq_count, seq_length, 2 * HD)
        )
        all_keys, all_values = pairs[..., :HD], pairs[..., HD:]
        scores = masked_scores(queries, all_keys, allowed, score_scale)
        row_max = jnp.max(scores, axis=-1, keepdims=True)
        exp_scores = jnp.exp(scores - row_max)
        row_total = jnp.sum(exp_scores, axis=-1, keepdims=True)
        weights = exp_scores / row_total
        log_total = row_max + jnp.log(row_total)
        mixture = jnp.einsum(
            "shqk,skd->sqhd", weights.astype(low), all_values, preferred_element_type=wide
        )
        mixed_low = mixture.reshape(row_count, q_width).astype(low)
        part = dot(mixed_low, w_out, (1, 1)).astype(low)
        total, gate_weights, up_weights = move(
            z_sums=[part], gathers=[gate_shards[layer], up_shards[layer]]
        )
        w_gate = gate_weights.reshape(model_width, hidden_units)
        w_up = up_weights.reshape(model_width, hidden_units)
        w_down = down_weights.reshape(model_width, hidden_units)
        middle = hidden + total.astype(wide)
        scale_two = lax.rsqrt(jnp.mean(middle * middle, axis=-1, keepdims=True) + NORM_EPS)
        normed_two = (middle * scale_two * gains[layer, 1]).astype(low)
        gate = dot(normed_two, w_gate, (1, 0))
        up = dot(normed_two, w_up, (1, 0))
        inner_low = (jax.nn.silu(gate) * up).astype(low)
        stored.append(
            (
                hidden,
                scale_one,
                normed,
                queries,
                all_keys,
                all_values,
                log_total,
                mixed_low,
                middle,
                scale_two,
                normed_two,
                gate,
                up,
                inner_low,
                w_in,
                w_out,
                w_gate,
                w_up,
                w_down,
            )
        )
        part = dot(inner_low, w_down, (1, 1)).astype(low)
        if layer + 1 < LAYERS:
            total, attention_weights, down_weights = move(
                z_sums=[part], gathers=[attention_shards[layer + 1], down_shards[layer + 1]]
            )
            hidden = middle + total.astype(wide)
        else:
            last_part = part

    def split(gradient):
        return gradient.astype(low).reshape(n, shard_rows, gradient.shape[1])

    def by_owner(row, width):
        return jnp.pad(row.reshape(n, 1, width), ((0, 0), (0, 0), (0, small_width - width)))

    grad_hidden = out_grad.astype(wide).reshape(row_count, model_width)
    done = [{} for _ in range(LAYERS)]
    small_grads = [None] * LAYERS
    waiting = []
    for layer in reversed(range(LAYERS)):
        (
            layer_input,
            scale_one,
            normed,
            queries,
            all_keys,
            all_values,
            log_total,
            mixed_low,
            middle,
            scale_two,
            normed_two,
            gate,
            up,
            inner_low,
            w_in,
            w_out,
            w_gate,
            w_up,
            w_down,
        ) = stored[layer]
        grad_low = grad_hidden.astype(low)
        grad_down_w = split(dot(grad_low, inner_low, (0, 0)))
        grad_inner = dot(grad_low, w_down, (1, 0))
        sigmoid_gate = jax.nn.sigmoid(gate)
        grad_gate = (
            grad_inner * up * sigmoid_gate * (1.0 + gate * (1.0 - sigmoid_gate))
        ).astype(low)
        grad_upper = (grad_inner * gate * sigmoid_gate).astype(low)
        grad_gate_w = split(dot(normed_two, grad_gate, (0, 0)))
        grad_up_w = split(dot(normed_two, grad_upper, (0, 0)))
        part = (dot(grad_gate, w_gate, (1, 1)) + dot(grad_upper, w_up, (1, 1))).astype(low)
        total, done[layer]["down"], done[layer]["gate"], *rest = move(
            z_sums=[part], scatters=[grad_down_w, grad_gate_w] + [a for _, _, a in waiting]
        )
        for (name, owner, _), result in zip(waiting, rest):
            done[owner][name] = result
        back_two, grad_gain_two = norm_back(middle, scale_two, gains[layer, 1], total.astype(wide))
        grad_middle = grad_hidden + back_two
        grad_mid_low = grad_middle.astype(low)
        grad_out_w = split(dot(grad_mid_low, mixed_low, (0, 0)))
        grad_mixed = (
            dot(grad_mid_low, w_out, (1, 0))
            .astype(low)
            .reshape(seq_count, local_len, heads_here, HD)
        )
        scores = masked_scores(queries, all_keys, allowed, score_scale)
        probabilities = jnp.exp(scores - log_total)
        grad_probs = jnp.einsum(
            "sqhd,skd->shqk", grad_mixed, all_values, preferred_element_type=wide
        )
        row_delta = jnp.sum(probabilities * grad_probs, axis=-1, keepdims=True)
        grad_scores = (probabilities * (grad_probs - row_delta)).astype(low)
        grad_queries = (
            jnp.einsum("shqk,skd->sqhd", grad_scores, all_keys, preferred_element_type=wide)
            * score_scale
        )
        grad_keys = (
            jnp.einsum("shqk,sqhd->skd", grad_scores, queries, preferred_element_type=wide)
            * score_scale
        )
        grad_values = jnp.einsum(
            "shqk,sqhd->skd", probabilities.astype(low), grad_mixed, preferred_element_type=wide
        )
        grad_pair = jnp.concatenate([grad_keys, grad_values], axis=2).astype(low)
        grad_pair = (
            grad_pair.reshape(seq_count, ctxs, local_len, 2 * HD)
            .transpose(1, 0, 2, 3)
            .reshape(ctxs, row_count, 2 * HD)
        )
        (grad_pair,) = move(swaps=[grad_pair])
        grad_pair = jnp.sum(grad_pair.astype(wide), axis=0)
        grad_heads = jnp.concatenate(
            [grad_queries.reshape(row_count, heads_here, HD), grad_pair[:, None, :HD]], axis=1
        )
        grad_lin = jnp.concatenate(
            [
                rotate_back(grad_heads, cosine, sine).reshape(row_count, q_width + HD),
                grad_pair[:, HD:],
            ],
            axis=1,
        ).astype(low)
        grad_in_w = split(dot(normed, grad_lin, (0, 0)))
        grad_bias = jnp.sum(grad_lin.astype(wide), axis=0)
        part = dot(grad_lin, w_in, (1, 1)).astype(low)
        zeros = jnp.zeros((2 * KV, HD), wide)
        kv_bias_grad = lax.dynamic_update_slice_in_dim(
            zeros, grad_bias[q_width : q_width + HD][None], kv_head, 0
        )
        kv_bias_grad = lax.dynamic_update_slice_in_dim(
            kv_bias_grad, grad_bias[q_width + HD :][None], KV + kv_head, 0
        )
        head_rows = grad_bias[:q_width].reshape(heads_here, HD)
        small_grads[layer] = [grad_gain_two, head_rows, kv_bias_grad.reshape(-1)]
        if layer > 0:
            total, done[layer]["up"] = move(z_sums=[part], scatters=[grad_up_w])
            waiting = [("out", layer, grad_out_w), ("in", layer, grad_in_w)]
        else:
            total, block_sum, done[layer]["up"], done[layer]["in"], done[layer]["out"] = move(
                z_sums=[part, last_part], scatters=[grad_up_w, grad_in_w, grad_out_w]
            )
        back_one, grad_gain_one = norm_back(
            layer_input, scale_one, gains[layer, 0], total.astype(wide)
        )
        small_grads[layer].insert(0, grad_gain_one)
        grad_hidden = grad_middle + back_one

    block_out = (stored[-1][8] + block_sum.astype(wide)).astype(low)
    block_out = block_out.reshape(seq_count, local_len, model_width)
    input_grad = grad_hidden.reshape(seq_count, local_len, model_width)

    small_part = []
    for layer in range(LAYERS):
        gain_one, gain_two, head_rows, kv_row = small_grads[layer]
        small_part += [by_owner(gain_one, shard_rows), by_owner(gain_two, shard_rows)]
        small_part += [by_owner(head_rows[head], head_part) for head in range(heads_here)]
        small_part.append(by_owner(kv_row, bias_part))
    small_part = jnp.pad(
        jnp.concatenate(small_part, axis=1), ((0, 0), (0, -small_rows % ROW_TILE), (0, 0))
    ).astype(low)
    (small_sum,) = move(scatters=[small_part])
    small_sum = small_sum[:small_rows].reshape(LAYERS, 2 + heads_here + 1, small_width)
    gains_grad = small_sum[:, :2, :shard_rows]
    query_bias_grad = small_sum[:, 2 : 2 + heads_here, :head_part]

    kv_part = jnp.stack([done[layer]["in"][:, q_width:] for layer in range(LAYERS)])
    kv_full = jnp.zeros((LAYERS, shard_rows, 2 * KV * HD), wide)
    kv_full = lax.dynamic_update_slice_in_dim(kv_full, kv_part[..., :HD], kv_head * HD, 2)
    kv_full = lax.dynamic_update_slice_in_dim(kv_full, kv_part[..., HD:], (KV + kv_head) * HD, 2)
    kv_weight_grad, kv_bias_grad = lax.psum(
        (kv_full, small_sum[:, 2 + heads_here, :bias_part]), "tensor"
    )

    stack = lambda name, f=lambda a: a: jnp.stack([f(done[layer][name]) for layer in range(LAYERS)])
    grads = (
        gains_grad,
        stack("in", lambda a: a[:, :q_width]),
        query_bias_grad,
        kv_weight_grad,
        kv_bias_grad,
        stack("out", lambda a: a.T),
        jnp.stack([stack("gate"), stack("up")], axis=2),
        stack("down", lambda a: a.T),
    )
    params = (
        norm_gains,
        query_weight,
        query_bias,
        kv_weight,
        kv_bias,
        out_weight,
        gate_up_weight,
        down_weight,
    )
    firsts, seconds = moments[:8], moments[8:]
    decays = (0.0, 1.0, 0.0, 1.0, 0.0, 1.0, 1.0, 1.0)
    rates = (0.5, 0.02, 0.5, 0.02, 0.5, 0.1, 0.02, 0.02)
    moved = [
        adam_update(
            params[i].astype(wide), grads[i], firsts[i], seconds[i], decays[i], rates[i]
        )
        for i in range(8)
    ]
    return (
        block_out,
        input_grad,
        *grads,
        *[moved[i][0] for i in range(8)],
        *[moved[i][1] for i in range(8)],
        *[moved[i][2] for i in range(8)],
    )


def solution(mesh):
    params = (
        P(None, None, ("dp", "ctx")),
        P(None, ("dp", "ctx"), "tensor"),
        P(None, "tensor", ("dp", "ctx")),
        P(None, ("dp", "ctx"), None),
        P(None, ("dp", "ctx")),
        P(None, "tensor", ("dp", "ctx")),
        P(None, ("dp", "ctx"), None, "tensor"),
        P(None, "tensor", ("dp", "ctx")),
    )
    rows = P("dp", "ctx", None)
    sizes = (mesh.shape["dp"], mesh.shape["ctx"], mesh.shape["tensor"])
    return jax.shard_map(
        functools.partial(local, sizes),
        mesh=mesh,
        in_specs=(rows, P("dp", None), rows, *params, *params, *params),
        out_specs=(rows, rows, *params, *params, *params, *params),
        check_vma=False,
    )
```

```python
import functools

import jax
import jax.numpy as jnp
from jax import lax
from jax.experimental import pallas as pl
from jax.experimental.layout import Layout, with_layout_constraint
from jax.experimental.pallas import tpu as pltpu
from jax.sharding import PartitionSpec as P

H = 12
KV = 2
HD = 128
LAYERS = 2

NORM_EPS = 1e-06
ROPE_BASE = 1000000.0
MASK_FILL = -1e30
beta_first = 0.9
beta_second = 0.95
adam_eps = 1e-08
decay_rate = 0.1
adam_step = 3.0

MESH = pl.DeviceIdType.MESH
ROW_TILE = 16
Z_CHUNKS = 8
NEAR_LEAD, FAR_LAG, NEAR_LAG = 2, 6, 8


class Place:
    def __init__(self, sizes):
        self.dps, self.ctxs, self.tensors = sizes
        self.xs = self.dps // 2
        self.dp = lax.axis_index("dp")
        self.ctx = lax.axis_index("ctx")
        self.tensor = lax.axis_index("tensor")
        self.x = self.dp // 2
        self.core = self.dp % 2

    def x_at(self, step):
        return lax.rem(self.x + step, self.xs)

    def ctx_at(self, step):
        return lax.rem(self.ctx + step, self.ctxs)

    def shard(self, x, core, ctx):
        return (x * 2 + core) * self.ctxs + ctx

    def to_x(self, x):
        return {"dp": x * 2 + self.core}

    def to_ctx(self, ctx):
        return {"ctx": ctx}

    def to_core(self):
        return {"dp": self.x * 2 + 1 - self.core}

    def to_tensor(self, tensor):
        return {"tensor": tensor}


class Sems:
    def __init__(self, send, recv):
        self.send, self.recv, self.used = send, recv, 0

    def take(self, count=1):
        first = self.used
        self.used += count
        return first

    def remote(self, src, dst, device, slot=None):
        slot = self.take() if slot is None else slot
        return pltpu.make_async_remote_copy(
            src_ref=src,
            dst_ref=dst,
            send_sem=self.send.at[slot],
            recv_sem=self.recv.at[slot],
            device_id=device,
            device_id_type=MESH,
        )

    def local(self, src, dst):
        return pltpu.make_async_copy(src, dst, self.send.at[self.take()])


def half_rows(rows):
    return min(rows, (rows // 2 + ROW_TILE - 1) // ROW_TILE * ROW_TILE)


def gather_steps(place, sems, shard, whole):
    rows = shard.shape[0]
    cut = half_rows(rows)
    spans = [(0, cut), (cut, rows - cut)]
    xs, ctxs = range(1, place.xs), range(1, place.ctxs)
    me = place.shard(place.x, place.core, place.ctx)
    sent, kept = [], {}

    def part(index, span):
        return whole.at[index, pl.ds(span[0], span[1])]

    def first():
        for step in xs:
            kept["x", step] = sems.remote(shard, whole.at[me], place.to_x(place.x_at(step)))
        for step in ctxs:
            kept["ctx", step] = sems.remote(shard, whole.at[me], place.to_ctx(place.ctx_at(step)))
        kept["core"] = sems.remote(shard, whole.at[me], place.to_core())
        kept["own"] = sems.local(shard, whole.at[me])
        for copy in kept.values():
            copy.start()

    def forward(index, span, device):
        copy = sems.remote(part(index, span), part(index, span), device)
        copy.start()
        sent.append(copy)
        return copy

    def second():
        for step in xs:
            kept["x", step].wait_recv()
            index = place.shard(place.x_at(place.xs - step), place.core, place.ctx)
            for other in ctxs:
                kept["far", step, other, 0] = forward(index, spans[0], place.to_ctx(place.ctx_at(other)))
            forward(index, (0, rows), place.to_core())
        for step in ctxs:
            kept["ctx", step].wait_recv()
            index = place.shard(place.x, place.core, place.ctx_at(place.ctxs - step))
            if spans[1][1] > 0:
                for other in xs:
                    kept["far", other, step, 1] = forward(
                        index, spans[1], place.to_x(place.x_at(other))
                    )
            forward(index, (0, rows), place.to_core())

    def third():
        for step in xs:
            for other in ctxs:
                index = place.shard(
                    place.x_at(place.xs - step), place.core, place.ctx_at(place.ctxs - other)
                )
                kept["far", step, other, 0].wait_recv()
                if spans[1][1] > 0:
                    kept["far", step, other, 1].wait_recv()
                forward(index, (0, rows), place.to_core())

    def last():
        for name, copy in kept.items():
            if name == "own":
                copy.wait()
            elif name[0] in ("x", "ctx"):
                copy.wait_send()
        kept["core"].wait()
        far = [copy for name, copy in kept.items() if name[0] == "far"]
        for copy in sent:
            if any(copy is other for other in far):
                copy.wait_send()
            else:
                copy.wait()

    return [first, second, third, last]


def gather_sems(sizes):
    xs, ctxs = sizes[0] // 2 - 1, sizes[1] - 1
    return 2 + 2 * (xs + ctxs) + 3 * xs * ctxs


def add_rows(rows, body):
    @pl.loop(0, rows // ROW_TILE)
    def _(block):
        body(pl.ds(pl.multiple_of(block * ROW_TILE, ROW_TILE), ROW_TILE))


def scatter_buffers(sizes, shape, dtype):
    n, rows, cols = shape
    xs, ctxs = sizes[0] // 2, sizes[1]
    cut = half_rows(rows)
    far = max(1, (xs - 1) * (ctxs - 1))
    return [
        pltpu.VMEM((xs, ctxs, rows, cols), dtype),
        pltpu.VMEM((xs, ctxs, rows, cols), dtype),
        pltpu.VMEM((far, cut, cols), dtype),
        pltpu.VMEM((far, max(ROW_TILE, rows - cut), cols), dtype),
        pltpu.VMEM((max(1, xs - 1 + ctxs - 1), rows, cols), dtype),
    ]


def scatter_sems(sizes):
    xs, ctxs = sizes[0] // 2 - 1, sizes[1] - 1
    return 2 * (xs + 1) + (xs + ctxs) + 2 * xs * ctxs


def scatter_steps(place, sems, whole, out, mine, other, far_x, far_ctx, near):
    rows = out.shape[0]
    cut = half_rows(rows)
    xs, ctxs = range(1, place.xs), range(1, place.ctxs)
    ahead = lambda step, turn: (step - 1) * len(ctxs) + turn - 1
    loads, swaps, sent = {}, {}, []
    far, close = {}, {}
    wide = lambda ref, *at: ref[at].astype(jnp.float32)

    def first():
        for step in list(xs) + [0]:
            to = place.x_at(step)
            at = place.shard(to, 1 - place.core, 0)
            swaps[step] = sems.remote(
                whole.at[pl.ds(at, place.ctxs)], other.at[step], place.to_core()
            )
            swaps[step].start()
            at = place.shard(to, place.core, 0)
            loads[step] = sems.local(whole.at[pl.ds(at, place.ctxs)], mine.at[step])
            loads[step].start()

    def second():
        for step in xs:
            loads[step].wait()
            swaps[step].wait_recv()
            for turn in ctxs:
                ctx = place.ctx_at(turn)

                def add(span):
                    total = wide(mine, step, ctx, span) + wide(other, step, ctx, span)
                    mine[step, ctx, span] = total.astype(mine.dtype)

                add_rows(rows, add)
                slot = ahead(step, turn)
                far[step, turn, 0] = sems.remote(
                    mine.at[step, ctx, pl.ds(0, cut)], far_x.at[slot], place.to_ctx(ctx)
                )
                far[step, turn, 0].start()
                if rows > cut:
                    far[step, turn, 1] = sems.remote(
                        mine.at[step, ctx, pl.ds(cut, rows - cut)],
                        far_ctx.at[slot],
                        place.to_x(place.x_at(step)),
                    )
                    far[step, turn, 1].start()
        loads[0].wait()
        swaps[0].wait_recv()

    def third():
        for turn in ctxs:
            ctx = place.ctx_at(turn)
            if rows > cut:
                for step in xs:
                    far[step, turn, 1].wait_recv()

            def add_near(span):
                total = wide(mine, 0, ctx, span) + wide(other, 0, ctx, span)
                mine[0, ctx, span] = total.astype(mine.dtype)

            def add_far(block):
                span = pl.ds(pl.multiple_of(cut + block * ROW_TILE, ROW_TILE), ROW_TILE)
                here = pl.ds(pl.multiple_of(block * ROW_TILE, ROW_TILE), ROW_TILE)
                total = wide(mine, 0, ctx, span) + wide(other, 0, ctx, span)
                for step in xs:
                    total = total + wide(far_ctx, ahead(step, turn), here)
                mine[0, ctx, span] = total.astype(mine.dtype)

            add_rows(cut, add_near)
            if rows > cut:
                pl.loop(0, (rows - cut) // ROW_TILE)(add_far)
            slot = len(xs) + turn - 1
            close["ctx", turn] = sems.remote(mine.at[0, ctx], near.at[slot], place.to_ctx(ctx))
            close["ctx", turn].start()
        for step in xs:
            for turn in ctxs:
                far[step, turn, 0].wait_recv()

            def add_cut(span):
                total = wide(mine, step, place.ctx, span) + wide(other, step, place.ctx, span)
                for turn in ctxs:
                    total = total + wide(far_x, ahead(step, turn), span)
                mine[step, place.ctx, span] = total.astype(mine.dtype)

            def add_rest(block):
                span = pl.ds(pl.multiple_of(cut + block * ROW_TILE, ROW_TILE), ROW_TILE)
                total = wide(mine, step, place.ctx, span) + wide(other, step, place.ctx, span)
                mine[step, place.ctx, span] = total.astype(mine.dtype)

            add_rows(cut, add_cut)
            if rows > cut:
                pl.loop(0, (rows - cut) // ROW_TILE)(add_rest)
            close["x", step] = sems.remote(
                mine.at[step, place.ctx], near.at[step - 1], place.to_x(place.x_at(step))
            )
            close["x", step].start()

    def last():
        for copy in close.values():
            copy.wait_recv()

        def add_own(span):
            total = wide(mine, 0, place.ctx, span) + wide(other, 0, place.ctx, span)
            for slot in range(len(xs) + len(ctxs)):
                total = total + wide(near, slot, span)
            out[span] = total.astype(out.dtype)

        add_rows(rows, add_own)
        for copy in (*far.values(), *close.values(), *swaps.values()):
            copy.wait_send()

    return [first, second, third, last]


def line_steps(place, sems, part, out, recv, acc):
    rows = part.shape[0]
    size = rows // (2 * Z_CHUNKS)
    line = place.tensors
    me = place.tensor
    left = me < (line + 1) // 2
    hops = jnp.where(left, me, line - 1 - me)
    ahead = jnp.where(left, 1, -1)
    near = jnp.where(left, 0, 1)
    far = 1 - near
    onward = place.to_tensor(lax.clamp(0, me + ahead, line - 1))
    back = place.to_tensor(lax.clamp(0, me - ahead, line - 1))
    base = sems.take(4 * Z_CHUNKS)
    inner = hops > 0

    def span(flow, chunk):
        return pl.ds(pl.multiple_of((flow * Z_CHUNKS + chunk) * size, size), size)

    def summing(flow, chunk, src, device):
        return sems.remote(
            src.at[span(flow, chunk)],
            recv.at[span(flow, chunk)],
            device,
            base + flow * Z_CHUNKS + chunk,
        )

    def sharing(flow, chunk, device):
        return sems.remote(
            out.at[span(flow, chunk)],
            out.at[span(flow, chunk)],
            device,
            base + (2 + flow) * Z_CHUNKS + chunk,
        )

    def add(flow, chunk, into):
        at = span(flow, chunk)
        total = part[at].astype(jnp.float32) + recv[at].astype(jnp.float32)
        into[at] = total.astype(into.dtype)

    def begin():
        @pl.when(hops == 0)
        def _():
            for chunk in range(Z_CHUNKS):
                summing(near, chunk, part, onward).start()

    def step(turn):
        def run():
            chunk = turn + NEAR_LEAD
            if 0 <= chunk < Z_CHUNKS:

                @pl.when(inner)
                def _():
                    summing(near, chunk, part, onward).wait_recv()
                    add(near, chunk, acc)
                    summing(near, chunk, acc, onward).start()

            chunk = turn
            if 0 <= chunk < Z_CHUNKS:
                summing(far, chunk, acc, back).wait_recv()

                @pl.when(inner)
                def _():
                    add(far, chunk, acc)
                    summing(far, chunk, acc, back).start()

                @pl.when(hops == 0)
                def _():
                    add(far, chunk, out)
                    sharing(far, chunk, onward).start()

            chunk = turn - FAR_LAG
            if 0 <= chunk < Z_CHUNKS:

                @pl.when(inner)
                def _():
                    sharing(far, chunk, onward).wait_recv()
                    sharing(far, chunk, onward).start()

            chunk = turn - NEAR_LAG
            if 0 <= chunk < Z_CHUNKS:
                sharing(near, chunk, back).wait_recv()

                @pl.when(inner)
                def _():
                    sharing(near, chunk, back).start()

        return run

    def end():
        for chunk in range(Z_CHUNKS):
            summing(near, chunk, acc, onward).wait_send()
            sharing(far, chunk, onward).wait_send()

            @pl.when(inner)
            def _():
                summing(far, chunk, acc, back).wait_send()
                sharing(near, chunk, back).wait_send()

    return [begin] + [step(turn) for turn in range(-NEAR_LEAD, Z_CHUNKS + NEAR_LAG)] + [end]


def transfer_kernel(sizes, counts, plan, *refs):
    z_count, g_count, s_count, p_count, w_count = counts
    inputs = sum(counts)
    ins, outs, rest = refs[:inputs], refs[inputs : 2 * inputs], list(refs[2 * inputs :])
    place = Place(sizes)
    sems = Sems(rest.pop(), rest.pop())

    barrier = pltpu.get_barrier_semaphore()
    partners = []
    arrived = 0
    if g_count or s_count:
        partners.append(place.to_core())
        partners += [place.to_x(place.x_at(step)) for step in range(1, place.xs)]
    if g_count or s_count or p_count or w_count:
        partners += [place.to_ctx(place.ctx_at(step)) for step in range(1, place.ctxs)]
    for partner in partners:
        pl.semaphore_signal(barrier, inc=1, device_id=partner, device_id_type=MESH)
    arrived = len(partners)
    if z_count:
        above = place.tensor < place.tensors - 1
        below = place.tensor > 0

        @pl.when(above)
        def _():
            pl.semaphore_signal(
                barrier, inc=1, device_id=place.to_tensor(place.tensor + 1), device_id_type=MESH
            )

        @pl.when(below)
        def _():
            pl.semaphore_signal(
                barrier, inc=1, device_id=place.to_tensor(place.tensor - 1), device_id_type=MESH
            )

        arrived = arrived + above.astype(jnp.int32) + below.astype(jnp.int32)
    pl.semaphore_wait(barrier, arrived)

    ins, outs = list(ins), list(outs)
    lines, planes, ends = [], [], []
    for _ in range(z_count):
        lines.append(line_steps(place, sems, ins.pop(0), outs.pop(0), rest.pop(0), rest.pop(0)))
    for _ in range(g_count):
        planes.append(gather_steps(place, sems, ins.pop(0), outs.pop(0)))
    for _ in range(s_count):
        buffers = [rest.pop(0) for _ in range(5)]
        planes.append(scatter_steps(place, sems, ins.pop(0), outs.pop(0), *buffers))
    small = []
    for index in range(p_count + w_count):
        src, dst = ins.pop(0), outs.pop(0)
        mine = place.ctx
        for step in range(1, place.ctxs):
            to = place.ctx_at(step)
            block = src if index < p_count else src.at[to]
            small.append(sems.remote(block, dst.at[mine], place.to_ctx(to)))
        block = src if index < p_count else src.at[mine]
        small.append(sems.local(block, dst.at[mine]))
    for copy in small:
        copy.start()
    for plane in planes:
        plane[0]()
    turns = max([len(line) for line in lines], default=0)
    for turn in range(turns + 1):
        for plane, at in zip(planes, plan):
            for stage in (1, 2):
                if min(at[stage - 1], turns) == turn:
                    plane[stage]()
        for line in lines:
            if turn < len(line):
                line[turn]()
    for plane in planes:
        plane[3]()
    for copy in small:
        copy.wait()


def transfer(sizes, number, z_sums=(), gathers=(), scatters=(), pieces=(), swaps=(), plan=((99, 99),) * 8):
    n = sizes[0] * sizes[1]
    any_space = pl.BlockSpec(memory_space=pl.ANY)
    in_vmem = pl.BlockSpec(memory_space=pltpu.VMEM)
    args = (*z_sums, *gathers, *scatters, *pieces, *swaps)
    in_specs = [in_vmem] * len(z_sums) + [any_space] * (len(args) - len(z_sums))
    out_specs = (
        [in_vmem] * len(z_sums)
        + [any_space] * len(gathers)
        + [in_vmem] * len(scatters)
        + [any_space] * (len(pieces) + len(swaps))
    )
    out_shape = (
        [jax.ShapeDtypeStruct(a.shape, a.dtype) for a in z_sums]
        + [jax.ShapeDtypeStruct((n, *a.shape), a.dtype) for a in gathers]
        + [jax.ShapeDtypeStruct(a.shape[1:], jnp.float32) for a in scatters]
        + [jax.ShapeDtypeStruct((sizes[1], *a.shape), a.dtype) for a in pieces]
        + [jax.ShapeDtypeStruct(a.shape, a.dtype) for a in swaps]
    )
    scratch = []
    for a in z_sums:
        scratch += [pltpu.VMEM(a.shape, a.dtype)] * 2
    for a in scatters:
        scratch += scatter_buffers(sizes, a.shape, a.dtype)
    count = (
        4 * Z_CHUNKS * len(z_sums)
        + gather_sems(sizes) * len(gathers)
        + scatter_sems(sizes) * len(scatters)
        + sizes[1] * (len(pieces) + len(swaps))
    )
    scratch += [pltpu.SemaphoreType.DMA((count,)), pltpu.SemaphoreType.DMA((count,))]
    counts = (len(z_sums), len(gathers), len(scatters), len(pieces), len(swaps))
    return pl.pallas_call(
        functools.partial(transfer_kernel, sizes, counts, plan),
        out_shape=out_shape,
        in_specs=in_specs,
        out_specs=out_specs,
        scratch_shapes=scratch,
        compiler_params=pltpu.CompilerParams(
            collective_id=number, has_side_effects=True, vmem_limit_bytes=56 << 20
        ),
        name="transfer%d" % number,
    )(*args)


TILE = 256


def mm(lhs, rhs, over):
    return lax.dot_general(
        lhs, rhs, (((over[0],), (over[1],)), ((), ())), preferred_element_type=jnp.float32
    )


def in_width(block, width):
    column = pl.program_id(0) * TILE + lax.broadcasted_iota(jnp.int32, block.shape, 1)
    return jnp.where(column < width, block, jnp.zeros_like(block))


def forward_tile(width, n2, w_gate, w_up, w_down, gate_out, up_out, inner_out, part_out, total):
    tile = pl.program_id(0)
    gate = mm(n2[...], w_gate[...], (1, 0))
    up = mm(n2[...], w_up[...], (1, 0))
    gate_out[...] = gate
    up_out[...] = up
    inner = in_width(gate * jax.nn.sigmoid(gate) * up, width).astype(jnp.bfloat16)
    inner_out[...] = inner
    product = mm(inner, in_width(w_down[...], width), (1, 1))

    @pl.when(tile == 0)
    def _():
        total[...] = product

    @pl.when(tile > 0)
    def _():
        total[...] += product

    @pl.when(tile == pl.num_programs(0) - 1)
    def _():
        part_out[...] = total[...].astype(part_out.dtype)


def forward_ffn(n2, w_gate, w_up, w_down):
    rows, model_width = n2.shape
    width = w_gate.shape[1]
    whole = pl.BlockSpec((rows, model_width), lambda j: (0, 0))
    weight = pl.BlockSpec((model_width, TILE), lambda j: (0, j))
    units = pl.BlockSpec((rows, TILE), lambda j: (0, j))
    return pl.pallas_call(
        functools.partial(forward_tile, width),
        grid=(pl.cdiv(width, TILE),),
        in_specs=[whole, weight, weight, weight],
        out_specs=[units, units, units, whole],
        out_shape=[
            jax.ShapeDtypeStruct((rows, width), jnp.float32),
            jax.ShapeDtypeStruct((rows, width), jnp.float32),
            jax.ShapeDtypeStruct((rows, width), jnp.bfloat16),
            jax.ShapeDtypeStruct((rows, model_width), jnp.bfloat16),
        ],
        scratch_shapes=[pltpu.VMEM((rows, model_width), jnp.float32)],
        compiler_params=pltpu.CompilerParams(vmem_limit_bytes=56 << 20),
        name="forward_ffn",
    )(n2, w_gate, w_up, w_down)


def backward_tile(
    width,
    grad,
    n2,
    gate_in,
    up_in,
    inner,
    w_gate,
    w_up,
    w_down,
    down_out,
    gate_out,
    up_out,
    part_out,
    grad_t,
    n2_t,
    total,
):
    tile = pl.program_id(0)

    @pl.when(tile == 0)
    def _():
        grad_t[...] = grad[...].T
        n2_t[...] = n2[...].T

    gate = gate_in[...]
    slope = jax.nn.sigmoid(gate)
    grad_inner = mm(grad[...], w_down[...], (1, 0))
    down_out[...] = mm(grad_t[...], inner[...], (1, 0)).astype(down_out.dtype)
    grad_gate = grad_inner * up_in[...] * slope * (1.0 + gate * (1.0 - slope))
    grad_gate = in_width(grad_gate, width).astype(jnp.bfloat16)
    grad_up = in_width(grad_inner * gate * slope, width).astype(jnp.bfloat16)
    product = mm(grad_gate, in_width(w_gate[...], width), (1, 1))
    product += mm(grad_up, in_width(w_up[...], width), (1, 1))

    @pl.when(tile == 0)
    def _():
        total[...] = product

    @pl.when(tile > 0)
    def _():
        total[...] += product

    gate_out[...] = mm(n2_t[...], grad_gate, (1, 0)).astype(gate_out.dtype)
    up_out[...] = mm(n2_t[...], grad_up, (1, 0)).astype(up_out.dtype)

    @pl.when(tile == pl.num_programs(0) - 1)
    def _():
        part_out[...] = total[...].astype(part_out.dtype)


def backward_ffn(grad, n2, gate, up, inner, w_gate, w_up, w_down):
    rows, model_width = n2.shape
    width = w_gate.shape[1]
    whole = pl.BlockSpec((rows, model_width), lambda j: (0, 0))
    weight = pl.BlockSpec((model_width, TILE), lambda j: (0, j))
    units = pl.BlockSpec((rows, TILE), lambda j: (0, j))
    like = jax.ShapeDtypeStruct((model_width, width), jnp.bfloat16)
    return pl.pallas_call(
        functools.partial(backward_tile, width),
        grid=(pl.cdiv(width, TILE),),
        in_specs=[whole, whole, units, units, units, weight, weight, weight],
        out_specs=[weight, weight, weight, whole],
        out_shape=[like, like, like, jax.ShapeDtypeStruct((rows, model_width), jnp.bfloat16)],
        scratch_shapes=[
            pltpu.VMEM((model_width, rows), jnp.bfloat16),
            pltpu.VMEM((model_width, rows), jnp.bfloat16),
            pltpu.VMEM((rows, model_width), jnp.float32),
        ],
        compiler_params=pltpu.CompilerParams(vmem_limit_bytes=56 << 20),
        name="backward_ffn",
    )(grad, n2, gate, up, inner, w_gate, w_up, w_down)


def rotate(values, cosine, sine):
    half_width = values.shape[-1] // 2
    first_half = values[..., :half_width]
    second_half = values[..., half_width:]
    return jnp.concatenate(
        [first_half * cosine - second_half * sine, second_half * cosine + first_half * sine],
        axis=-1,
    )


def rotate_back(grad_rows, cosine, sine):
    return rotate(grad_rows, cosine, -sine)


def norm_back(values, norm_scale, gain, grad_rows):
    weighted = grad_rows * gain
    inner_mean = jnp.mean(weighted * values, axis=-1, keepdims=True)
    grad_values = (
        norm_scale * weighted - values * (norm_scale * norm_scale * norm_scale) * inner_mean
    )
    return (grad_values, jnp.sum(grad_rows * values * norm_scale, axis=0))


def adam_update(weight, gradient, first_old, second_old, decayed, step_rate):
    first_new = beta_first * first_old + (1.0 - beta_first) * gradient
    second_new = beta_second * second_old + (1.0 - beta_second) * gradient * gradient
    mean_hat = first_new / (1.0 - beta_first**adam_step)
    square_hat = second_new / (1.0 - beta_second**adam_step)
    new_weight = weight - step_rate * (
        mean_hat / (jnp.sqrt(square_hat) + adam_eps) + decayed * decay_rate * weight
    )
    return (first_new, second_new, new_weight)


def dot(lhs, rhs, over):
    return lax.dot_general(lhs, rhs, ((over[0:1], over[1:2]), ((), ())), preferred_element_type=jnp.float32)


def masked_scores(queries, all_keys, allowed, score_scale):
    scores = (
        jnp.einsum("sqhd,skd->shqk", queries, all_keys, preferred_element_type=jnp.float32)
        * score_scale
    )
    return jnp.where(allowed, scores, MASK_FILL)


def local(
    sizes,
    hidden_in,
    segment_ids,
    out_grad,
    norm_gains,
    query_weight,
    query_bias,
    kv_weight,
    kv_bias,
    out_weight,
    gate_up_weight,
    down_weight,
    *moments,
):
    low = jnp.bfloat16
    wide = jnp.float32
    dps, ctxs, tensors = sizes
    n = dps * ctxs
    seq_count, local_len, model_width = hidden_in.shape
    seq_length = segment_ids.shape[1]
    row_count = seq_count * local_len
    shard_rows = query_weight.shape[1]
    heads_here = query_weight.shape[2] // HD
    q_width = heads_here * HD
    hidden_units = down_weight.shape[1]
    local_start = lax.axis_index("ctx") * local_len
    kv_head = lax.axis_index("tensor") * heads_here // (H // KV)
    score_scale = HD ** (-0.5)
    numbers = iter(range(1, 100))

    def move(**what):
        return transfer(sizes, next(numbers), **what)

    attention_shards = [
        jnp.concatenate(
            [
                query_weight[layer],
                lax.dynamic_slice_in_dim(kv_weight[layer], kv_head * HD, HD, 1),
                lax.dynamic_slice_in_dim(kv_weight[layer], (KV + kv_head) * HD, HD, 1),
                out_weight[layer].T,
            ],
            axis=1,
        )
        for layer in range(LAYERS)
    ]
    gate_shards = [gate_up_weight[layer, :, 0] for layer in range(LAYERS)]
    up_shards = [gate_up_weight[layer, :, 1] for layer in range(LAYERS)]
    down_shards = [down_weight[layer].T for layer in range(LAYERS)]

    bias_part = kv_bias.shape[1]
    head_part = query_bias.shape[2]
    small_width = -(-max(shard_rows, bias_part) // 128) * 128
    pad = lambda a: jnp.pad(a, ((0, 0), (0, small_width - a.shape[1])))
    small_rows = LAYERS * (2 + heads_here + 1)
    small_shard = jnp.pad(
        jnp.concatenate(
            [
                pad(norm_gains.reshape(LAYERS * 2, shard_rows)),
                pad(query_bias.reshape(LAYERS * heads_here, head_part)),
                pad(kv_bias),
            ],
            axis=0,
        ),
        ((0, -small_rows % ROW_TILE), (0, 0)),
    )

    small, attention_weights = move(gathers=[small_shard, attention_shards[0]])
    at = LAYERS * 2
    gains = (
        small[:, :at, :shard_rows]
        .transpose(1, 0, 2)
        .reshape(LAYERS, 2, model_width)
        .astype(wide)
    )
    q_biases = (
        small[:, at : at + LAYERS * heads_here, :head_part]
        .transpose(1, 0, 2)
        .reshape(LAYERS, q_width)
        .astype(wide)
    )
    at += LAYERS * heads_here
    kv_biases = small[:, at : at + LAYERS, :bias_part].transpose(1, 0, 2).reshape(LAYERS, 2 * KV, HD)
    kv_biases = jnp.concatenate(
        [
            lax.dynamic_slice_in_dim(kv_biases, kv_head, 1, 1)[:, 0],
            lax.dynamic_slice_in_dim(kv_biases, KV + kv_head, 1, 1)[:, 0],
        ],
        axis=1,
    ).astype(wide)

    own_segments = lax.dynamic_slice_in_dim(segment_ids, local_start, local_len, 1)
    earlier = jnp.sum(
        (segment_ids[:, None, :] < own_segments[:, :, None]).astype(jnp.int32), axis=-1
    )
    token_index = local_start + jnp.arange(local_len, dtype=jnp.int32)
    position = (token_index[None, :] - earlier).astype(wide)
    frequency = ROPE_BASE ** (-jnp.arange(HD // 2, dtype=wide) / (HD // 2))
    angles = position[..., None] * frequency
    cosine = jnp.cos(angles).reshape(row_count, 1, HD // 2)
    sine = jnp.sin(angles).reshape(row_count, 1, HD // 2)
    key_index = jnp.arange(seq_length, dtype=jnp.int32)
    allowed = (own_segments[:, :, None] == segment_ids[:, None, :]) & (
        key_index[None, None, :] <= token_index[None, :, None]
    )
    allowed = allowed[:, None]

    hidden = hidden_in.astype(wide).reshape(row_count, model_width)
    stored = []
    gate_weights = up_weights = down_weights = None
    for layer in range(LAYERS):
        w_attention = attention_weights.reshape(model_width, q_width + 2 * HD + q_width)
        w_in = w_attention[:, : q_width + 2 * HD]
        w_out = w_attention[:, q_width + 2 * HD :]
        scale_one = lax.rsqrt(jnp.mean(hidden * hidden, axis=-1, keepdims=True) + NORM_EPS)
        normed = (hidden * scale_one * gains[layer, 0]).astype(low)
        lin = dot(normed, w_in, (1, 0)) + jnp.concatenate([q_biases[layer], kv_biases[layer]])
        lin_heads = lin[:, : q_width + HD].reshape(row_count, heads_here + 1, HD)
        turned = rotate(lin_heads, cosine, sine).astype(low)
        queries = turned[:, :heads_here].reshape(seq_count, local_len, heads_here, HD)
        pair = jnp.concatenate([turned[:, heads_here], lin[:, q_width + HD :].astype(low)], axis=1)
        if layer == 0:
            down_weights, pairs = move(gathers=[down_shards[0]], pieces=[pair])
        else:
            (pairs,) = move(pieces=[pair])
        pairs = (
            pairs.reshape(ctxs, seq_count, local_len, 2 * HD)
            .transpose(1, 0, 2, 3)
            .reshape(seq_count, seq_length, 2 * HD)
        )
        all_keys, all_values = pairs[..., :HD], pairs[..., HD:]
        scores = masked_scores(queries, all_keys, allowed, score_scale)
        row_max = jnp.max(scores, axis=-1, keepdims=True)
        exp_scores = jnp.exp(scores - row_max)
        row_total = jnp.sum(exp_scores, axis=-1, keepdims=True)
        weights = exp_scores / row_total
        log_total = row_max + jnp.log(row_total)
        mixture = jnp.einsum(
            "shqk,skd->sqhd", weights.astype(low), all_values, preferred_element_type=wide
        )
        mixed_low = mixture.reshape(row_count, q_width).astype(low)
        part = dot(mixed_low, w_out, (1, 1)).astype(low)
        total, gate_weights, up_weights = move(
            z_sums=[part],
            gathers=[gate_shards[layer], up_shards[layer]],
            plan=((15, 99), (16, 99)),
        )
        w_gate = gate_weights.reshape(model_width, hidden_units)
        w_up = up_weights.reshape(model_width, hidden_units)
        w_down = down_weights.reshape(model_width, hidden_units)
        middle = hidden + total.astype(wide)
        scale_two = lax.rsqrt(jnp.mean(middle * middle, axis=-1, keepdims=True) + NORM_EPS)
        normed_two = (middle * scale_two * gains[layer, 1]).astype(low)
        gate, up, inner_low, part = forward_ffn(normed_two, w_gate, w_up, w_down)
        stored.append(
            (
                hidden,
                scale_one,
                normed,
                queries,
                all_keys,
                all_values,
                log_total,
                mixed_low,
                middle,
                scale_two,
                normed_two,
                gate,
                up,
                inner_low,
                w_in,
                w_out,
                w_gate,
                w_up,
                w_down,
            )
        )
        if layer + 1 < LAYERS:
            total, attention_weights, down_weights = move(
                z_sums=[part],
                gathers=[attention_shards[layer + 1], down_shards[layer + 1]],
                plan=((7, 17), (12, 18)),
            )
            hidden = middle + total.astype(wide)
        else:
            last_part = part

    def split(gradient):
        return gradient.astype(low).reshape(n, shard_rows, gradient.shape[1])

    def by_owner(row, width):
        return jnp.pad(row.reshape(n, 1, width), ((0, 0), (0, 0), (0, small_width - width)))

    grad_hidden = out_grad.astype(wide).reshape(row_count, model_width)
    done = [{} for _ in range(LAYERS)]
    small_grads = [None] * LAYERS
    waiting = []
    for layer in reversed(range(LAYERS)):
        (
            layer_input,
            scale_one,
            normed,
            queries,
            all_keys,
            all_values,
            log_total,
            mixed_low,
            middle,
            scale_two,
            normed_two,
            gate,
            up,
            inner_low,
            w_in,
            w_out,
            w_gate,
            w_up,
            w_down,
        ) = stored[layer]
        grad_low = grad_hidden.astype(low)
        grad_down_w, grad_gate_w, grad_up_w, part = backward_ffn(
            grad_low, normed_two, gate, up, inner_low, w_gate, w_up, w_down
        )
        grad_down_w, grad_gate_w, grad_up_w = (
            split(grad) for grad in (grad_down_w, grad_gate_w, grad_up_w)
        )
        waiting += [("gate", layer, grad_gate_w)]
        if layer > 0:
            waiting += [("down", layer, grad_down_w)]
        total, *rest = move(
            z_sums=[part],
            scatters=[a for _, _, a in waiting],
            plan=((4, 13), (5, 15)) if layer > 0 else ((3, 8), (4, 9), (5, 15)),
        )
        for (name, owner, _), result in zip(waiting, rest):
            done[owner][name] = result
        back_two, grad_gain_two = norm_back(middle, scale_two, gains[layer, 1], total.astype(wide))
        grad_middle = grad_hidden + back_two
        grad_mid_low = grad_middle.astype(low)
        grad_out_w = split(dot(grad_mid_low, mixed_low, (0, 0)))
        grad_mixed = (
            dot(grad_mid_low, w_out, (1, 0))
            .astype(low)
            .reshape(seq_count, local_len, heads_here, HD)
        )
        scores = masked_scores(queries, all_keys, allowed, score_scale)
        probabilities = jnp.exp(scores - log_total)
        grad_probs = jnp.einsum(
            "sqhd,skd->shqk", grad_mixed, all_values, preferred_element_type=wide
        )
        row_delta = jnp.sum(probabilities * grad_probs, axis=-1, keepdims=True)
        grad_scores = (probabilities * (grad_probs - row_delta)).astype(low)
        grad_queries = (
            jnp.einsum("shqk,skd->sqhd", grad_scores, all_keys, preferred_element_type=wide)
            * score_scale
        )
        grad_keys = (
            jnp.einsum("shqk,sqhd->skd", grad_scores, queries, preferred_element_type=wide)
            * score_scale
        )
        grad_values = jnp.einsum(
            "shqk,sqhd->skd", probabilities.astype(low), grad_mixed, preferred_element_type=wide
        )
        grad_pair = jnp.concatenate([grad_keys, grad_values], axis=2).astype(low)
        grad_pair = (
            grad_pair.reshape(seq_count, ctxs, local_len, 2 * HD)
            .transpose(1, 0, 2, 3)
            .reshape(ctxs, row_count, 2 * HD)
        )
        (grad_pair,) = move(swaps=[grad_pair])
        grad_pair = jnp.sum(grad_pair.astype(wide), axis=0)
        grad_heads = jnp.concatenate(
            [grad_queries.reshape(row_count, heads_here, HD), grad_pair[:, None, :HD]], axis=1
        )
        grad_lin = jnp.concatenate(
            [
                rotate_back(grad_heads, cosine, sine).reshape(row_count, q_width + HD),
                grad_pair[:, HD:],
            ],
            axis=1,
        ).astype(low)
        grad_in_w = split(dot(normed, grad_lin, (0, 0)))
        grad_bias = jnp.sum(grad_lin.astype(wide), axis=0)
        part = dot(grad_lin, w_in, (1, 1)).astype(low)
        zeros = jnp.zeros((2 * KV, HD), wide)
        kv_bias_grad = lax.dynamic_update_slice_in_dim(
            zeros, grad_bias[q_width : q_width + HD][None], kv_head, 0
        )
        kv_bias_grad = lax.dynamic_update_slice_in_dim(
            kv_bias_grad, grad_bias[q_width + HD :][None], KV + kv_head, 0
        )
        head_rows = grad_bias[:q_width].reshape(heads_here, HD)
        small_grads[layer] = [grad_gain_two, head_rows, kv_bias_grad.reshape(-1)]
        if layer > 0:
            total, done[layer]["up"] = move(
                z_sums=[part], scatters=[grad_up_w], plan=((3, 10),)
            )
            waiting = [("out", layer, grad_out_w), ("in", layer, grad_in_w)]
        else:
            total, block_sum, *rest = move(
                z_sums=[part, last_part],
                scatters=[grad_up_w, grad_down_w, grad_in_w, grad_out_w],
                plan=((4, 10), (5, 12), (5, 13), (6, 14)),
            )
            done[layer]["up"], done[layer]["down"], done[layer]["in"], done[layer]["out"] = rest
        back_one, grad_gain_one = norm_back(
            layer_input, scale_one, gains[layer, 0], total.astype(wide)
        )
        small_grads[layer].insert(0, grad_gain_one)
        grad_hidden = grad_middle + back_one

    block_out = (stored[-1][8] + block_sum.astype(wide)).astype(low)
    block_out = block_out.reshape(seq_count, local_len, model_width)
    input_grad = grad_hidden.reshape(seq_count, local_len, model_width)

    small_part = []
    for layer in range(LAYERS):
        gain_one, gain_two, head_rows, kv_row = small_grads[layer]
        small_part += [by_owner(gain_one, shard_rows), by_owner(gain_two, shard_rows)]
        small_part += [by_owner(head_rows[head], head_part) for head in range(heads_here)]
        small_part.append(by_owner(kv_row, bias_part))
    small_part = jnp.pad(
        jnp.concatenate(small_part, axis=1), ((0, 0), (0, -small_rows % ROW_TILE), (0, 0))
    ).astype(low)
    (small_sum,) = move(scatters=[small_part])
    small_sum = small_sum[:small_rows].reshape(LAYERS, 2 + heads_here + 1, small_width)
    gains_grad = small_sum[:, :2, :shard_rows]
    query_bias_grad = small_sum[:, 2 : 2 + heads_here, :head_part]

    kv_part = jnp.stack([done[layer]["in"][:, q_width:] for layer in range(LAYERS)])
    kv_full = jnp.zeros((LAYERS, shard_rows, 2 * KV * HD), wide)
    kv_full = lax.dynamic_update_slice_in_dim(kv_full, kv_part[..., :HD], kv_head * HD, 2)
    kv_full = lax.dynamic_update_slice_in_dim(kv_full, kv_part[..., HD:], (KV + kv_head) * HD, 2)
    kv_weight_grad, kv_bias_grad = lax.psum(
        (kv_full, small_sum[:, 2 + heads_here, :bias_part]), "tensor"
    )

    stack = lambda name, f=lambda a: a: jnp.stack([f(done[layer][name]) for layer in range(LAYERS)])
    gate_up_grad = jnp.stack(
        [
            jnp.stack([done[layer]["gate"], done[layer]["up"]], axis=1)
            for layer in range(LAYERS)
        ]
    )
    gate_up_grad = lax.optimization_barrier(
        with_layout_constraint(gate_up_grad, Layout((0, 1, 2, 3)))
    )
    grads = (
        gains_grad,
        stack("in", lambda a: a[:, :q_width]),
        query_bias_grad,
        kv_weight_grad,
        kv_bias_grad,
        stack("out", lambda a: a.T),
        gate_up_grad,
        stack("down", lambda a: a.T),
    )
    params = (
        norm_gains,
        query_weight,
        query_bias,
        kv_weight,
        kv_bias,
        out_weight,
        gate_up_weight,
        down_weight,
    )
    firsts, seconds = moments[:8], moments[8:]
    decays = (0.0, 1.0, 0.0, 1.0, 0.0, 1.0, 1.0, 1.0)
    rates = (0.5, 0.02, 0.5, 0.02, 0.5, 0.1, 0.02, 0.02)
    moved = [
        adam_update(
            params[i].astype(wide), grads[i], firsts[i], seconds[i], decays[i], rates[i]
        )
        for i in range(8)
    ]
    return (
        block_out,
        input_grad,
        *grads,
        *[moved[i][0] for i in range(8)],
        *[moved[i][1] for i in range(8)],
        *[moved[i][2] for i in range(8)],
    )


def solution(mesh):
    params = (
        P(None, None, ("dp", "ctx")),
        P(None, ("dp", "ctx"), "tensor"),
        P(None, "tensor", ("dp", "ctx")),
        P(None, ("dp", "ctx"), None),
        P(None, ("dp", "ctx")),
        P(None, "tensor", ("dp", "ctx")),
        P(None, ("dp", "ctx"), None, "tensor"),
        P(None, "tensor", ("dp", "ctx")),
    )
    rows = P("dp", "ctx", None)
    sizes = (mesh.shape["dp"], mesh.shape["ctx"], mesh.shape["tensor"])
    return jax.shard_map(
        functools.partial(local, sizes),
        mesh=mesh,
        in_specs=(rows, P("dp", None), rows, *params, *params, *params),
        out_specs=(rows, rows, *params, *params, *params, *params),
        check_vma=False,
    )
```

```python
import functools

import jax
import jax.numpy as jnp
from jax import lax
from jax.experimental import pallas as pl
from jax.experimental.layout import Layout, with_layout_constraint
from jax.experimental.pallas import tpu as pltpu
from jax.sharding import PartitionSpec as P

H = 12
KV = 2
HD = 128
LAYERS = 2

NORM_EPS = 1e-06
ROPE_BASE = 1000000.0
MASK_FILL = -1e30
beta_first = 0.9
beta_second = 0.95
adam_eps = 1e-08
decay_rate = 0.1
adam_step = 3.0

MESH = pl.DeviceIdType.MESH
ROW_TILE = 16
Z_CHUNKS = 8
NEAR_LEAD, FAR_LAG, NEAR_LAG = 2, 6, 8


class Place:
    def __init__(self, sizes):
        self.dps, self.ctxs, self.tensors = sizes
        self.xs = self.dps // 2
        self.dp = lax.axis_index("dp")
        self.ctx = lax.axis_index("ctx")
        self.tensor = lax.axis_index("tensor")
        self.x = self.dp // 2
        self.core = self.dp % 2

    def x_at(self, step):
        return lax.rem(self.x + step, self.xs)

    def ctx_at(self, step):
        return lax.rem(self.ctx + step, self.ctxs)

    def shard(self, x, core, ctx):
        return (x * 2 + core) * self.ctxs + ctx

    def to_x(self, x):
        return {"dp": x * 2 + self.core}

    def to_ctx(self, ctx):
        return {"ctx": ctx}

    def to_core(self):
        return {"dp": self.x * 2 + 1 - self.core}

    def to_tensor(self, tensor):
        return {"tensor": tensor}


class Sems:
    def __init__(self, send, recv):
        self.send, self.recv, self.used = send, recv, 0

    def take(self, count=1):
        first = self.used
        self.used += count
        return first

    def remote(self, src, dst, device, slot=None):
        slot = self.take() if slot is None else slot
        return pltpu.make_async_remote_copy(
            src_ref=src,
            dst_ref=dst,
            send_sem=self.send.at[slot],
            recv_sem=self.recv.at[slot],
            device_id=device,
            device_id_type=MESH,
        )

    def local(self, src, dst):
        return pltpu.make_async_copy(src, dst, self.send.at[self.take()])


def half_rows(rows):
    return min(rows, (rows // 2 + ROW_TILE - 1) // ROW_TILE * ROW_TILE)


def gather_steps(place, sems, shard, whole):
    rows = shard.shape[0]
    cut = half_rows(rows)
    spans = [(0, cut), (cut, rows - cut)]
    xs, ctxs = range(1, place.xs), range(1, place.ctxs)
    me = place.shard(place.x, place.core, place.ctx)
    sent, kept = [], {}

    def part(index, span):
        return whole.at[index, pl.ds(span[0], span[1])]

    def first():
        for step in xs:
            kept["x", step] = sems.remote(shard, whole.at[me], place.to_x(place.x_at(step)))
        for step in ctxs:
            kept["ctx", step] = sems.remote(shard, whole.at[me], place.to_ctx(place.ctx_at(step)))
        kept["core"] = sems.remote(shard, whole.at[me], place.to_core())
        kept["own"] = sems.local(shard, whole.at[me])
        for copy in kept.values():
            copy.start()

    def forward(index, span, device):
        copy = sems.remote(part(index, span), part(index, span), device)
        copy.start()
        sent.append(copy)
        return copy

    def second():
        for step in xs:
            kept["x", step].wait_recv()
            index = place.shard(place.x_at(place.xs - step), place.core, place.ctx)
            for other in ctxs:
                kept["far", step, other, 0] = forward(index, spans[0], place.to_ctx(place.ctx_at(other)))
            forward(index, (0, rows), place.to_core())
        for step in ctxs:
            kept["ctx", step].wait_recv()
            index = place.shard(place.x, place.core, place.ctx_at(place.ctxs - step))
            if spans[1][1] > 0:
                for other in xs:
                    kept["far", other, step, 1] = forward(
                        index, spans[1], place.to_x(place.x_at(other))
                    )
            forward(index, (0, rows), place.to_core())

    def third():
        for step in xs:
            for other in ctxs:
                index = place.shard(
                    place.x_at(place.xs - step), place.core, place.ctx_at(place.ctxs - other)
                )
                kept["far", step, other, 0].wait_recv()
                if spans[1][1] > 0:
                    kept["far", step, other, 1].wait_recv()
                forward(index, (0, rows), place.to_core())

    def last():
        for name, copy in kept.items():
            if name == "own":
                copy.wait()
            elif name[0] in ("x", "ctx"):
                copy.wait_send()
        kept["core"].wait()
        far = [copy for name, copy in kept.items() if name[0] == "far"]
        for copy in sent:
            if any(copy is other for other in far):
                copy.wait_send()
            else:
                copy.wait()

    return [first, second, third, last]


def gather_sems(sizes):
    xs, ctxs = sizes[0] // 2 - 1, sizes[1] - 1
    return 2 + 2 * (xs + ctxs) + 3 * xs * ctxs


def add_rows(rows, body):
    @pl.loop(0, rows // ROW_TILE)
    def _(block):
        body(pl.ds(pl.multiple_of(block * ROW_TILE, ROW_TILE), ROW_TILE))


def scatter_buffers(sizes, shape, dtype):
    n, rows, cols = shape
    xs, ctxs = sizes[0] // 2, sizes[1]
    cut = half_rows(rows)
    far = max(1, (xs - 1) * (ctxs - 1))
    return [
        pltpu.VMEM((xs, ctxs, rows, cols), dtype),
        pltpu.VMEM((xs, ctxs, rows, cols), dtype),
        pltpu.VMEM((far, cut, cols), dtype),
        pltpu.VMEM((far, max(ROW_TILE, rows - cut), cols), dtype),
        pltpu.VMEM((max(1, xs - 1 + ctxs - 1), rows, cols), dtype),
    ]


def scatter_sems(sizes):
    xs, ctxs = sizes[0] // 2 - 1, sizes[1] - 1
    return 2 * (xs + 1) + (xs + ctxs) + 2 * xs * ctxs


def scatter_steps(place, sems, whole, out, mine, other, far_x, far_ctx, near):
    rows = out.shape[0]
    cut = half_rows(rows)
    xs, ctxs = range(1, place.xs), range(1, place.ctxs)
    ahead = lambda step, turn: (step - 1) * len(ctxs) + turn - 1
    loads, swaps, sent = {}, {}, []
    far, close = {}, {}
    wide = lambda ref, *at: ref[at].astype(jnp.float32)

    def first():
        for step in list(xs) + [0]:
            to = place.x_at(step)
            at = place.shard(to, 1 - place.core, 0)
            swaps[step] = sems.remote(
                whole.at[pl.ds(at, place.ctxs)], other.at[step], place.to_core()
            )
            swaps[step].start()
            at = place.shard(to, place.core, 0)
            loads[step] = sems.local(whole.at[pl.ds(at, place.ctxs)], mine.at[step])
            loads[step].start()

    def second():
        for step in xs:
            loads[step].wait()
            swaps[step].wait_recv()
            for turn in ctxs:
                ctx = place.ctx_at(turn)

                def add(span):
                    total = wide(mine, step, ctx, span) + wide(other, step, ctx, span)
                    mine[step, ctx, span] = total.astype(mine.dtype)

                add_rows(rows, add)
                slot = ahead(step, turn)
                far[step, turn, 0] = sems.remote(
                    mine.at[step, ctx, pl.ds(0, cut)], far_x.at[slot], place.to_ctx(ctx)
                )
                far[step, turn, 0].start()
                if rows > cut:
                    far[step, turn, 1] = sems.remote(
                        mine.at[step, ctx, pl.ds(cut, rows - cut)],
                        far_ctx.at[slot],
                        place.to_x(place.x_at(step)),
                    )
                    far[step, turn, 1].start()
        loads[0].wait()
        swaps[0].wait_recv()

    def third():
        for turn in ctxs:
            ctx = place.ctx_at(turn)
            if rows > cut:
                for step in xs:
                    far[step, turn, 1].wait_recv()

            def add_near(span):
                total = wide(mine, 0, ctx, span) + wide(other, 0, ctx, span)
                mine[0, ctx, span] = total.astype(mine.dtype)

            def add_far(block):
                span = pl.ds(pl.multiple_of(cut + block * ROW_TILE, ROW_TILE), ROW_TILE)
                here = pl.ds(pl.multiple_of(block * ROW_TILE, ROW_TILE), ROW_TILE)
                total = wide(mine, 0, ctx, span) + wide(other, 0, ctx, span)
                for step in xs:
                    total = total + wide(far_ctx, ahead(step, turn), here)
                mine[0, ctx, span] = total.astype(mine.dtype)

            add_rows(cut, add_near)
            if rows > cut:
                pl.loop(0, (rows - cut) // ROW_TILE)(add_far)
            slot = len(xs) + turn - 1
            close["ctx", turn] = sems.remote(mine.at[0, ctx], near.at[slot], place.to_ctx(ctx))
            close["ctx", turn].start()
        for step in xs:
            for turn in ctxs:
                far[step, turn, 0].wait_recv()

            def add_cut(span):
                total = wide(mine, step, place.ctx, span) + wide(other, step, place.ctx, span)
                for turn in ctxs:
                    total = total + wide(far_x, ahead(step, turn), span)
                mine[step, place.ctx, span] = total.astype(mine.dtype)

            def add_rest(block):
                span = pl.ds(pl.multiple_of(cut + block * ROW_TILE, ROW_TILE), ROW_TILE)
                total = wide(mine, step, place.ctx, span) + wide(other, step, place.ctx, span)
                mine[step, place.ctx, span] = total.astype(mine.dtype)

            add_rows(cut, add_cut)
            if rows > cut:
                pl.loop(0, (rows - cut) // ROW_TILE)(add_rest)
            close["x", step] = sems.remote(
                mine.at[step, place.ctx], near.at[step - 1], place.to_x(place.x_at(step))
            )
            close["x", step].start()

    def last():
        for copy in close.values():
            copy.wait_recv()

        def add_own(span):
            total = wide(mine, 0, place.ctx, span) + wide(other, 0, place.ctx, span)
            for slot in range(len(xs) + len(ctxs)):
                total = total + wide(near, slot, span)
            out[span] = total.astype(out.dtype)

        add_rows(rows, add_own)
        for copy in (*far.values(), *close.values(), *swaps.values()):
            copy.wait_send()

    return [first, second, third, last]


def line_steps(place, sems, part, out, recv, acc):
    rows = part.shape[0]
    size = rows // (2 * Z_CHUNKS)
    line = place.tensors
    me = place.tensor
    left = me < (line + 1) // 2
    hops = jnp.where(left, me, line - 1 - me)
    ahead = jnp.where(left, 1, -1)
    near = jnp.where(left, 0, 1)
    far = 1 - near
    onward = place.to_tensor(lax.clamp(0, me + ahead, line - 1))
    back = place.to_tensor(lax.clamp(0, me - ahead, line - 1))
    base = sems.take(4 * Z_CHUNKS)
    inner = hops > 0

    def span(flow, chunk):
        return pl.ds(pl.multiple_of((flow * Z_CHUNKS + chunk) * size, size), size)

    def summing(flow, chunk, src, device):
        return sems.remote(
            src.at[span(flow, chunk)],
            recv.at[span(flow, chunk)],
            device,
            base + flow * Z_CHUNKS + chunk,
        )

    def sharing(flow, chunk, device):
        return sems.remote(
            out.at[span(flow, chunk)],
            out.at[span(flow, chunk)],
            device,
            base + (2 + flow) * Z_CHUNKS + chunk,
        )

    def add(flow, chunk, into):
        at = span(flow, chunk)
        total = part[at].astype(jnp.float32) + recv[at].astype(jnp.float32)
        into[at] = total.astype(into.dtype)

    def begin():
        @pl.when(hops == 0)
        def _():
            for chunk in range(Z_CHUNKS):
                summing(near, chunk, part, onward).start()

    def step(turn):
        def run():
            chunk = turn + NEAR_LEAD
            if 0 <= chunk < Z_CHUNKS:

                @pl.when(inner)
                def _():
                    summing(near, chunk, part, onward).wait_recv()
                    add(near, chunk, acc)
                    summing(near, chunk, acc, onward).start()

            chunk = turn
            if 0 <= chunk < Z_CHUNKS:
                summing(far, chunk, acc, back).wait_recv()

                @pl.when(inner)
                def _():
                    add(far, chunk, acc)
                    summing(far, chunk, acc, back).start()

                @pl.when(hops == 0)
                def _():
                    add(far, chunk, out)
                    sharing(far, chunk, onward).start()

            chunk = turn - FAR_LAG
            if 0 <= chunk < Z_CHUNKS:

                @pl.when(inner)
                def _():
                    sharing(far, chunk, onward).wait_recv()
                    sharing(far, chunk, onward).start()

            chunk = turn - NEAR_LAG
            if 0 <= chunk < Z_CHUNKS:
                sharing(near, chunk, back).wait_recv()

                @pl.when(inner)
                def _():
                    sharing(near, chunk, back).start()

        return run

    def end():
        for chunk in range(Z_CHUNKS):
            summing(near, chunk, acc, onward).wait_send()
            sharing(far, chunk, onward).wait_send()

            @pl.when(inner)
            def _():
                summing(far, chunk, acc, back).wait_send()
                sharing(near, chunk, back).wait_send()

    return [begin] + [step(turn) for turn in range(-NEAR_LEAD, Z_CHUNKS + NEAR_LAG)] + [end]


class Work:
    def __init__(self, body, inputs, outputs, scratch, sems, part, makes=()):
        self.body, self.inputs, self.outputs = body, inputs, outputs
        self.scratch, self.sems, self.part, self.makes = scratch, sems, part, makes


def take(refs, count):
    taken, refs[:count] = refs[:count], []
    return taken


def greet(place, plane, ctx, line):
    barrier = pltpu.get_barrier_semaphore()
    partners = []
    if plane:
        partners.append(place.to_core())
        partners += [place.to_x(place.x_at(step)) for step in range(1, place.xs)]
    if ctx:
        partners += [place.to_ctx(place.ctx_at(step)) for step in range(1, place.ctxs)]
    for partner in partners:
        pl.semaphore_signal(barrier, inc=1, device_id=partner, device_id_type=MESH)
    arrived = len(partners)
    if line:
        above = place.tensor < place.tensors - 1
        below = place.tensor > 0

        @pl.when(above)
        def _():
            pl.semaphore_signal(
                barrier, inc=1, device_id=place.to_tensor(place.tensor + 1), device_id_type=MESH
            )

        @pl.when(below)
        def _():
            pl.semaphore_signal(
                barrier, inc=1, device_id=place.to_tensor(place.tensor - 1), device_id_type=MESH
            )

        arrived = arrived + above.astype(jnp.int32) + below.astype(jnp.int32)
    pl.semaphore_wait(barrier, arrived)


def transfer_kernel(sizes, counts, plan, work, *refs):
    z_count, g_count, s_count, p_count, w_count = counts
    refs = list(refs)
    given = 0 if work else z_count
    ins = take(refs, sum(counts) - z_count + given - (len(work.makes) if work else 0))
    work_ins = take(refs, len(work.inputs)) if work else []
    outs = take(refs, sum(counts))
    work_outs = take(refs, len(work.outputs)) if work else []
    sem_refs = refs[-2:]
    rest = refs[:-2]
    place = Place(sizes)
    sems = Sems(*sem_refs)
    plane = bool(g_count or s_count)
    greet(place, plane, plane or p_count or w_count or work, z_count)

    lines, planes = [], []
    parts = take(rest, 1) if work else take(ins, z_count)
    for part in parts:
        lines.append(line_steps(place, sems, part, outs.pop(0), rest.pop(0), rest.pop(0)))
    for _ in range(g_count):
        planes.append(gather_steps(place, sems, ins.pop(0), outs.pop(0)))
    made = take(rest, len(work.makes)) if work else []
    for index in range(s_count):
        early = index < s_count - len(made)
        source = ins.pop(0) if early else made[index - s_count]
        planes.append(scatter_steps(place, sems, source, outs.pop(0), *take(rest, 5)))
    late = len(planes) - len(made)
    small = []
    for index in range(p_count + w_count):
        src, dst = ins.pop(0), outs.pop(0)
        mine = place.ctx
        for step in range(1, place.ctxs):
            to = place.ctx_at(step)
            block = src if index < p_count else src.at[to]
            small.append(sems.remote(block, dst.at[mine], place.to_ctx(to)))
        block = src if index < p_count else src.at[mine]
        small.append(sems.local(block, dst.at[mine]))
    for copy in small:
        copy.start()
    body = iter(())
    if work:
        body = work.body(place, sems, work_ins, work_outs, rest, parts[0], *made)
    next(body, None)
    for steps in planes[:late]:
        steps[0]()
    next(body, None)
    for steps, at in zip(planes, plan):
        if at[0] < 0:
            steps[1]()
    next(body, None)
    turns = max([len(line) for line in lines], default=0)
    for turn in range(turns + 1):
        if turn == 1 and made:
            next(body, None)
            for steps in planes[late:]:
                steps[0]()
        for steps, at in zip(planes, plan):
            for stage in (1, 2):
                if min(at[stage - 1], turns) == turn:
                    steps[stage]()
        for line in lines:
            if turn < len(line):
                line[turn]()
    for steps in planes:
        steps[3]()
    for copy in small:
        copy.wait()


def transfer(
    sizes,
    number,
    z_sums=(),
    gathers=(),
    scatters=(),
    pieces=(),
    swaps=(),
    plan=((99, 99),) * 8,
    work=None,
):
    n = sizes[0] * sizes[1]
    any_space = pl.BlockSpec(memory_space=pl.ANY)
    in_vmem = pl.BlockSpec(memory_space=pltpu.VMEM)
    given = () if work else z_sums
    early = len(scatters)
    if work:
        z_sums = (work.part,)
        scatters = (*scatters, *work.makes)
    args = (*given, *gathers, *scatters[:early], *pieces, *swaps)
    in_specs = [in_vmem] * len(given) + [any_space] * (len(args) - len(given))
    out_specs = (
        [in_vmem] * len(z_sums)
        + [any_space] * len(gathers)
        + [in_vmem] * len(scatters)
        + [any_space] * (len(pieces) + len(swaps))
    )
    out_shape = (
        [jax.ShapeDtypeStruct(a.shape, a.dtype) for a in z_sums]
        + [jax.ShapeDtypeStruct((n, *a.shape), a.dtype) for a in gathers]
        + [jax.ShapeDtypeStruct(a.shape[1:], jnp.float32) for a in scatters]
        + [jax.ShapeDtypeStruct((sizes[1], *a.shape), a.dtype) for a in pieces]
        + [jax.ShapeDtypeStruct(a.shape, a.dtype) for a in swaps]
    )
    scratch = []
    if work:
        args += tuple(work.inputs)
        in_specs += [in_vmem] * len(work.inputs)
        out_specs += [in_vmem] * len(work.outputs)
        out_shape += work.outputs
        scratch.append(pltpu.VMEM(work.part.shape, work.part.dtype))
    for a in z_sums:
        scratch += [pltpu.VMEM(a.shape, a.dtype)] * 2
    if work:
        scratch += [pltpu.VMEM(a.shape, a.dtype) for a in work.makes]
    for a in scatters:
        scratch += scatter_buffers(sizes, a.shape, a.dtype)
    count = (
        4 * Z_CHUNKS * len(z_sums)
        + gather_sems(sizes) * len(gathers)
        + scatter_sems(sizes) * len(scatters)
        + sizes[1] * (len(pieces) + len(swaps))
    )
    if work:
        scratch += work.scratch
        count += work.sems
    scratch += [pltpu.SemaphoreType.DMA((count,)), pltpu.SemaphoreType.DMA((count,))]
    counts = (len(z_sums), len(gathers), len(scatters), len(pieces), len(swaps))
    return pl.pallas_call(
        functools.partial(transfer_kernel, sizes, counts, plan, work),
        out_shape=out_shape,
        in_specs=in_specs,
        out_specs=out_specs,
        scratch_shapes=scratch,
        compiler_params=pltpu.CompilerParams(
            collective_id=number, has_side_effects=True, vmem_limit_bytes=62 << 20
        ),
        cost_estimate=pl.CostEstimate(
            flops=30_000_000_000, bytes_accessed=150_000_000, transcendentals=0
        ),
        name="transfer%d" % number,
    )(*args)


def mm(lhs, rhs, over):
    return lax.dot_general(
        lhs, rhs, (((over[0],), (over[1],)), ((), ())), preferred_element_type=jnp.float32
    )


def turn_heads(values, cosine, sine):
    return values * cosine + pltpu.roll(values, HD // 2, 1) * sine


def allowed_pairs(place, query_segments, key_segments, local_len):
    shape = (local_len, key_segments.shape[1])
    query = place.ctx * local_len + lax.broadcasted_iota(jnp.int32, shape, 0)
    key = lax.broadcasted_iota(jnp.int32, shape, 1)
    return jnp.logical_and(query_segments == key_segments, key <= query)


def sequence_pairs(pairs, sequence, local_len, column):
    block = pairs[:, pl.ds(sequence * local_len, local_len), pl.ds(column * HD, HD)]
    return block.reshape(-1, HD)


def attend(seq_count, place, sems, ins, outs, scratch, part):
    normed, w_attention, bias, cosine, sine, query_segments, key_segments = ins
    queries, pairs, log_total, mixed = outs
    rows = normed.shape[0]
    local_len = rows // seq_count
    q_width = queries.shape[1]
    heads = q_width // HD
    cos, sin = cosine[...], sine[...]
    columns = pl.ds(q_width, 2 * HD)
    lin = mm(normed[...], w_attention[:, columns], (1, 0)) + bias[:, columns]
    me = place.ctx
    pairs[me, :, :HD] = turn_heads(lin[:, :HD], cos, sin).astype(jnp.bfloat16)
    pairs[me, :, HD:] = lin[:, HD:].astype(jnp.bfloat16)
    sent = [
        sems.remote(pairs.at[me], pairs.at[me], place.to_ctx(place.ctx_at(step)))
        for step in range(1, place.ctxs)
    ]
    for copy in sent:
        copy.start()
    yield
    yield
    lin = mm(normed[...], w_attention[:, :q_width], (1, 0)) + bias[:, :q_width]
    for index in range(heads):
        columns = slice(index * HD, (index + 1) * HD)
        queries[:, columns] = turn_heads(lin[:, columns], cos, sin).astype(jnp.bfloat16)
    for copy in sent:
        copy.wait()
    for sequence in range(seq_count):
        span = pl.ds(sequence * local_len, local_len)
        allowed = allowed_pairs(
            place, query_segments[span, :], key_segments[pl.ds(sequence, 1), :], local_len
        )
        keys = sequence_pairs(pairs, sequence, local_len, 0)
        values = sequence_pairs(pairs, sequence, local_len, 1)
        for index in range(heads):
            columns = pl.ds(index * HD, HD)
            scores = mm(queries[span, columns], keys, (1, 1)) * HD ** (-0.5)
            scores = jnp.where(allowed, scores, MASK_FILL)
            row_max = jnp.max(scores, axis=1, keepdims=True)
            exp_scores = jnp.exp(scores - row_max)
            row_total = jnp.sum(exp_scores, axis=1, keepdims=True)
            weights = (exp_scores / row_total).astype(jnp.bfloat16)
            log_total[span, pl.ds(index, 1)] = row_max + jnp.log(row_total)
            mixed[span, columns] = mm(weights, values, (1, 0)).astype(jnp.bfloat16)
    w_out = w_attention[:, q_width + 2 * HD :]
    part[...] = mm(mixed[...], w_out, (1, 1)).astype(part.dtype)


def attend_back(seq_count, place, sems, ins, outs, scratch, part, in_grad, out_grad):
    grad, normed, w_attention, cosine, sine, query_segments, key_segments = ins[:7]
    queries, pairs, log_total, mixed = ins[7:]
    (lin_grad,) = outs
    mixed_grad, pair_grad, got = scratch
    rows = grad.shape[0]
    local_len = rows // seq_count
    q_width = queries.shape[1]
    heads = q_width // HD
    scale = HD ** (-0.5)
    yield
    cos, sin = cosine[...], -sine[...]
    w_in = w_attention[:, : q_width + 2 * HD]
    w_out = w_attention[:, q_width + 2 * HD :]
    mixed_grad[...] = mm(grad[...], w_out, (1, 0)).astype(jnp.bfloat16)
    totals = log_total[...].T
    for sequence in range(seq_count):
        first = sequence * local_len
        span = pl.ds(first, local_len)
        keys = sequence_pairs(pairs, sequence, local_len, 0)
        values = sequence_pairs(pairs, sequence, local_len, 1)
        shape = (keys.shape[0], local_len)
        key = lax.broadcasted_iota(jnp.int32, shape, 0)
        query = place.ctx * local_len + lax.broadcasted_iota(jnp.int32, shape, 1)
        same = key_segments[:, pl.ds(sequence, 1)] == query_segments[:, span]
        allowed = jnp.logical_and(same, key <= query)
        key_grad = value_grad = None
        for index in range(heads):
            columns = pl.ds(index * HD, HD)
            query_rows = queries[span, columns]
            grad_rows = mixed_grad[span, columns]
            scores = mm(keys, query_rows, (1, 1)) * scale
            scores = jnp.where(allowed, scores, MASK_FILL)
            weights = jnp.exp(scores - totals[index : index + 1, first : first + local_len])
            weight_grads = mm(values, grad_rows, (1, 1))
            row_delta = jnp.sum(weights * weight_grads, axis=0, keepdims=True)
            score_grads = (weights * (weight_grads - row_delta)).astype(jnp.bfloat16)
            for_keys = mm(score_grads, query_rows, (1, 0))
            for_values = mm(weights.astype(jnp.bfloat16), grad_rows, (1, 0))
            key_grad = for_keys if key_grad is None else key_grad + for_keys
            value_grad = for_values if value_grad is None else value_grad + for_values
            query_grad = mm(score_grads, keys, (0, 0)) * scale
            lin_grad[span, columns] = turn_heads(
                query_grad, cosine[span, :], -sine[span, :]
            ).astype(jnp.bfloat16)
        pieces = (place.ctxs, local_len, HD)
        pair_grad[:, span, :HD] = (key_grad * scale).astype(jnp.bfloat16).reshape(pieces)
        pair_grad[:, span, HD:] = value_grad.astype(jnp.bfloat16).reshape(pieces)
    sent = []
    for step in range(1, place.ctxs):
        to = place.ctx_at(step)
        sent.append(sems.remote(pair_grad.at[to], got.at[step - 1], place.to_ctx(to)))
        sent[-1].start()
    yield
    total = pair_grad[place.ctx].astype(jnp.float32)
    for step, copy in enumerate(sent):
        copy.wait()
        total = total + got[step].astype(jnp.float32)
    lin_grad[:, pl.ds(q_width, HD)] = turn_heads(total[:, :HD], cos, sin).astype(jnp.bfloat16)
    lin_grad[:, pl.ds(q_width + HD, HD)] = total[:, HD:].astype(jnp.bfloat16)
    part[...] = mm(lin_grad[...], w_in, (1, 1)).astype(part.dtype)
    yield
    product = mm(normed[...], lin_grad[...], (0, 0)).astype(in_grad.dtype)
    in_grad[...] = product.reshape(in_grad.shape)
    product = mm(grad[...], mixed[...], (0, 0)).astype(out_grad.dtype)
    out_grad[...] = product.reshape(out_grad.shape)


def finish_kernel(sizes, *refs):
    refs = list(refs)
    gain_grads = take(refs, 2 * LAYERS)
    lin_grads = take(refs, LAYERS)
    in_grads = take(refs, LAYERS)
    sums, kv_parts, kv_rows, rows, send, recv = refs
    place = Place(sizes)
    sems = Sems(send, recv)
    shard_rows, width = in_grads[0].shape
    q_width = width - 2 * HD
    group = H // KV
    heads = q_width // HD
    dps, ctxs, tensors = sizes
    at = lambda index, step, size: lax.rem(index + step, size)
    line = [place.to_tensor(at(place.tensor, step, tensors)) for step in range(1, tensors)]
    plane = [
        {"dp": at(place.dp, step, dps), "ctx": at(place.ctx, turn, ctxs)}
        for step in range(dps)
        for turn in range(ctxs)
        if step or turn
    ]
    barrier = pltpu.get_barrier_semaphore()
    for device in line + plane:
        pl.semaphore_signal(barrier, inc=1, device_id=device, device_id_type=MESH)

    me = place.tensor
    here = place.dp * ctxs + place.ctx
    kv_rows[me] = jnp.zeros(kv_rows.shape[1:], jnp.float32)
    rows[here] = jnp.zeros(rows.shape[1:], jnp.float32)
    for layer in range(LAYERS):
        span = pl.ds(layer * shard_rows, shard_rows)
        kv_parts[me, span, :] = in_grads[layer][:, q_width:].astype(kv_parts.dtype)
        bias = jnp.sum(lin_grads[layer][...].astype(jnp.float32), axis=0, keepdims=True)
        kv_rows[me, pl.ds(layer, 1), :] = bias[:, q_width:]
        rows[here, pl.ds(2 * LAYERS + layer, 1), pl.ds(0, q_width)] = bias[:, :q_width]
    for index, gain in enumerate(gain_grads):
        rows[here, pl.ds(index, 1), :] = gain[...]
    pl.semaphore_wait(barrier, len(line) + len(plane))

    big = [sems.remote(kv_parts.at[me], kv_parts.at[me], device) for device in line]
    first = [sems.remote(kv_rows.at[me], kv_rows.at[me], device) for device in line]
    for copy in first + big:
        copy.start()
    for copy in first:
        copy.wait()
    for head in range(KV):
        owners = [t for t in range(tensors) if t * heads // group == head]
        total = sum(kv_rows[t, pl.ds(0, LAYERS), :] for t in owners)
        span = pl.ds(3 * LAYERS, LAYERS)
        rows[here, span, pl.ds(head * HD, HD)] = total[:, :HD]
        rows[here, span, pl.ds((KV + head) * HD, HD)] = total[:, HD:]
    second = [sems.remote(rows.at[here], rows.at[here], device) for device in plane]
    for copy in second:
        copy.start()
    for copy in second:
        copy.wait()
    total = rows[0]
    for index in range(1, dps * ctxs):
        total = total + rows[index]
    sums[...] = total
    for copy in big:
        copy.wait()


def finish(sizes, number, gain_grads, lin_grads, in_grads):
    dps, ctxs, tensors = sizes
    in_vmem = pl.BlockSpec(memory_space=pltpu.VMEM)
    args = (*[gain[None] for gain in gain_grads], *lin_grads, *in_grads)
    height, width = -(-4 * LAYERS // 8) * 8, gain_grads[0].shape[0]
    count = 2 * (tensors - 1) + dps * ctxs - 1
    return pl.pallas_call(
        functools.partial(finish_kernel, sizes),
        out_shape=[
            jax.ShapeDtypeStruct((height, width), jnp.float32),
            jax.ShapeDtypeStruct((tensors, LAYERS * in_grads[0].shape[0], 2 * HD), jnp.bfloat16),
        ],
        in_specs=[in_vmem] * len(args),
        out_specs=[in_vmem] * 2,
        scratch_shapes=[
            pltpu.VMEM((tensors, 8, 2 * HD), jnp.float32),
            pltpu.VMEM((dps * ctxs, height, width), jnp.float32),
            pltpu.SemaphoreType.DMA((count,)),
            pltpu.SemaphoreType.DMA((count,)),
        ],
        compiler_params=pltpu.CompilerParams(
            collective_id=number, has_side_effects=True, vmem_limit_bytes=32 << 20
        ),
        name="finish",
    )(*args)


def adam_update(weight, gradient, first_old, second_old, decayed, step_rate):
    first_new = beta_first * first_old + (1.0 - beta_first) * gradient
    second_new = beta_second * second_old + (1.0 - beta_second) * gradient * gradient
    mean_hat = first_new / (1.0 - beta_first**adam_step)
    square_hat = second_new / (1.0 - beta_second**adam_step)
    new_weight = weight - step_rate * (
        mean_hat / (jnp.sqrt(square_hat) + adam_eps) + decayed * decay_rate * weight
    )
    return (first_new, second_new, new_weight)


def pair_adam_block(step_rate, weight, first, second, *rest):
    grads, outs = rest[: 2 * LAYERS], rest[2 * LAYERS :]
    for layer in range(LAYERS):

        @pl.when(pl.program_id(0) == layer)
        def _():
            gate, up = grads[2 * layer], grads[2 * layer + 1]
            grad = jnp.stack([gate[...], up[...]], axis=1)[None]
            moved = adam_update(
                weight[...].astype(jnp.float32), grad, first[...], second[...], 1.0, step_rate
            )
            for out, value in zip(outs, (grad, *moved)):
                out[...] = value


def pair_adam(weight, first, second, grads, step_rate):
    layers, rows, _, columns = weight.shape
    size = rows // (4 if rows % 64 == 0 else 3)
    last = rows // size - 1
    block = pl.BlockSpec((1, size, 2, columns), lambda layer, i: (layer, i, 0, 0))

    def grad_block(own):
        at = lambda layer, i: (jnp.where(layer == own, i, jnp.where(layer < own, 0, last)), 0)
        return pl.BlockSpec((size, columns), at)

    return pl.pallas_call(
        functools.partial(pair_adam_block, step_rate),
        grid=(layers, rows // size),
        in_specs=[block] * 3 + [grad_block(own) for own in range(layers) for _ in range(2)],
        out_specs=[block] * 4,
        out_shape=[jax.ShapeDtypeStruct(weight.shape, jnp.float32)] * 4,
        compiler_params=pltpu.CompilerParams(vmem_limit_bytes=56 << 20),
        name="pair_adam",
    )(weight, first, second, *grads)


TILE = 256
DOWN_TILES = 4


def in_width(block, width):
    column = pl.program_id(0) * TILE + lax.broadcasted_iota(jnp.int32, block.shape, 1)
    return jnp.where(column < width, block, jnp.zeros_like(block))


def forward_tile(width, n2, w_gate, w_up, w_down, gate_out, up_out, inner_out, part_out, total):
    tile = pl.program_id(0)
    gate = mm(n2[...], w_gate[...], (1, 0))
    up = mm(n2[...], w_up[...], (1, 0))
    gate_out[...] = gate
    up_out[...] = up
    inner = in_width(gate * jax.nn.sigmoid(gate) * up, width).astype(jnp.bfloat16)
    inner_out[...] = inner
    product = mm(inner, in_width(w_down[...], width), (1, 1))

    @pl.when(tile == 0)
    def _():
        total[...] = product

    @pl.when(tile > 0)
    def _():
        total[...] += product

    @pl.when(tile == pl.num_programs(0) - 1)
    def _():
        part_out[...] = total[...].astype(part_out.dtype)


def forward_ffn(n2, w_gate, w_up, w_down):
    rows, model_width = n2.shape
    width = w_gate.shape[1]
    whole = pl.BlockSpec((rows, model_width), lambda j: (0, 0))
    weight = pl.BlockSpec((model_width, TILE), lambda j: (0, j))
    units = pl.BlockSpec((rows, TILE), lambda j: (0, j))
    return pl.pallas_call(
        functools.partial(forward_tile, width),
        grid=(pl.cdiv(width, TILE),),
        in_specs=[whole, weight, weight, weight],
        out_specs=[units, units, units, whole],
        out_shape=[
            jax.ShapeDtypeStruct((rows, width), jnp.float32),
            jax.ShapeDtypeStruct((rows, width), jnp.float32),
            jax.ShapeDtypeStruct((rows, width), jnp.bfloat16),
            jax.ShapeDtypeStruct((rows, model_width), jnp.bfloat16),
        ],
        scratch_shapes=[pltpu.VMEM((rows, model_width), jnp.float32)],
        compiler_params=pltpu.CompilerParams(vmem_limit_bytes=56 << 20),
        name="forward_ffn",
    )(n2, w_gate, w_up, w_down)


def backward_tile(
    width,
    grad,
    n2,
    gate_in,
    up_in,
    inner,
    w_gate,
    w_up,
    w_down,
    down_out,
    down_rest,
    gate_out,
    up_out,
    part_out,
    grad_t,
    n2_t,
    total,
):
    tile = pl.program_id(0)

    @pl.when(tile == 0)
    def _():
        grad_t[...] = grad[...].T
        n2_t[...] = n2[...].T

    gate = gate_in[...]
    slope = jax.nn.sigmoid(gate)
    grad_inner = mm(grad[...], w_down[...], (1, 0))
    down_grad = mm(grad_t[...], inner[...], (1, 0)).astype(down_out.dtype)

    @pl.when(tile < DOWN_TILES)
    def _():
        down_out[...] = down_grad

    @pl.when(tile >= DOWN_TILES)
    def _():
        down_rest[...] = down_grad

    grad_gate = grad_inner * up_in[...] * slope * (1.0 + gate * (1.0 - slope))
    grad_gate = in_width(grad_gate, width).astype(jnp.bfloat16)
    grad_up = in_width(grad_inner * gate * slope, width).astype(jnp.bfloat16)
    product = mm(grad_gate, in_width(w_gate[...], width), (1, 1))
    product += mm(grad_up, in_width(w_up[...], width), (1, 1))

    @pl.when(tile == 0)
    def _():
        total[...] = product

    @pl.when(tile > 0)
    def _():
        total[...] += product

    gate_out[...] = mm(n2_t[...], grad_gate, (1, 0)).astype(gate_out.dtype)
    up_out[...] = mm(n2_t[...], grad_up, (1, 0)).astype(up_out.dtype)

    @pl.when(tile == pl.num_programs(0) - 1)
    def _():
        part_out[...] = total[...].astype(part_out.dtype)


def backward_ffn(grad, n2, gate, up, inner, w_gate, w_up, w_down):
    rows, model_width = n2.shape
    width = w_gate.shape[1]
    whole = pl.BlockSpec((rows, model_width), lambda j: (0, 0))
    weight = pl.BlockSpec((model_width, TILE), lambda j: (0, j))
    units = pl.BlockSpec((rows, TILE), lambda j: (0, j))
    like = lambda size: jax.ShapeDtypeStruct((model_width, size), jnp.bfloat16)
    cut = DOWN_TILES * TILE
    before = pl.BlockSpec((model_width, TILE), lambda j: (0, jnp.minimum(j, DOWN_TILES - 1)))
    behind = pl.BlockSpec((model_width, TILE), lambda j: (0, jnp.maximum(j - DOWN_TILES, 0)))
    return pl.pallas_call(
        functools.partial(backward_tile, width),
        grid=(pl.cdiv(width, TILE),),
        in_specs=[whole, whole, units, units, units, weight, weight, weight],
        out_specs=[before, behind, weight, weight, whole],
        out_shape=[
            like(cut),
            like(width - cut),
            like(width),
            like(width),
            jax.ShapeDtypeStruct((rows, model_width), jnp.bfloat16),
        ],
        scratch_shapes=[
            pltpu.VMEM((model_width, rows), jnp.bfloat16),
            pltpu.VMEM((model_width, rows), jnp.bfloat16),
            pltpu.VMEM((rows, model_width), jnp.float32),
        ],
        compiler_params=pltpu.CompilerParams(vmem_limit_bytes=56 << 20),
        name="backward_ffn",
    )(grad, n2, gate, up, inner, w_gate, w_up, w_down)


def rotate(values, cosine, sine):
    half_width = values.shape[-1] // 2
    first_half = values[..., :half_width]
    second_half = values[..., half_width:]
    return jnp.concatenate(
        [first_half * cosine - second_half * sine, second_half * cosine + first_half * sine],
        axis=-1,
    )


def rotate_back(grad_rows, cosine, sine):
    return rotate(grad_rows, cosine, -sine)


def norm_back(values, norm_scale, gain, grad_rows):
    weighted = grad_rows * gain
    inner_mean = jnp.mean(weighted * values, axis=-1, keepdims=True)
    grad_values = (
        norm_scale * weighted - values * (norm_scale * norm_scale * norm_scale) * inner_mean
    )
    return (grad_values, jnp.sum(grad_rows * values * norm_scale, axis=0))


def local(
    sizes,
    hidden_in,
    segment_ids,
    out_grad,
    norm_gains,
    query_weight,
    query_bias,
    kv_weight,
    kv_bias,
    out_weight,
    gate_up_weight,
    down_weight,
    *moments,
):
    low = jnp.bfloat16
    wide = jnp.float32
    dps, ctxs, tensors = sizes
    n = dps * ctxs
    seq_count, local_len, model_width = hidden_in.shape
    seq_length = segment_ids.shape[1]
    row_count = seq_count * local_len
    shard_rows = query_weight.shape[1]
    heads_here = query_weight.shape[2] // HD
    q_width = heads_here * HD
    hidden_units = down_weight.shape[1]
    local_start = lax.axis_index("ctx") * local_len
    kv_head = lax.axis_index("tensor") * heads_here // (H // KV)
    score_scale = HD ** (-0.5)
    numbers = iter(range(1, 100))

    def move(**what):
        return transfer(sizes, next(numbers), **what)

    attention_shards = [
        jnp.concatenate(
            [
                query_weight[layer],
                lax.dynamic_slice_in_dim(kv_weight[layer], kv_head * HD, HD, 1),
                lax.dynamic_slice_in_dim(kv_weight[layer], (KV + kv_head) * HD, HD, 1),
                out_weight[layer].T,
            ],
            axis=1,
        )
        for layer in range(LAYERS)
    ]
    down_shards = [down_weight[layer].T for layer in range(LAYERS)]

    def after(array, *earlier):
        return lax.optimization_barrier((array, *earlier))[0]

    def gather(shard):
        return lax.all_gather(shard, ("dp", "ctx"), axis=0, tiled=True)

    def scatter(gradient):
        return lax.psum_scatter(gradient, ("dp", "ctx"), scatter_dimension=0, tiled=True)

    bias_part = kv_bias.shape[1]
    head_part = query_bias.shape[2]
    small_width = -(-max(shard_rows, bias_part) // 128) * 128
    pad = lambda a: jnp.pad(a, ((0, 0), (0, small_width - a.shape[1])))
    small_rows = LAYERS * (2 + heads_here + 1)
    small_shard = jnp.pad(
        jnp.concatenate(
            [
                pad(norm_gains.reshape(LAYERS * 2, shard_rows)),
                pad(query_bias.reshape(LAYERS * heads_here, head_part)),
                pad(kv_bias),
            ],
            axis=0,
        ),
        ((0, -small_rows % ROW_TILE), (0, 0)),
    )

    small, attention_weights = move(gathers=[small_shard, attention_shards[0]])
    gate_up = after(gate_up_weight, small)
    gate_shards = [after(gate_up[layer, :, 0]) for layer in range(LAYERS)]
    up_shards = [after(gate_up[layer, :, 1]) for layer in range(LAYERS)]
    at = LAYERS * 2
    gains = (
        small[:, :at, :shard_rows]
        .transpose(1, 0, 2)
        .reshape(LAYERS, 2, model_width)
        .astype(wide)
    )
    q_biases = (
        small[:, at : at + LAYERS * heads_here, :head_part]
        .transpose(1, 0, 2)
        .reshape(LAYERS, q_width)
        .astype(wide)
    )
    at += LAYERS * heads_here
    kv_biases = small[:, at : at + LAYERS, :bias_part].transpose(1, 0, 2).reshape(LAYERS, 2 * KV, HD)
    kv_biases = jnp.concatenate(
        [
            lax.dynamic_slice_in_dim(kv_biases, kv_head, 1, 1)[:, 0],
            lax.dynamic_slice_in_dim(kv_biases, KV + kv_head, 1, 1)[:, 0],
        ],
        axis=1,
    ).astype(wide)

    own_segments = lax.dynamic_slice_in_dim(segment_ids, local_start, local_len, 1)
    earlier = jnp.sum(
        (segment_ids[:, None, :] < own_segments[:, :, None]).astype(jnp.int32), axis=-1
    )
    token_index = local_start + jnp.arange(local_len, dtype=jnp.int32)
    position = (token_index[None, :] - earlier).astype(wide)
    frequency = ROPE_BASE ** (-jnp.arange(HD // 2, dtype=wide) / (HD // 2))
    angles = position[..., None] * frequency
    cosine = jnp.cos(angles).reshape(row_count, 1, HD // 2)
    sine = jnp.sin(angles).reshape(row_count, 1, HD // 2)
    cos_wide = jnp.concatenate([cosine[:, 0], cosine[:, 0]], axis=1)
    sin_wide = jnp.concatenate([-sine[:, 0], sine[:, 0]], axis=1)
    hidden = hidden_in.astype(wide).reshape(row_count, model_width)
    stored = []
    for layer in range(LAYERS):
        w_attention = attention_weights.reshape(model_width, q_width + 2 * HD + q_width)
        scale_one = lax.rsqrt(jnp.mean(hidden * hidden, axis=-1, keepdims=True) + NORM_EPS)
        normed = (hidden * scale_one * gains[layer, 0]).astype(low)
        work = Work(
            functools.partial(attend, seq_count),
            [
                normed,
                w_attention,
                jnp.concatenate([q_biases[layer], kv_biases[layer]])[None],
                cos_wide,
                sin_wide,
                own_segments.reshape(row_count, 1),
                segment_ids,
            ],
            [
                jax.ShapeDtypeStruct((row_count, q_width), low),
                jax.ShapeDtypeStruct((ctxs, row_count, 2 * HD), low),
                jax.ShapeDtypeStruct((row_count, HD), wide),
                jax.ShapeDtypeStruct((row_count, q_width), low),
            ],
            [],
            ctxs,
            jax.ShapeDtypeStruct((row_count, model_width), low),
        )
        mine = [gate_shards[layer], up_shards[layer]]
        if layer == 0:
            mine.append(down_shards[layer])
        total, *moved, queries, pairs, log_total, mixed_low = move(
            work=work, gathers=mine, plan=((8, 14), (12, 18), (14, 99))
        )
        if layer == 0:
            down_weights = moved.pop()
        w_gate, w_up, w_down = [
            a.reshape(model_width, hidden_units) for a in (*moved, down_weights)
        ]
        middle = hidden + total.astype(wide)
        scale_two = lax.rsqrt(jnp.mean(middle * middle, axis=-1, keepdims=True) + NORM_EPS)
        normed_two = (middle * scale_two * gains[layer, 1]).astype(low)
        gate, up, inner_low, part = forward_ffn(normed_two, w_gate, w_up, w_down)
        stored.append(
            (
                hidden,
                scale_one,
                normed,
                queries,
                pairs,
                log_total,
                mixed_low,
                middle,
                scale_two,
                normed_two,
                gate,
                up,
                inner_low,
                w_attention,
                w_gate,
                w_up,
                w_down,
            )
        )
        if layer + 1 < LAYERS:
            total, attention_weights, down_weights = move(
                z_sums=[part],
                gathers=[attention_shards[layer + 1], down_shards[layer + 1]],
                plan=((8, 15), (13, 18)),
            )
            hidden = middle + total.astype(wide)
        else:
            last_part = part

    def split(gradient):
        return gradient.astype(low).reshape(n, shard_rows, gradient.shape[1])

    grad_hidden = out_grad.astype(wide).reshape(row_count, model_width)
    done = [{} for _ in range(LAYERS)]
    small_grads = [None] * LAYERS
    for layer in reversed(range(LAYERS)):
        (
            layer_input,
            scale_one,
            normed,
            queries,
            pairs,
            log_total,
            mixed_low,
            middle,
            scale_two,
            normed_two,
            gate,
            up,
            inner_low,
            w_attention,
            w_gate,
            w_up,
            w_down,
        ) = stored[layer]
        grad_low = grad_hidden.astype(low)
        *ffn_grads, part = backward_ffn(
            grad_low, normed_two, gate, up, inner_low, w_gate, w_up, w_down
        )
        down_first, down_rest, grad_gate_w, grad_up_w = (split(grad) for grad in ffn_grads)
        total, done[layer]["gate"], done[layer]["down_first"] = move(
            z_sums=[part], scatters=[grad_gate_w, down_first], plan=((2, 9), (3, 11))
        )
        back_two, grad_gain_two = norm_back(middle, scale_two, gains[layer, 1], total.astype(wide))
        grad_middle = grad_hidden + back_two
        grad_mid_low = grad_middle.astype(low)
        work = Work(
            functools.partial(attend_back, seq_count),
            [
                grad_mid_low,
                normed,
                w_attention,
                cos_wide,
                sin_wide,
                own_segments.reshape(1, row_count),
                segment_ids.T,
                queries,
                pairs,
                log_total,
                mixed_low,
            ],
            [jax.ShapeDtypeStruct((row_count, q_width + 2 * HD), low)],
            [
                pltpu.VMEM((row_count, q_width), low),
                pltpu.VMEM((ctxs, row_count, 2 * HD), low),
                pltpu.VMEM((max(1, ctxs - 1), row_count, 2 * HD), low),
            ],
            ctxs,
            jax.ShapeDtypeStruct((row_count, model_width), low),
            [
                jax.ShapeDtypeStruct((n, shard_rows, q_width + 2 * HD), low),
                jax.ShapeDtypeStruct((n, shard_rows, q_width), low),
            ],
        )
        total, *results, grad_lin = move(
            work=work,
            scatters=[grad_up_w, down_rest],
            plan=((-1, 4), (-1, 6), (5, 9), (5, 10)),
        )
        for name, result in zip(("up", "down_rest", "in", "out"), results):
            done[layer][name] = result
        done[layer]["lin"] = grad_lin
        back_one, grad_gain_one = norm_back(
            layer_input, scale_one, gains[layer, 0], total.astype(wide)
        )
        small_grads[layer] = [grad_gain_one, grad_gain_two]
        grad_hidden = grad_middle + back_one

    last_total = lax.psum(after(last_part, grad_hidden), "tensor")
    block_out = (stored[-1][7] + last_total.astype(wide)).astype(low)
    block_out = block_out.reshape(seq_count, local_len, model_width)
    input_grad = grad_hidden.reshape(seq_count, local_len, model_width)

    sums, kv_parts = finish(
        sizes,
        next(numbers),
        [gain for layer in range(LAYERS) for gain in small_grads[layer]],
        [done[layer]["lin"] for layer in range(LAYERS)],
        [done[layer]["in"] for layer in range(LAYERS)],
    )
    shard = lax.axis_index("dp") * ctxs + lax.axis_index("ctx")
    cut = lambda a, size: lax.dynamic_slice_in_dim(a, shard * size, size, a.ndim - 1)
    gains_grad = cut(sums[: 2 * LAYERS], shard_rows).reshape(LAYERS, 2, shard_rows)
    q_rows = sums[2 * LAYERS : 3 * LAYERS, :q_width].reshape(LAYERS, heads_here, HD)
    query_bias_grad = cut(q_rows, head_part)
    kv_bias_grad = cut(sums[3 * LAYERS : 4 * LAYERS, : 2 * KV * HD], bias_part)
    kv_heads = []
    for head in range(KV):
        owners = [t for t in range(tensors) if t * heads_here // (H // KV) == head]
        kv_heads.append(sum(kv_parts[t].astype(wide) for t in owners))
    kv_weight_grad = jnp.concatenate(
        [a[:, :HD] for a in kv_heads] + [a[:, HD:] for a in kv_heads], axis=1
    ).reshape(LAYERS, shard_rows, 2 * KV * HD)

    stack = lambda name, f=lambda a: a: jnp.stack([f(done[layer][name]) for layer in range(LAYERS)])
    down_grad = jnp.concatenate([stack("down_first"), stack("down_rest")], axis=2)
    grads = [
        gains_grad,
        stack("in", lambda a: a[:, :q_width]),
        query_bias_grad,
        kv_weight_grad,
        kv_bias_grad,
        stack("out", lambda a: a.T),
        None,
        down_grad.transpose(0, 2, 1),
    ]
    params = (
        norm_gains,
        query_weight,
        query_bias,
        kv_weight,
        kv_bias,
        out_weight,
        gate_up_weight,
        down_weight,
    )
    firsts, seconds = moments[:8], moments[8:]
    decays = (0.0, 1.0, 0.0, 1.0, 0.0, 1.0, 1.0, 1.0)
    rates = (0.5, 0.02, 0.5, 0.02, 0.5, 0.1, 0.02, 0.02)
    moved = []
    for i in range(8):
        if grads[i] is None:
            pair = [done[layer][name] for layer in range(LAYERS) for name in ("gate", "up")]
            grads[i], *new = pair_adam(params[i], firsts[i], seconds[i], pair, rates[i])
        else:
            new = adam_update(
                params[i].astype(wide), grads[i], firsts[i], seconds[i], decays[i], rates[i]
            )
        moved.append(new)
    return (
        block_out,
        input_grad,
        *grads,
        *[moved[i][0] for i in range(8)],
        *[moved[i][1] for i in range(8)],
        *[moved[i][2] for i in range(8)],
    )


def solution(mesh):
    params = (
        P(None, None, ("dp", "ctx")),
        P(None, ("dp", "ctx"), "tensor"),
        P(None, "tensor", ("dp", "ctx")),
        P(None, ("dp", "ctx"), None),
        P(None, ("dp", "ctx")),
        P(None, "tensor", ("dp", "ctx")),
        P(None, ("dp", "ctx"), None, "tensor"),
        P(None, "tensor", ("dp", "ctx")),
    )
    rows = P("dp", "ctx", None)
    sizes = (mesh.shape["dp"], mesh.shape["ctx"], mesh.shape["tensor"])
    return jax.shard_map(
        functools.partial(local, sizes),
        mesh=mesh,
        in_specs=(rows, P("dp", None), rows, *params, *params, *params),
        out_specs=(rows, rows, *params, *params, *params, *params),
        check_vma=False,
    )
```

```python
import functools

import jax
import jax.numpy as jnp
from jax import lax
from jax.experimental import pallas as pl
from jax.experimental.layout import Layout, with_layout_constraint
from jax.experimental.pallas import tpu as pltpu
from jax.sharding import PartitionSpec as P

H = 12
KV = 2
HD = 128
LAYERS = 2

NORM_EPS = 1e-06
ROPE_BASE = 1000000.0
MASK_FILL = -1e30
beta_first = 0.9
beta_second = 0.95
adam_eps = 1e-08
decay_rate = 0.1
adam_step = 3.0

MESH = pl.DeviceIdType.MESH
ROW_TILE = 16
Z_CHUNKS = 8
NEAR_LEAD, FAR_LAG, NEAR_LAG = 2, 6, 8


class Place:
    def __init__(self, sizes):
        self.dps, self.ctxs, self.tensors = sizes
        self.xs = self.dps // 2
        self.dp = lax.axis_index("dp")
        self.ctx = lax.axis_index("ctx")
        self.tensor = lax.axis_index("tensor")
        self.x = self.dp // 2
        self.core = self.dp % 2

    def x_at(self, step):
        return lax.rem(self.x + step, self.xs)

    def ctx_at(self, step):
        return lax.rem(self.ctx + step, self.ctxs)

    def shard(self, x, core, ctx):
        return (x * 2 + core) * self.ctxs + ctx

    def to_x(self, x):
        return {"dp": x * 2 + self.core}

    def to_ctx(self, ctx):
        return {"ctx": ctx}

    def to_core(self):
        return {"dp": self.x * 2 + 1 - self.core}

    def to_tensor(self, tensor):
        return {"tensor": tensor}

    def plane_partners(self):
        return [
            {"dp": lax.rem(self.dp + step, self.dps), "ctx": self.ctx_at(turn)}
            for step in range(self.dps)
            for turn in range(self.ctxs)
            if step or turn
        ]

    def line_partners(self):
        return [
            self.to_tensor(lax.rem(self.tensor + step, self.tensors))
            for step in range(1, self.tensors)
        ]


class Sems:
    def __init__(self, send, recv):
        self.send, self.recv, self.used = send, recv, 0

    def take(self, count=1):
        first = self.used
        self.used += count
        return first

    def remote(self, src, dst, device, slot=None):
        slot = self.take() if slot is None else slot
        return pltpu.make_async_remote_copy(
            src_ref=src,
            dst_ref=dst,
            send_sem=self.send.at[slot],
            recv_sem=self.recv.at[slot],
            device_id=device,
            device_id_type=MESH,
        )

    def local(self, src, dst):
        return pltpu.make_async_copy(src, dst, self.send.at[self.take()])


def half_rows(rows):
    return min(rows, (rows // 2 + ROW_TILE - 1) // ROW_TILE * ROW_TILE)


def gather_steps(place, sems, shard, whole):
    rows = shard.shape[0]
    cut = half_rows(rows)
    spans = [(0, cut), (cut, rows - cut)]
    xs, ctxs = range(1, place.xs), range(1, place.ctxs)
    me = place.shard(place.x, place.core, place.ctx)
    sent, kept = [], {}

    def part(index, span):
        return whole.at[index, pl.ds(span[0], span[1])]

    def first():
        for step in xs:
            kept["x", step] = sems.remote(shard, whole.at[me], place.to_x(place.x_at(step)))
        for step in ctxs:
            kept["ctx", step] = sems.remote(shard, whole.at[me], place.to_ctx(place.ctx_at(step)))
        kept["core"] = sems.remote(shard, whole.at[me], place.to_core())
        kept["own"] = sems.local(shard, whole.at[me])
        for copy in kept.values():
            copy.start()

    def forward(index, span, device):
        copy = sems.remote(part(index, span), part(index, span), device)
        copy.start()
        sent.append(copy)
        return copy

    def second():
        for step in xs:
            kept["x", step].wait_recv()
            index = place.shard(place.x_at(place.xs - step), place.core, place.ctx)
            for other in ctxs:
                kept["far", step, other, 0] = forward(index, spans[0], place.to_ctx(place.ctx_at(other)))
            forward(index, (0, rows), place.to_core())
        for step in ctxs:
            kept["ctx", step].wait_recv()
            index = place.shard(place.x, place.core, place.ctx_at(place.ctxs - step))
            if spans[1][1] > 0:
                for other in xs:
                    kept["far", other, step, 1] = forward(
                        index, spans[1], place.to_x(place.x_at(other))
                    )
            forward(index, (0, rows), place.to_core())

    def third():
        for step in xs:
            for other in ctxs:
                index = place.shard(
                    place.x_at(place.xs - step), place.core, place.ctx_at(place.ctxs - other)
                )
                kept["far", step, other, 0].wait_recv()
                if spans[1][1] > 0:
                    kept["far", step, other, 1].wait_recv()
                forward(index, (0, rows), place.to_core())

    def last():
        for name, copy in kept.items():
            if name == "own":
                copy.wait()
            elif name[0] in ("x", "ctx"):
                copy.wait_send()
        kept["core"].wait()
        far = [copy for name, copy in kept.items() if name[0] == "far"]
        for copy in sent:
            if any(copy is other for other in far):
                copy.wait_send()
            else:
                copy.wait()

    return [first, second, third, last]


def gather_sems(sizes):
    xs, ctxs = sizes[0] // 2 - 1, sizes[1] - 1
    return 2 + 2 * (xs + ctxs) + 3 * xs * ctxs


def add_rows(rows, body):
    @pl.loop(0, rows // ROW_TILE)
    def _(block):
        body(pl.ds(pl.multiple_of(block * ROW_TILE, ROW_TILE), ROW_TILE))


def scatter_buffers(sizes, shape, dtype):
    n, rows, cols = shape
    xs, ctxs = sizes[0] // 2, sizes[1]
    cut = half_rows(rows)
    far = max(1, (xs - 1) * (ctxs - 1))
    return [
        pltpu.VMEM((xs, ctxs, rows, cols), dtype),
        pltpu.VMEM((xs, ctxs, rows, cols), dtype),
        pltpu.VMEM((far, cut, cols), dtype),
        pltpu.VMEM((far, max(ROW_TILE, rows - cut), cols), dtype),
        pltpu.VMEM((max(1, xs - 1 + ctxs - 1), rows, cols), dtype),
    ]


def scatter_sems(sizes):
    xs, ctxs = sizes[0] // 2 - 1, sizes[1] - 1
    return 2 * (xs + 1) + (xs + ctxs) + 2 * xs * ctxs


def scatter_steps(place, sems, whole, out, mine, other, far_x, far_ctx, near):
    rows = out.shape[0]
    cut = half_rows(rows)
    xs, ctxs = range(1, place.xs), range(1, place.ctxs)
    ahead = lambda step, turn: (step - 1) * len(ctxs) + turn - 1
    loads, swaps, sent = {}, {}, []
    far, close = {}, {}
    wide = lambda ref, *at: ref[at].astype(jnp.float32)

    def first():
        for step in list(xs) + [0]:
            to = place.x_at(step)
            at = place.shard(to, 1 - place.core, 0)
            swaps[step] = sems.remote(
                whole.at[pl.ds(at, place.ctxs)], other.at[step], place.to_core()
            )
            swaps[step].start()
            at = place.shard(to, place.core, 0)
            loads[step] = sems.local(whole.at[pl.ds(at, place.ctxs)], mine.at[step])
            loads[step].start()

    def second():
        for step in xs:
            loads[step].wait()
            swaps[step].wait_recv()
            for turn in ctxs:
                ctx = place.ctx_at(turn)

                def add(span):
                    total = wide(mine, step, ctx, span) + wide(other, step, ctx, span)
                    mine[step, ctx, span] = total.astype(mine.dtype)

                add_rows(rows, add)
                slot = ahead(step, turn)
                far[step, turn, 0] = sems.remote(
                    mine.at[step, ctx, pl.ds(0, cut)], far_x.at[slot], place.to_ctx(ctx)
                )
                far[step, turn, 0].start()
                if rows > cut:
                    far[step, turn, 1] = sems.remote(
                        mine.at[step, ctx, pl.ds(cut, rows - cut)],
                        far_ctx.at[slot],
                        place.to_x(place.x_at(step)),
                    )
                    far[step, turn, 1].start()
        loads[0].wait()
        swaps[0].wait_recv()

    def third():
        for turn in ctxs:
            ctx = place.ctx_at(turn)
            if rows > cut:
                for step in xs:
                    far[step, turn, 1].wait_recv()

            def add_near(span):
                total = wide(mine, 0, ctx, span) + wide(other, 0, ctx, span)
                mine[0, ctx, span] = total.astype(mine.dtype)

            def add_far(block):
                span = pl.ds(pl.multiple_of(cut + block * ROW_TILE, ROW_TILE), ROW_TILE)
                here = pl.ds(pl.multiple_of(block * ROW_TILE, ROW_TILE), ROW_TILE)
                total = wide(mine, 0, ctx, span) + wide(other, 0, ctx, span)
                for step in xs:
                    total = total + wide(far_ctx, ahead(step, turn), here)
                mine[0, ctx, span] = total.astype(mine.dtype)

            add_rows(cut, add_near)
            if rows > cut:
                pl.loop(0, (rows - cut) // ROW_TILE)(add_far)
            slot = len(xs) + turn - 1
            close["ctx", turn] = sems.remote(mine.at[0, ctx], near.at[slot], place.to_ctx(ctx))
            close["ctx", turn].start()
        for step in xs:
            for turn in ctxs:
                far[step, turn, 0].wait_recv()

            def add_cut(span):
                total = wide(mine, step, place.ctx, span) + wide(other, step, place.ctx, span)
                for turn in ctxs:
                    total = total + wide(far_x, ahead(step, turn), span)
                mine[step, place.ctx, span] = total.astype(mine.dtype)

            def add_rest(block):
                span = pl.ds(pl.multiple_of(cut + block * ROW_TILE, ROW_TILE), ROW_TILE)
                total = wide(mine, step, place.ctx, span) + wide(other, step, place.ctx, span)
                mine[step, place.ctx, span] = total.astype(mine.dtype)

            add_rows(cut, add_cut)
            if rows > cut:
                pl.loop(0, (rows - cut) // ROW_TILE)(add_rest)
            close["x", step] = sems.remote(
                mine.at[step, place.ctx], near.at[step - 1], place.to_x(place.x_at(step))
            )
            close["x", step].start()

    def last():
        for copy in close.values():
            copy.wait_recv()

        def add_own(span):
            total = wide(mine, 0, place.ctx, span) + wide(other, 0, place.ctx, span)
            for slot in range(len(xs) + len(ctxs)):
                total = total + wide(near, slot, span)
            out[span] = total.astype(out.dtype)

        add_rows(rows, add_own)
        for copy in (*far.values(), *close.values(), *swaps.values()):
            copy.wait_send()

    return [first, second, third, last]


def line_steps(place, sems, part, out, recv, acc):
    rows = part.shape[0]
    size = rows // (2 * Z_CHUNKS)
    line = place.tensors
    me = place.tensor
    left = me < (line + 1) // 2
    hops = jnp.where(left, me, line - 1 - me)
    ahead = jnp.where(left, 1, -1)
    near = jnp.where(left, 0, 1)
    far = 1 - near
    onward = place.to_tensor(lax.clamp(0, me + ahead, line - 1))
    back = place.to_tensor(lax.clamp(0, me - ahead, line - 1))
    base = sems.take(4 * Z_CHUNKS)
    inner = hops > 0

    def span(flow, chunk):
        return pl.ds(pl.multiple_of((flow * Z_CHUNKS + chunk) * size, size), size)

    def summing(flow, chunk, src, device):
        return sems.remote(
            src.at[span(flow, chunk)],
            recv.at[span(flow, chunk)],
            device,
            base + flow * Z_CHUNKS + chunk,
        )

    def sharing(flow, chunk, device):
        return sems.remote(
            out.at[span(flow, chunk)],
            out.at[span(flow, chunk)],
            device,
            base + (2 + flow) * Z_CHUNKS + chunk,
        )

    def add(flow, chunk, into):
        at = span(flow, chunk)
        total = part[at].astype(jnp.float32) + recv[at].astype(jnp.float32)
        into[at] = total.astype(into.dtype)

    def begin():
        @pl.when(hops == 0)
        def _():
            for chunk in range(Z_CHUNKS):
                summing(near, chunk, part, onward).start()

    def step(turn):
        def run():
            chunk = turn + NEAR_LEAD
            if 0 <= chunk < Z_CHUNKS:

                @pl.when(inner)
                def _():
                    summing(near, chunk, part, onward).wait_recv()
                    add(near, chunk, acc)
                    summing(near, chunk, acc, onward).start()

            chunk = turn
            if 0 <= chunk < Z_CHUNKS:
                summing(far, chunk, acc, back).wait_recv()

                @pl.when(inner)
                def _():
                    add(far, chunk, acc)
                    summing(far, chunk, acc, back).start()

                @pl.when(hops == 0)
                def _():
                    add(far, chunk, out)
                    sharing(far, chunk, onward).start()

            chunk = turn - FAR_LAG
            if 0 <= chunk < Z_CHUNKS:

                @pl.when(inner)
                def _():
                    sharing(far, chunk, onward).wait_recv()
                    sharing(far, chunk, onward).start()

            chunk = turn - NEAR_LAG
            if 0 <= chunk < Z_CHUNKS:
                sharing(near, chunk, back).wait_recv()

                @pl.when(inner)
                def _():
                    sharing(near, chunk, back).start()

        return run

    def end():
        for chunk in range(Z_CHUNKS):
            summing(near, chunk, acc, onward).wait_send()
            sharing(far, chunk, onward).wait_send()

            @pl.when(inner)
            def _():
                summing(far, chunk, acc, back).wait_send()
                sharing(near, chunk, back).wait_send()

    return [begin] + [step(turn) for turn in range(-NEAR_LEAD, Z_CHUNKS + NEAR_LAG)] + [end]


class Work:
    def __init__(
        self, body, inputs, outputs, scratch, sems, part, makes=(), shards=(), whole_plane=False
    ):
        self.body, self.inputs, self.outputs = body, inputs, outputs
        self.scratch, self.sems, self.part, self.makes = scratch, sems, part, makes
        self.shards, self.whole_plane = shards, whole_plane


def take(refs, count):
    taken, refs[:count] = refs[:count], []
    return taken


def greet(place, plane, ctx, line, whole_plane=False, whole_line=False):
    barrier = pltpu.get_barrier_semaphore()
    partners = []
    if whole_plane:
        partners += place.plane_partners()
    else:
        if plane:
            partners.append(place.to_core())
            partners += [place.to_x(place.x_at(step)) for step in range(1, place.xs)]
        if ctx:
            partners += [place.to_ctx(place.ctx_at(step)) for step in range(1, place.ctxs)]
    if whole_line:
        partners += place.line_partners()
    for partner in partners:
        pl.semaphore_signal(barrier, inc=1, device_id=partner, device_id_type=MESH)
    arrived = len(partners)
    if line and not whole_line:
        above = place.tensor < place.tensors - 1
        below = place.tensor > 0

        @pl.when(above)
        def _():
            pl.semaphore_signal(
                barrier, inc=1, device_id=place.to_tensor(place.tensor + 1), device_id_type=MESH
            )

        @pl.when(below)
        def _():
            pl.semaphore_signal(
                barrier, inc=1, device_id=place.to_tensor(place.tensor - 1), device_id_type=MESH
            )

        arrived = arrived + above.astype(jnp.int32) + below.astype(jnp.int32)
    pl.semaphore_wait(barrier, arrived)


def transfer_kernel(sizes, counts, plan, work, *refs):
    z_count, g_count, s_count, p_count = counts
    refs = list(refs)
    given = 0 if work else z_count
    own = len(work.makes) + len(work.shards) if work else 0
    ins = take(refs, sum(counts) - z_count + given - own)
    work_ins = take(refs, len(work.inputs)) if work else []
    outs = take(refs, sum(counts))
    work_outs = take(refs, len(work.outputs)) if work else []
    sem_refs = refs[-2:]
    rest = refs[:-2]
    place = Place(sizes)
    sems = Sems(*sem_refs)
    plane = bool(g_count or s_count)
    whole_plane = bool(work) and work.whole_plane
    greet(place, plane, plane or work, z_count, whole_plane, p_count)

    lines, planes = [], []
    parts = take(rest, 1) if work else take(ins, z_count)
    for part in parts:
        lines.append(line_steps(place, sems, part, outs.pop(0), rest.pop(0), rest.pop(0)))
    shards = take(rest, len(work.shards)) if work else []
    made = take(rest, len(work.makes)) if work else []
    for index in range(g_count):
        shard = shards[index] if index < len(shards) else ins.pop(0)
        planes.append(gather_steps(place, sems, shard, outs.pop(0)))
    for index in range(s_count):
        early = index < s_count - len(made)
        source = ins.pop(0) if early else made[index - s_count]
        planes.append(scatter_steps(place, sems, source, outs.pop(0), *take(rest, 5)))
    late = len(planes) - len(made)
    small = []
    for _ in range(p_count):
        src, dst = ins.pop(0), outs.pop(0)
        small.append(sems.local(src, dst.at[place.tensor]))
        for partner in place.line_partners():
            small.append(sems.remote(src, dst.at[place.tensor], partner))
    for copy in small:
        copy.start()
    body, asked = iter(()), set()
    if work:
        body = work.body(place, sems, work_ins, work_outs, rest, parts[0], *shards, *made)
    for request in body:
        if request is None:
            break
        for which, stage in request:
            asked.add((which, stage))
            planes[which][stage]()
    for which in range(late):
        if (which, 0) not in asked:
            planes[which][0]()
    turns, working = max([len(line) for line in lines], default=0), bool(work)
    for turn in range(turns + 1):
        if turn > 0 and working:
            working = next(body, "done") is None
            if not working:
                for steps in planes[late:]:
                    steps[0]()
        for which, (steps, at) in enumerate(zip(planes, plan)):
            for stage in (1, 2):
                if min(at[stage - 1], turns) == turn and (which, stage) not in asked:
                    steps[stage]()
        for line in lines:
            if turn < len(line):
                line[turn]()
    for steps in planes:
        steps[3]()
    for copy in small:
        copy.wait()


def transfer(
    sizes,
    number,
    z_sums=(),
    gathers=(),
    scatters=(),
    line_pieces=(),
    plan=((99, 99),) * 8,
    work=None,
):
    n = sizes[0] * sizes[1]
    any_space = pl.BlockSpec(memory_space=pl.ANY)
    in_vmem = pl.BlockSpec(memory_space=pltpu.VMEM)
    given = () if work else z_sums
    early, given_shards = len(scatters), gathers
    if work:
        z_sums = (work.part,)
        gathers = (*work.shards, *gathers)
        scatters = (*scatters, *work.makes)
    args = (*given, *given_shards, *scatters[:early], *line_pieces)
    in_specs = [in_vmem] * len(given) + [any_space] * (len(args) - len(given))
    out_specs = (
        [in_vmem] * len(z_sums)
        + [any_space] * len(gathers)
        + [in_vmem] * len(scatters)
        + [any_space] * len(line_pieces)
    )
    out_shape = (
        [jax.ShapeDtypeStruct(a.shape, a.dtype) for a in z_sums]
        + [jax.ShapeDtypeStruct((n, *a.shape), a.dtype) for a in gathers]
        + [jax.ShapeDtypeStruct(a.shape[1:], jnp.float32) for a in scatters]
        + [jax.ShapeDtypeStruct((sizes[2], *a.shape), a.dtype) for a in line_pieces]
    )
    scratch = []
    if work:
        args += tuple(work.inputs)
        in_specs += [in_vmem] * len(work.inputs)
        out_specs += [in_vmem] * len(work.outputs)
        out_shape += work.outputs
        scratch.append(pltpu.VMEM(work.part.shape, work.part.dtype))
    for a in z_sums:
        scratch += [pltpu.VMEM(a.shape, a.dtype)] * 2
    if work:
        scratch += [pltpu.VMEM(a.shape, a.dtype) for a in (*work.shards, *work.makes)]
    for a in scatters:
        scratch += scatter_buffers(sizes, a.shape, a.dtype)
    count = (
        4 * Z_CHUNKS * len(z_sums)
        + gather_sems(sizes) * len(gathers)
        + scatter_sems(sizes) * len(scatters)
        + sizes[2] * len(line_pieces)
    )
    if work:
        scratch += work.scratch
        count += work.sems
    scratch += [pltpu.SemaphoreType.DMA((count,)), pltpu.SemaphoreType.DMA((count,))]
    counts = (len(z_sums), len(gathers), len(scatters), len(line_pieces))
    return pl.pallas_call(
        functools.partial(transfer_kernel, sizes, counts, plan, work),
        out_shape=out_shape,
        in_specs=in_specs,
        out_specs=out_specs,
        scratch_shapes=scratch,
        compiler_params=pltpu.CompilerParams(
            collective_id=number, has_side_effects=True, vmem_limit_bytes=62 << 20
        ),
        cost_estimate=pl.CostEstimate(
            flops=30_000_000_000, bytes_accessed=150_000_000, transcendentals=0
        ),
        name="transfer%d" % number,
    )(*args)


LATE_PIECES = 1


def mm(lhs, rhs, over):
    return lax.dot_general(
        lhs, rhs, (((over[0],), (over[1],)), ((), ())), preferred_element_type=jnp.float32
    )


def turn_heads(values, cosine, sine):
    return values * cosine + pltpu.roll(values, HD // 2, 1) * sine


def allowed_pairs(place, query_segments, key_segments, local_len):
    shape = (local_len, key_segments.shape[1])
    query = place.ctx * local_len + lax.broadcasted_iota(jnp.int32, shape, 0)
    key = lax.broadcasted_iota(jnp.int32, shape, 1)
    return jnp.logical_and(query_segments == key_segments, key <= query)


def sequence_pairs(pairs, sequence, local_len, column):
    block = pairs[:, pl.ds(sequence * local_len, local_len), pl.ds(column * HD, HD)]
    return block.reshape(-1, HD)


def normalize(rows, block, read, gain, write):
    @pl.loop(0, rows // block)
    def _(index):
        span = pl.ds(pl.multiple_of(index * block, block), block)
        values = read(span)
        scale = lax.rsqrt(jnp.mean(values * values, axis=1, keepdims=True) + NORM_EPS)
        write(span, (values * scale * gain).astype(jnp.bfloat16))


def attention_shard(layer, kv_head, query_weight, kv_weight, out_weight, shard):
    q_width = query_weight.shape[2]
    shard[:, pl.ds(0, q_width)] = query_weight[layer]
    for index, head in enumerate((kv_head, KV + kv_head)):
        columns = pl.ds(pl.multiple_of(head * HD, HD), HD)
        shard[:, pl.ds(q_width + index * HD, HD)] = kv_weight[layer, :, columns]
    shard[:, pl.ds(q_width + 2 * HD, q_width)] = out_weight[layer]


def split_pair(layer, weight, gate, up):
    @pl.loop(0, weight.shape[1] // ROW_TILE)
    def _(index):
        span = pl.ds(pl.multiple_of(index * ROW_TILE, ROW_TILE), ROW_TILE)
        both = weight[layer, span, :, :].astype(jnp.float32)
        gate[span, :] = both[:, 0, :].astype(gate.dtype)
        up[span, :] = both[:, 1, :].astype(up.dtype)


def attend(layer, seq_count, place, sems, ins, outs, scratch, part, *shards):
    if layer == 0:
        x_in, own_table, cosine, sine, query_segments, key_segments = ins[:6]
        query_weight, kv_weight, out_weight, gate_up_weight = ins[6:]
        queries, pairs, log_total, mixed, normed, w_attention, table = outs[:7]
        next_shards = outs[7:]
        tables, shard = scratch
        first_head = place.tensor * query_weight.shape[2] // HD // (H // KV)
        attention_shard(0, first_head, query_weight, kv_weight, out_weight, shard)
        here = place.shard(place.x, place.core, place.ctx)
        sent = [
            sems.remote(own_table, tables.at[here], partner) for partner in place.plane_partners()
        ]
        sent.append(sems.local(own_table, tables.at[here]))
        steps = gather_steps(place, sems, shard, w_attention)
        steps[0]()
        for copy in sent:
            copy.start()
        split_pair(0, gate_up_weight, *shards)
        steps[1]()
        yield [(0, 0)]
        for copy in sent:
            copy.wait()
        total = tables[0]
        for index in range(1, tables.shape[0]):
            total = total + tables[index]
        table[...] = total
        read = lambda span: x_in[span, :].astype(jnp.float32)
    else:
        middle, sums, table, w_attention, cosine, sine, query_segments, key_segments = ins
        queries, pairs, log_total, mixed, normed, x_out = outs

        def read(span):
            values = middle[span, :] + sums[span, :].astype(jnp.float32)
            x_out[span, :] = values
            return values

    rows = normed.shape[0]
    local_len = rows // seq_count
    q_width = queries.shape[1]
    heads = q_width // HD
    weight = lambda start, size: w_attention[:, :, pl.ds(start, size)].reshape(-1, size)

    def write(span, values):
        normed[span, :] = values

    normalize(rows, 64, read, table[pl.ds(2 * layer, 1), :], write)
    if layer == 0:
        steps[2]()
        steps[3]()
    cos, sin = cosine[...], sine[...]
    kv_head = place.tensor * heads // (H // KV)
    bias_row = pl.ds(3 * LAYERS + layer, 1)
    bias_at = lambda head: table[bias_row, pl.ds(pl.multiple_of(head * HD, HD), HD)]
    lin = mm(normed[...], weight(q_width, 2 * HD), (1, 0))
    me = place.ctx
    pairs[me, :, :HD] = turn_heads(lin[:, :HD] + bias_at(kv_head), cos, sin).astype(jnp.bfloat16)
    pairs[me, :, HD:] = (lin[:, HD:] + bias_at(KV + kv_head)).astype(jnp.bfloat16)
    sent = [
        sems.remote(pairs.at[me], pairs.at[me], place.to_ctx(place.ctx_at(step)))
        for step in range(1, place.ctxs)
    ]
    for copy in sent:
        copy.start()
    yield [(1, 0), (2, 0)] if layer == 0 else [(0, 0), (1, 0)]
    bias = table[pl.ds(2 * LAYERS + layer, 1), pl.ds(0, q_width)]
    lin = mm(normed[...], weight(0, q_width), (1, 0)) + bias
    for index in range(heads):
        columns = slice(index * HD, (index + 1) * HD)
        queries[:, columns] = turn_heads(lin[:, columns], cos, sin).astype(jnp.bfloat16)
    for copy in sent:
        copy.wait()
    for sequence in range(seq_count):
        span = pl.ds(sequence * local_len, local_len)
        allowed = allowed_pairs(
            place, query_segments[span, :], key_segments[pl.ds(sequence, 1), :], local_len
        )
        keys = sequence_pairs(pairs, sequence, local_len, 0)
        values = sequence_pairs(pairs, sequence, local_len, 1)
        for index in range(heads):
            columns = pl.ds(index * HD, HD)
            scores = mm(queries[span, columns], keys, (1, 1)) * HD ** (-0.5)
            scores = jnp.where(allowed, scores, MASK_FILL)
            row_max = jnp.max(scores, axis=1, keepdims=True)
            exp_scores = jnp.exp(scores - row_max)
            row_total = jnp.sum(exp_scores, axis=1, keepdims=True)
            weights = (exp_scores / row_total).astype(jnp.bfloat16)
            log_total[span, pl.ds(index, 1)] = row_max + jnp.log(row_total)
            mixed[span, columns] = mm(weights, values, (1, 0)).astype(jnp.bfloat16)
    part[...] = mm(mixed[...], weight(q_width + 2 * HD, q_width), (1, 1)).astype(part.dtype)
    yield None
    if layer == 0:
        for other in range(1, LAYERS):
            yield None
            shard, gate, up = next_shards[3 * other - 3 : 3 * other]
            attention_shard(other, first_head, query_weight, kv_weight, out_weight, shard)
            split_pair(other, gate_up_weight, gate, up)


def attend_back(seq_count, place, sems, ins, outs, scratch, part, in_grad, out_grad):
    grad, normed, w_attention, cosine, sine, query_segments, key_segments = ins[:7]
    queries, pairs, log_total, mixed = ins[7:]
    (lin_grad,) = outs
    mixed_grad, pair_grad, got = scratch
    rows = grad.shape[0]
    local_len = rows // seq_count
    q_width = queries.shape[1]
    heads = q_width // HD
    scale = HD ** (-0.5)
    yield [(0, 0), (1, 0)]
    cos, sin = cosine[...], -sine[...]
    weight = lambda start, size: w_attention[:, :, pl.ds(start, size)].reshape(-1, size)
    w_out = weight(q_width + 2 * HD, q_width)
    mixed_grad[...] = mm(grad[...], w_out, (1, 0)).astype(jnp.bfloat16)
    totals = log_total[...].T
    for sequence in range(seq_count):
        first = sequence * local_len
        span = pl.ds(first, local_len)
        keys = sequence_pairs(pairs, sequence, local_len, 0)
        values = sequence_pairs(pairs, sequence, local_len, 1)
        shape = (keys.shape[0], local_len)
        key = lax.broadcasted_iota(jnp.int32, shape, 0)
        query = place.ctx * local_len + lax.broadcasted_iota(jnp.int32, shape, 1)
        same = key_segments[:, pl.ds(sequence, 1)] == query_segments[:, span]
        allowed = jnp.logical_and(same, key <= query)
        key_grad = value_grad = None
        for index in range(heads):
            columns = pl.ds(index * HD, HD)
            query_rows = queries[span, columns]
            grad_rows = mixed_grad[span, columns]
            scores = mm(keys, query_rows, (1, 1)) * scale
            scores = jnp.where(allowed, scores, MASK_FILL)
            weights = jnp.exp(scores - totals[index : index + 1, first : first + local_len])
            weight_grads = mm(values, grad_rows, (1, 1))
            row_delta = jnp.sum(weights * weight_grads, axis=0, keepdims=True)
            score_grads = (weights * (weight_grads - row_delta)).astype(jnp.bfloat16)
            for_keys = mm(score_grads, query_rows, (1, 0))
            for_values = mm(weights.astype(jnp.bfloat16), grad_rows, (1, 0))
            key_grad = for_keys if key_grad is None else key_grad + for_keys
            value_grad = for_values if value_grad is None else value_grad + for_values
            query_grad = mm(score_grads, keys, (0, 0)) * scale
            lin_grad[span, columns] = turn_heads(
                query_grad, cosine[span, :], -sine[span, :]
            ).astype(jnp.bfloat16)
        pieces = (place.ctxs, local_len, HD)
        pair_grad[:, span, :HD] = (key_grad * scale).astype(jnp.bfloat16).reshape(pieces)
        pair_grad[:, span, HD:] = value_grad.astype(jnp.bfloat16).reshape(pieces)
    sent = []
    for step in range(1, place.ctxs):
        to = place.ctx_at(step)
        sent.append(sems.remote(pair_grad.at[to], got.at[step - 1], place.to_ctx(to)))
        sent[-1].start()
    yield [(0, 1), (1, 1)]
    total = pair_grad[place.ctx].astype(jnp.float32)
    for step, copy in enumerate(sent):
        copy.wait()
        total = total + got[step].astype(jnp.float32)
    lin_grad[:, pl.ds(q_width, HD)] = turn_heads(total[:, :HD], cos, sin).astype(jnp.bfloat16)
    lin_grad[:, pl.ds(q_width + HD, HD)] = total[:, HD:].astype(jnp.bfloat16)
    part[...] = mm(lin_grad[...], weight(0, q_width + 2 * HD), (1, 1)).astype(part.dtype)
    yield None
    shard_rows = in_grad.shape[1]
    width = normed.shape[1] // LATE_PIECES
    for piece in range(LATE_PIECES):
        columns = pl.ds(piece * width, width)
        shards = pl.ds(piece * width // shard_rows, width // shard_rows)
        for rows_in, grads_in, made in ((normed, lin_grad, in_grad), (grad, mixed, out_grad)):
            product = mm(rows_in[:, columns], grads_in[...], (0, 0)).astype(made.dtype)
            made[shards] = product.reshape(-1, *made.shape[1:])
            yield None


def finish_kernel(sizes, *refs):
    refs = list(refs)
    gain_grads = take(refs, 2 * LAYERS)
    lin_grads = take(refs, LAYERS)
    (in_grad,) = take(refs, 1)
    sums, kv_parts, kv_rows, rows, send, recv = refs
    place = Place(sizes)
    sems = Sems(send, recv)
    width = in_grad.shape[1]
    q_width = width - 2 * HD
    group = H // KV
    heads = q_width // HD
    dps, ctxs, tensors = sizes
    line, plane = place.line_partners(), place.plane_partners()
    barrier = pltpu.get_barrier_semaphore()
    for device in line + plane:
        pl.semaphore_signal(barrier, inc=1, device_id=device, device_id_type=MESH)

    me = place.tensor
    here = place.dp * ctxs + place.ctx
    kv_rows[me] = jnp.zeros(kv_rows.shape[1:], jnp.float32)
    rows[here] = jnp.zeros(rows.shape[1:], jnp.float32)
    kv_parts[me] = in_grad[:, q_width:].astype(kv_parts.dtype)
    for layer in range(LAYERS):
        bias = jnp.sum(lin_grads[layer][...].astype(jnp.float32), axis=0, keepdims=True)
        kv_rows[me, pl.ds(layer, 1), :] = bias[:, q_width:]
        rows[here, pl.ds(2 * LAYERS + layer, 1), pl.ds(0, q_width)] = bias[:, :q_width]
    for index, gain in enumerate(gain_grads):
        rows[here, pl.ds(index, 1), :] = gain[...]
    pl.semaphore_wait(barrier, len(line) + len(plane))

    big = [sems.remote(kv_parts.at[me], kv_parts.at[me], device) for device in line]
    first = [sems.remote(kv_rows.at[me], kv_rows.at[me], device) for device in line]
    for copy in first + big:
        copy.start()
    for copy in first:
        copy.wait()
    for head in range(KV):
        owners = [t for t in range(tensors) if t * heads // group == head]
        total = sum(kv_rows[t, pl.ds(0, LAYERS), :] for t in owners)
        span = pl.ds(3 * LAYERS, LAYERS)
        rows[here, span, pl.ds(head * HD, HD)] = total[:, :HD]
        rows[here, span, pl.ds((KV + head) * HD, HD)] = total[:, HD:]
    second = [sems.remote(rows.at[here], rows.at[here], device) for device in plane]
    for copy in second:
        copy.start()
    for copy in second:
        copy.wait()
    total = rows[0]
    for index in range(1, dps * ctxs):
        total = total + rows[index]
    sums[...] = total
    for copy in big:
        copy.wait()


def finish(sizes, number, gain_grads, lin_grads, in_grad):
    dps, ctxs, tensors = sizes
    in_vmem = pl.BlockSpec(memory_space=pltpu.VMEM)
    args = (*[gain[None] for gain in gain_grads], *lin_grads, in_grad)
    height, width = -(-4 * LAYERS // 8) * 8, gain_grads[0].shape[0]
    count = 2 * (tensors - 1) + dps * ctxs - 1
    return pl.pallas_call(
        functools.partial(finish_kernel, sizes),
        out_shape=[
            jax.ShapeDtypeStruct((height, width), jnp.float32),
            jax.ShapeDtypeStruct((tensors, in_grad.shape[0], 2 * HD), jnp.bfloat16),
        ],
        in_specs=[in_vmem] * len(args),
        out_specs=[in_vmem] * 2,
        scratch_shapes=[
            pltpu.VMEM((tensors, 8, 2 * HD), jnp.float32),
            pltpu.VMEM((dps * ctxs, height, width), jnp.float32),
            pltpu.SemaphoreType.DMA((count,)),
            pltpu.SemaphoreType.DMA((count,)),
        ],
        compiler_params=pltpu.CompilerParams(
            collective_id=number, has_side_effects=True, vmem_limit_bytes=32 << 20
        ),
        name="finish",
    )(*args)


def adam_update(weight, gradient, first_old, second_old, decayed, step_rate):
    first_new = beta_first * first_old + (1.0 - beta_first) * gradient
    second_new = beta_second * second_old + (1.0 - beta_second) * gradient * gradient
    mean_hat = first_new / (1.0 - beta_first**adam_step)
    square_hat = second_new / (1.0 - beta_second**adam_step)
    new_weight = weight - step_rate * (
        mean_hat / (jnp.sqrt(square_hat) + adam_eps) + decayed * decay_rate * weight
    )
    return (first_new, second_new, new_weight)


def pair_adam_block(step_rate, weight, first, second, *rest):
    grads, outs = rest[: 2 * LAYERS], rest[2 * LAYERS :]
    for layer in range(LAYERS):

        @pl.when(pl.program_id(0) == layer)
        def _():
            gate, up = grads[2 * layer], grads[2 * layer + 1]
            grad = jnp.stack([gate[...], up[...]], axis=1)[None]
            moved = adam_update(
                weight[...].astype(jnp.float32), grad, first[...], second[...], 1.0, step_rate
            )
            for out, value in zip(outs, (grad, *moved)):
                out[...] = value


def pair_adam(weight, first, second, grads, step_rate):
    layers, rows, _, columns = weight.shape
    size = rows // (4 if rows % 64 == 0 else 3)
    last = rows // size - 1
    block = pl.BlockSpec((1, size, 2, columns), lambda layer, i: (layer, i, 0, 0))

    def grad_block(own):
        at = lambda layer, i: (jnp.where(layer == own, i, jnp.where(layer < own, 0, last)), 0)
        return pl.BlockSpec((size, columns), at)

    return pl.pallas_call(
        functools.partial(pair_adam_block, step_rate),
        grid=(layers, rows // size),
        in_specs=[block] * 3 + [grad_block(own) for own in range(layers) for _ in range(2)],
        out_specs=[block] * 4,
        out_shape=[jax.ShapeDtypeStruct(weight.shape, jnp.float32)] * 4,
        compiler_params=pltpu.CompilerParams(vmem_limit_bytes=56 << 20),
        name="pair_adam",
    )(weight, first, second, *grads)


TILE = 256
DOWN_TILES = 4


def in_width(block, width):
    column = pl.program_id(0) * TILE + lax.broadcasted_iota(jnp.int32, block.shape, 1)
    return jnp.where(column < width, block, jnp.zeros_like(block))


def forward_tile(
    width, layer, x_in, sums, table, w_gate, w_up, w_down, middle, n2, gate_out, up_out, inner_out, part_out, total
):
    tile = pl.program_id(0)

    @pl.when(tile == 0)
    def _():
        def read(span):
            values = x_in[span, :].astype(jnp.float32) + sums[span, :].astype(jnp.float32)
            middle[span, :] = values
            return values

        def write(span, values):
            n2[span, :] = values

        normalize(n2.shape[0], 64, read, table[pl.ds(2 * layer + 1, 1), :], write)

    gate = mm(n2[...], w_gate[...], (1, 0))
    up = mm(n2[...], w_up[...], (1, 0))
    gate_out[...] = gate
    up_out[...] = up
    inner = in_width(gate * jax.nn.sigmoid(gate) * up, width).astype(jnp.bfloat16)
    inner_out[...] = inner
    product = mm(inner, in_width(w_down[...], width), (1, 1))

    @pl.when(tile == 0)
    def _():
        total[...] = product

    @pl.when(tile > 0)
    def _():
        total[...] += product

    @pl.when(tile == pl.num_programs(0) - 1)
    def _():
        part_out[...] = total[...].astype(part_out.dtype)


def forward_ffn(layer, x_in, sums, table, w_gate, w_up, w_down):
    rows, model_width = x_in.shape
    width = w_gate.shape[1]
    whole = pl.BlockSpec((rows, model_width), lambda j: (0, 0))
    weight = pl.BlockSpec((model_width, TILE), lambda j: (0, j))
    units = pl.BlockSpec((rows, TILE), lambda j: (0, j))
    return pl.pallas_call(
        functools.partial(forward_tile, width, layer),
        grid=(pl.cdiv(width, TILE),),
        in_specs=[whole, whole, pl.BlockSpec(table.shape, lambda j: (0, 0)), weight, weight, weight],
        out_specs=[whole, whole, units, units, units, whole],
        out_shape=[
            jax.ShapeDtypeStruct((rows, model_width), jnp.float32),
            jax.ShapeDtypeStruct((rows, model_width), jnp.bfloat16),
            jax.ShapeDtypeStruct((rows, width), jnp.float32),
            jax.ShapeDtypeStruct((rows, width), jnp.float32),
            jax.ShapeDtypeStruct((rows, width), jnp.bfloat16),
            jax.ShapeDtypeStruct((rows, model_width), jnp.bfloat16),
        ],
        scratch_shapes=[pltpu.VMEM((rows, model_width), jnp.float32)],
        compiler_params=pltpu.CompilerParams(vmem_limit_bytes=56 << 20),
        name="forward_ffn",
    )(x_in, sums, table, w_gate, w_up, w_down)


def backward_tile(
    width,
    grad,
    n2,
    gate_in,
    up_in,
    inner,
    w_gate,
    w_up,
    w_down,
    down_out,
    down_rest,
    gate_out,
    up_out,
    part_out,
    grad_t,
    n2_t,
    total,
):
    tile = pl.program_id(0)

    @pl.when(tile == 0)
    def _():
        grad_t[...] = grad[...].T
        n2_t[...] = n2[...].T

    gate = gate_in[...]
    slope = jax.nn.sigmoid(gate)
    grad_inner = mm(grad[...], w_down[...], (1, 0))
    down_grad = mm(grad_t[...], inner[...], (1, 0)).astype(down_out.dtype)

    @pl.when(tile < DOWN_TILES)
    def _():
        down_out[...] = down_grad

    @pl.when(tile >= DOWN_TILES)
    def _():
        down_rest[...] = down_grad

    grad_gate = grad_inner * up_in[...] * slope * (1.0 + gate * (1.0 - slope))
    grad_gate = in_width(grad_gate, width).astype(jnp.bfloat16)
    grad_up = in_width(grad_inner * gate * slope, width).astype(jnp.bfloat16)
    product = mm(grad_gate, in_width(w_gate[...], width), (1, 1))
    product += mm(grad_up, in_width(w_up[...], width), (1, 1))

    @pl.when(tile == 0)
    def _():
        total[...] = product

    @pl.when(tile > 0)
    def _():
        total[...] += product

    gate_out[...] = mm(n2_t[...], grad_gate, (1, 0)).astype(gate_out.dtype)
    up_out[...] = mm(n2_t[...], grad_up, (1, 0)).astype(up_out.dtype)

    @pl.when(tile == pl.num_programs(0) - 1)
    def _():
        part_out[...] = total[...].astype(part_out.dtype)


def backward_ffn(grad, n2, gate, up, inner, w_gate, w_up, w_down):
    rows, model_width = n2.shape
    width = w_gate.shape[1]
    whole = pl.BlockSpec((rows, model_width), lambda j: (0, 0))
    weight = pl.BlockSpec((model_width, TILE), lambda j: (0, j))
    units = pl.BlockSpec((rows, TILE), lambda j: (0, j))
    like = lambda size: jax.ShapeDtypeStruct((model_width, size), jnp.bfloat16)
    cut = DOWN_TILES * TILE
    before = pl.BlockSpec((model_width, TILE), lambda j: (0, jnp.minimum(j, DOWN_TILES - 1)))
    behind = pl.BlockSpec((model_width, TILE), lambda j: (0, jnp.maximum(j - DOWN_TILES, 0)))
    return pl.pallas_call(
        functools.partial(backward_tile, width),
        grid=(pl.cdiv(width, TILE),),
        in_specs=[whole, whole, units, units, units, weight, weight, weight],
        out_specs=[before, behind, weight, weight, whole],
        out_shape=[
            like(cut),
            like(width - cut),
            like(width),
            like(width),
            jax.ShapeDtypeStruct((rows, model_width), jnp.bfloat16),
        ],
        scratch_shapes=[
            pltpu.VMEM((model_width, rows), jnp.bfloat16),
            pltpu.VMEM((model_width, rows), jnp.bfloat16),
            pltpu.VMEM((rows, model_width), jnp.float32),
        ],
        compiler_params=pltpu.CompilerParams(vmem_limit_bytes=56 << 20),
        name="backward_ffn",
    )(grad, n2, gate, up, inner, w_gate, w_up, w_down)


def rotate(values, cosine, sine):
    half_width = values.shape[-1] // 2
    first_half = values[..., :half_width]
    second_half = values[..., half_width:]
    return jnp.concatenate(
        [first_half * cosine - second_half * sine, second_half * cosine + first_half * sine],
        axis=-1,
    )


def rotate_back(grad_rows, cosine, sine):
    return rotate(grad_rows, cosine, -sine)


def norm_back(values, gain, grad_rows):
    norm_scale = lax.rsqrt(jnp.mean(values * values, axis=-1, keepdims=True) + NORM_EPS)
    weighted = grad_rows * gain
    inner_mean = jnp.mean(weighted * values, axis=-1, keepdims=True)
    grad_values = (
        norm_scale * weighted - values * (norm_scale * norm_scale * norm_scale) * inner_mean
    )
    return (grad_values, jnp.sum(grad_rows * values * norm_scale, axis=0))


def local(
    sizes,
    hidden_in,
    segment_ids,
    out_grad,
    norm_gains,
    query_weight,
    query_bias,
    kv_weight,
    kv_bias,
    out_weight,
    gate_up_weight,
    down_weight,
    *moments,
):
    low = jnp.bfloat16
    wide = jnp.float32
    dps, ctxs, tensors = sizes
    n = dps * ctxs
    seq_count, local_len, model_width = hidden_in.shape
    seq_length = segment_ids.shape[1]
    row_count = seq_count * local_len
    shard_rows = query_weight.shape[1]
    heads_here = query_weight.shape[2] // HD
    q_width = heads_here * HD
    hidden_units = down_weight.shape[1]
    local_start = lax.axis_index("ctx") * local_len
    kv_head = lax.axis_index("tensor") * heads_here // (H // KV)
    score_scale = HD ** (-0.5)
    numbers = iter(range(1, 100))

    def move(**what):
        return transfer(sizes, next(numbers), **what)

    down_shards = [down_weight[layer].T for layer in range(LAYERS)]

    def after(array, *earlier):
        return lax.optimization_barrier((array, *earlier))[0]

    head_part, bias_part = query_bias.shape[2], kv_bias.shape[1]
    shard = lax.axis_index("dp") * ctxs + lax.axis_index("ctx")

    def placed(part, width):
        zeros = jnp.zeros((*part.shape[:-1], width), wide)
        return lax.dynamic_update_slice_in_dim(
            zeros, part.astype(wide), shard * part.shape[-1], part.ndim - 1
        )

    own_table = jnp.concatenate(
        [
            placed(norm_gains, model_width).reshape(2 * LAYERS, model_width),
            jnp.pad(
                placed(query_bias, HD).reshape(LAYERS, q_width),
                ((0, 0), (0, model_width - q_width)),
            ),
            jnp.pad(
                placed(kv_bias, 2 * KV * HD), ((0, 0), (0, model_width - 2 * KV * HD))
            ),
        ]
    )
    own_table = jnp.pad(own_table, ((0, -own_table.shape[0] % 8), (0, 0)))
    own_segments = lax.dynamic_slice_in_dim(segment_ids, local_start, local_len, 1)
    earlier = jnp.sum(
        (segment_ids[:, None, :] < own_segments[:, :, None]).astype(jnp.int32), axis=-1
    )
    token_index = local_start + jnp.arange(local_len, dtype=jnp.int32)
    position = (token_index[None, :] - earlier).astype(wide)
    frequency = ROPE_BASE ** (-jnp.arange(HD // 2, dtype=wide) / (HD // 2))
    angles = position[..., None] * frequency
    cosine = jnp.cos(angles).reshape(row_count, 1, HD // 2)
    sine = jnp.sin(angles).reshape(row_count, 1, HD // 2)
    cos_wide = jnp.concatenate([cosine[:, 0], cosine[:, 0]], axis=1)
    sin_wide = jnp.concatenate([-sine[:, 0], sine[:, 0]], axis=1)
    hidden = hidden_in.reshape(row_count, model_width)
    stored = []
    for layer in range(LAYERS):
        sides = [cos_wide, sin_wide, own_segments.reshape(row_count, 1), segment_ids]
        outputs = [
            jax.ShapeDtypeStruct((row_count, q_width), low),
            jax.ShapeDtypeStruct((ctxs, row_count, 2 * HD), low),
            jax.ShapeDtypeStruct((row_count, HD), wide),
            jax.ShapeDtypeStruct((row_count, q_width), low),
            jax.ShapeDtypeStruct((row_count, model_width), low),
        ]
        if layer == 0:
            unit_shard = jax.ShapeDtypeStruct((shard_rows, hidden_units), low)
            attention_shard = jax.ShapeDtypeStruct((shard_rows, 2 * q_width + 2 * HD), low)
            outputs.append(jax.ShapeDtypeStruct((n, *attention_shard.shape), low))
            outputs.append(jax.ShapeDtypeStruct(own_table.shape, wide))
            outputs += [attention_shard, unit_shard, unit_shard] * (LAYERS - 1)
            weights = [query_weight, kv_weight, out_weight.transpose(0, 2, 1), gate_up_weight]
            work = Work(
                functools.partial(attend, layer, seq_count),
                [hidden, own_table, *sides, *weights],
                outputs,
                [
                    pltpu.VMEM((n, *own_table.shape), wide),
                    pltpu.VMEM(attention_shard.shape, low),
                ],
                n + gather_sems(sizes) + ctxs,
                jax.ShapeDtypeStruct((row_count, model_width), low),
                shards=[unit_shard, unit_shard],
                whole_plane=True,
            )
            total, *moved = move(
                work=work, gathers=[down_shards[0]], plan=((8, 14), (12, 18), (14, 99))
            )
            w_gate, w_up, down_weights = moved[:3]
            queries, pairs, log_total, mixed_low, normed, w_attention, table = moved[3:10]
            later_shards = moved[10:]
        else:
            outputs.append(jax.ShapeDtypeStruct((row_count, model_width), wide))
            work = Work(
                functools.partial(attend, layer, seq_count),
                [middle, total, table, w_attention, *sides],
                outputs,
                [],
                ctxs,
                jax.ShapeDtypeStruct((row_count, model_width), low),
            )
            total, w_gate, w_up, queries, pairs, log_total, mixed_low, normed, hidden = move(
                work=work,
                gathers=later_shards[3 * layer - 2 : 3 * layer],
                plan=((8, 14), (12, 18)),
            )
        w_gate, w_up, w_down = [
            a.reshape(model_width, hidden_units) for a in (w_gate, w_up, down_weights)
        ]
        middle, normed_two, gate, up, inner_low, part = forward_ffn(
            layer, hidden, total, table, w_gate, w_up, w_down
        )
        stored.append(
            (
                hidden,
                normed,
                queries,
                pairs,
                log_total,
                mixed_low,
                middle,
                normed_two,
                gate,
                up,
                inner_low,
                w_attention,
                w_gate,
                w_up,
                w_down,
            )
        )
        if layer + 1 < LAYERS:
            total, w_attention, down_weights = move(
                z_sums=[part],
                gathers=[later_shards[3 * layer], down_shards[layer + 1]],
                plan=((8, 15), (13, 18)),
            )
        else:
            last_part = part

    def split(gradient):
        return gradient.astype(low).reshape(n, shard_rows, gradient.shape[1])

    grad_hidden = out_grad.astype(wide).reshape(row_count, model_width)
    done = [{} for _ in range(LAYERS)]
    small_grads = [None] * LAYERS
    for layer in reversed(range(LAYERS)):
        (
            layer_input,
            normed,
            queries,
            pairs,
            log_total,
            mixed_low,
            middle,
            normed_two,
            gate,
            up,
            inner_low,
            w_attention,
            w_gate,
            w_up,
            w_down,
        ) = stored[layer]
        grad_low = grad_hidden.astype(low)
        *ffn_grads, part = backward_ffn(
            grad_low, normed_two, gate, up, inner_low, w_gate, w_up, w_down
        )
        down_first, down_rest, grad_gate_w, grad_up_w = (split(grad) for grad in ffn_grads)
        total, done[layer]["gate"], done[layer]["down_first"] = move(
            z_sums=[part], scatters=[grad_gate_w, down_first], plan=((2, 9), (3, 11))
        )
        back_two, grad_gain_two = norm_back(middle, table[2 * layer + 1], total.astype(wide))
        grad_middle = grad_hidden + back_two
        grad_mid_low = grad_middle.astype(low)
        work = Work(
            functools.partial(attend_back, seq_count),
            [
                grad_mid_low,
                normed,
                w_attention,
                cos_wide,
                sin_wide,
                own_segments.reshape(1, row_count),
                segment_ids.T,
                queries,
                pairs,
                log_total,
                mixed_low,
            ],
            [jax.ShapeDtypeStruct((row_count, q_width + 2 * HD), low)],
            [
                pltpu.VMEM((row_count, q_width), low),
                pltpu.VMEM((ctxs, row_count, 2 * HD), low),
                pltpu.VMEM((max(1, ctxs - 1), row_count, 2 * HD), low),
            ],
            ctxs,
            jax.ShapeDtypeStruct((row_count, model_width), low),
            [
                jax.ShapeDtypeStruct((n, shard_rows, q_width + 2 * HD), low),
                jax.ShapeDtypeStruct((n, shard_rows, q_width), low),
            ],
        )
        extra = [kv_part] if layer + 1 < LAYERS else []
        total, *results, grad_lin = move(
            work=work,
            line_pieces=extra,
            scatters=[grad_up_w, down_rest],
            plan=((-1, 4), (-1, 6), (6, 10), (6, 10)),
        )
        for name, result in zip(("up", "down_rest", "in", "out"), results):
            done[layer][name] = result
        done[layer]["lin"] = grad_lin
        kv_part = done[layer]["in"][:, q_width:].astype(low)
        if extra:
            done[layer + 1]["kv"] = results[-1]
        back_one, grad_gain_one = norm_back(
            layer_input.astype(wide), table[2 * layer], total.astype(wide)
        )
        small_grads[layer] = [grad_gain_one, grad_gain_two]
        grad_hidden = grad_middle + back_one
        if layer + 1 == LAYERS:
            half = row_count // 2
            last_totals = [lax.psum(after(last_part[:half], total), "tensor")]

    sums, kv_parts = finish(
        sizes,
        next(numbers),
        [gain for layer in range(LAYERS) for gain in small_grads[layer]],
        [done[layer]["lin"] for layer in range(LAYERS)],
        done[0]["in"],
    )
    done[0]["kv"] = kv_parts
    cut = lambda a, size: lax.dynamic_slice_in_dim(a, shard * size, size, a.ndim - 1)
    last_totals.append(lax.psum(after(last_part[half:], sums), "tensor"))
    last_total = jnp.concatenate([after(last_totals[0], sums), last_totals[1]])
    block_out = (stored[-1][6] + last_total.astype(wide)).astype(low)
    block_out = block_out.reshape(seq_count, local_len, model_width)
    input_grad = grad_hidden.reshape(seq_count, local_len, model_width)

    gains_grad = cut(sums[: 2 * LAYERS], shard_rows).reshape(LAYERS, 2, shard_rows)
    q_rows = sums[2 * LAYERS : 3 * LAYERS, :q_width].reshape(LAYERS, heads_here, HD)
    query_bias_grad = cut(q_rows, head_part)
    kv_bias_grad = cut(sums[3 * LAYERS : 4 * LAYERS, : 2 * KV * HD], bias_part)
    kv_weight_grad = []
    for layer in range(LAYERS):
        heads = []
        for head in range(KV):
            owners = [t for t in range(tensors) if t * heads_here // (H // KV) == head]
            heads.append(sum(done[layer]["kv"][t].astype(wide) for t in owners))
        kv_weight_grad.append(
            jnp.concatenate([a[:, :HD] for a in heads] + [a[:, HD:] for a in heads], axis=1)
        )
    kv_weight_grad = jnp.stack(kv_weight_grad)

    stack = lambda name, f=lambda a: a: jnp.stack([f(done[layer][name]) for layer in range(LAYERS)])
    down_grad = jnp.concatenate([stack("down_first"), stack("down_rest")], axis=2)
    grads = [
        gains_grad,
        stack("in", lambda a: a[:, :q_width]),
        query_bias_grad,
        kv_weight_grad,
        kv_bias_grad,
        stack("out", lambda a: a.T),
        None,
        down_grad.transpose(0, 2, 1),
    ]
    params = (
        norm_gains,
        query_weight,
        query_bias,
        kv_weight,
        kv_bias,
        out_weight,
        gate_up_weight,
        down_weight,
    )
    firsts, seconds = moments[:8], moments[8:]
    decays = (0.0, 1.0, 0.0, 1.0, 0.0, 1.0, 1.0, 1.0)
    rates = (0.5, 0.02, 0.5, 0.02, 0.5, 0.1, 0.02, 0.02)
    moved = []
    for i in range(8):
        if grads[i] is None:
            pair = [done[layer][name] for layer in range(LAYERS) for name in ("gate", "up")]
            grads[i], *new = pair_adam(params[i], firsts[i], seconds[i], pair, rates[i])
        else:
            new = adam_update(
                params[i].astype(wide), grads[i], firsts[i], seconds[i], decays[i], rates[i]
            )
        moved.append(new)
    return (
        block_out,
        input_grad,
        *grads,
        *[moved[i][0] for i in range(8)],
        *[moved[i][1] for i in range(8)],
        *[moved[i][2] for i in range(8)],
    )


def solution(mesh):
    params = (
        P(None, None, ("dp", "ctx")),
        P(None, ("dp", "ctx"), "tensor"),
        P(None, "tensor", ("dp", "ctx")),
        P(None, ("dp", "ctx"), None),
        P(None, ("dp", "ctx")),
        P(None, "tensor", ("dp", "ctx")),
        P(None, ("dp", "ctx"), None, "tensor"),
        P(None, "tensor", ("dp", "ctx")),
    )
    rows = P("dp", "ctx", None)
    sizes = (mesh.shape["dp"], mesh.shape["ctx"], mesh.shape["tensor"])
    return jax.shard_map(
        functools.partial(local, sizes),
        mesh=mesh,
        in_specs=(rows, P("dp", None), rows, *params, *params, *params),
        out_specs=(rows, rows, *params, *params, *params, *params),
        check_vma=False,
    )
```

```python
import functools

import jax
import jax.numpy as jnp
from jax import lax
from jax.experimental import pallas as pl
from jax.experimental.layout import Layout, with_layout_constraint
from jax.experimental.pallas import tpu as pltpu
from jax.sharding import PartitionSpec as P

H = 12
KV = 2
HD = 128
LAYERS = 2

NORM_EPS = 1e-06
ROPE_BASE = 1000000.0
MASK_FILL = -1e30
beta_first = 0.9
beta_second = 0.95
adam_eps = 1e-08
decay_rate = 0.1
adam_step = 3.0

MESH = pl.DeviceIdType.MESH
ROW_TILE = 16
Z_CHUNKS = 8
NEAR_LEAD, FAR_LAG, NEAR_LAG = 2, 6, 8


class Place:
    def __init__(self, sizes):
        self.dps, self.ctxs, self.tensors = sizes
        self.xs = self.dps // 2
        self.dp = lax.axis_index("dp")
        self.ctx = lax.axis_index("ctx")
        self.tensor = lax.axis_index("tensor")
        self.x = self.dp // 2
        self.core = self.dp % 2

    def x_at(self, step):
        return lax.rem(self.x + step, self.xs)

    def ctx_at(self, step):
        return lax.rem(self.ctx + step, self.ctxs)

    def shard(self, x, core, ctx):
        return (x * 2 + core) * self.ctxs + ctx

    def to_x(self, x):
        return {"dp": x * 2 + self.core}

    def to_ctx(self, ctx):
        return {"ctx": ctx}

    def to_core(self):
        return {"dp": self.x * 2 + 1 - self.core}

    def to_tensor(self, tensor):
        return {"tensor": tensor}

    def plane_partners(self):
        return [
            {"dp": lax.rem(self.dp + step, self.dps), "ctx": self.ctx_at(turn)}
            for step in range(self.dps)
            for turn in range(self.ctxs)
            if step or turn
        ]

    def line_partners(self):
        return [
            self.to_tensor(lax.rem(self.tensor + step, self.tensors))
            for step in range(1, self.tensors)
        ]


class Sems:
    def __init__(self, send, recv):
        self.send, self.recv, self.used = send, recv, 0

    def take(self, count=1):
        first = self.used
        self.used += count
        return first

    def remote(self, src, dst, device, slot=None):
        slot = self.take() if slot is None else slot
        return pltpu.make_async_remote_copy(
            src_ref=src,
            dst_ref=dst,
            send_sem=self.send.at[slot],
            recv_sem=self.recv.at[slot],
            device_id=device,
            device_id_type=MESH,
        )

    def local(self, src, dst):
        return pltpu.make_async_copy(src, dst, self.send.at[self.take()])


def half_rows(rows):
    return min(rows, (rows // 2 + ROW_TILE - 1) // ROW_TILE * ROW_TILE)


def gather_steps(place, sems, shard, whole):
    rows = shard.shape[0]
    cut = half_rows(rows)
    spans = [(0, cut), (cut, rows - cut)]
    xs, ctxs = range(1, place.xs), range(1, place.ctxs)
    me = place.shard(place.x, place.core, place.ctx)
    sent, kept = [], {}

    def part(index, span):
        return whole.at[index, pl.ds(span[0], span[1])]

    def first():
        for step in xs:
            kept["x", step] = sems.remote(shard, whole.at[me], place.to_x(place.x_at(step)))
        for step in ctxs:
            kept["ctx", step] = sems.remote(shard, whole.at[me], place.to_ctx(place.ctx_at(step)))
        kept["core"] = sems.remote(shard, whole.at[me], place.to_core())
        kept["own"] = sems.local(shard, whole.at[me])
        for copy in kept.values():
            copy.start()

    def forward(index, span, device):
        copy = sems.remote(part(index, span), part(index, span), device)
        copy.start()
        sent.append(copy)
        return copy

    def second():
        for step in xs:
            kept["x", step].wait_recv()
            index = place.shard(place.x_at(place.xs - step), place.core, place.ctx)
            for other in ctxs:
                kept["far", step, other, 0] = forward(index, spans[0], place.to_ctx(place.ctx_at(other)))
            forward(index, (0, rows), place.to_core())
        for step in ctxs:
            kept["ctx", step].wait_recv()
            index = place.shard(place.x, place.core, place.ctx_at(place.ctxs - step))
            if spans[1][1] > 0:
                for other in xs:
                    kept["far", other, step, 1] = forward(
                        index, spans[1], place.to_x(place.x_at(other))
                    )
            forward(index, (0, rows), place.to_core())

    def third():
        for step in xs:
            for other in ctxs:
                index = place.shard(
                    place.x_at(place.xs - step), place.core, place.ctx_at(place.ctxs - other)
                )
                kept["far", step, other, 0].wait_recv()
                if spans[1][1] > 0:
                    kept["far", step, other, 1].wait_recv()
                forward(index, (0, rows), place.to_core())

    def last():
        for name, copy in kept.items():
            if name == "own":
                copy.wait()
            elif name[0] in ("x", "ctx"):
                copy.wait_send()
        kept["core"].wait()
        far = [copy for name, copy in kept.items() if name[0] == "far"]
        for copy in sent:
            if any(copy is other for other in far):
                copy.wait_send()
            else:
                copy.wait()

    return [first, second, third, last]


def gather_sems(sizes):
    xs, ctxs = sizes[0] // 2 - 1, sizes[1] - 1
    return 2 + 2 * (xs + ctxs) + 3 * xs * ctxs


def add_rows(rows, body):
    @pl.loop(0, rows // ROW_TILE)
    def _(block):
        body(pl.ds(pl.multiple_of(block * ROW_TILE, ROW_TILE), ROW_TILE))


def scatter_buffers(sizes, shape, dtype):
    n, rows, cols = shape
    xs, ctxs = sizes[0] // 2, sizes[1]
    cut = half_rows(rows)
    far = max(1, (xs - 1) * (ctxs - 1))
    return [
        pltpu.VMEM((xs, ctxs, rows, cols), dtype),
        pltpu.VMEM((xs, ctxs, rows, cols), dtype),
        pltpu.VMEM((far, cut, cols), dtype),
        pltpu.VMEM((far, max(ROW_TILE, rows - cut), cols), dtype),
        pltpu.VMEM((max(1, xs - 1 + ctxs - 1), rows, cols), dtype),
    ]


def scatter_sems(sizes):
    xs, ctxs = sizes[0] // 2 - 1, sizes[1] - 1
    return (xs + 1) * (ctxs + 2) + (xs + ctxs) + 2 * xs * ctxs


def scatter_steps(place, sems, whole, out, mine, other, far_x, far_ctx, near):
    rows = out.shape[0]
    cut = half_rows(rows)
    xs, ctxs = range(1, place.xs), range(1, place.ctxs)
    ahead = lambda step, turn: (step - 1) * len(ctxs) + turn - 1
    loads, swaps, sent = {}, {}, []
    far, close = {}, {}
    wide = lambda ref, *at: ref[at].astype(jnp.float32)

    def first():
        order = [(step, turn) for step in xs for turn in ctxs]
        order += [(0, turn) for turn in ctxs] + [(step, 0) for step in xs] + [(0, 0)]
        for step, turn in order:
            ctx = place.ctx_at(turn)
            at = place.shard(place.x_at(step), 1 - place.core, ctx)
            swaps[step, turn] = sems.remote(whole.at[at], other.at[step, ctx], place.to_core())
            swaps[step, turn].start()
        for step in list(xs) + [0]:
            at = place.shard(place.x_at(step), place.core, 0)
            loads[step] = sems.local(whole.at[pl.ds(at, place.ctxs)], mine.at[step])
            loads[step].start()

    def second():
        for step in xs:
            loads[step].wait()
            for turn in ctxs:
                ctx = place.ctx_at(turn)
                swaps[step, turn].wait_recv()

                def add(span):
                    total = wide(mine, step, ctx, span) + wide(other, step, ctx, span)
                    mine[step, ctx, span] = total.astype(mine.dtype)

                add_rows(rows, add)
                slot = ahead(step, turn)
                far[step, turn, 0] = sems.remote(
                    mine.at[step, ctx, pl.ds(0, cut)], far_x.at[slot], place.to_ctx(ctx)
                )
                far[step, turn, 0].start()
                if rows > cut:
                    far[step, turn, 1] = sems.remote(
                        mine.at[step, ctx, pl.ds(cut, rows - cut)],
                        far_ctx.at[slot],
                        place.to_x(place.x_at(step)),
                    )
                    far[step, turn, 1].start()

    def third():
        loads[0].wait()
        for turn in ctxs:
            ctx = place.ctx_at(turn)
            swaps[0, turn].wait_recv()
            if rows > cut:
                for step in xs:
                    far[step, turn, 1].wait_recv()

            def add_near(span):
                total = wide(mine, 0, ctx, span) + wide(other, 0, ctx, span)
                mine[0, ctx, span] = total.astype(mine.dtype)

            def add_far(block):
                span = pl.ds(pl.multiple_of(cut + block * ROW_TILE, ROW_TILE), ROW_TILE)
                here = pl.ds(pl.multiple_of(block * ROW_TILE, ROW_TILE), ROW_TILE)
                total = wide(mine, 0, ctx, span) + wide(other, 0, ctx, span)
                for step in xs:
                    total = total + wide(far_ctx, ahead(step, turn), here)
                mine[0, ctx, span] = total.astype(mine.dtype)

            add_rows(cut, add_near)
            if rows > cut:
                pl.loop(0, (rows - cut) // ROW_TILE)(add_far)
            slot = len(xs) + turn - 1
            close["ctx", turn] = sems.remote(mine.at[0, ctx], near.at[slot], place.to_ctx(ctx))
            close["ctx", turn].start()
        for step in xs:
            swaps[step, 0].wait_recv()
            for turn in ctxs:
                far[step, turn, 0].wait_recv()

            def add_cut(span):
                total = wide(mine, step, place.ctx, span) + wide(other, step, place.ctx, span)
                for turn in ctxs:
                    total = total + wide(far_x, ahead(step, turn), span)
                mine[step, place.ctx, span] = total.astype(mine.dtype)

            def add_rest(block):
                span = pl.ds(pl.multiple_of(cut + block * ROW_TILE, ROW_TILE), ROW_TILE)
                total = wide(mine, step, place.ctx, span) + wide(other, step, place.ctx, span)
                mine[step, place.ctx, span] = total.astype(mine.dtype)

            add_rows(cut, add_cut)
            if rows > cut:
                pl.loop(0, (rows - cut) // ROW_TILE)(add_rest)
            close["x", step] = sems.remote(
                mine.at[step, place.ctx], near.at[step - 1], place.to_x(place.x_at(step))
            )
            close["x", step].start()

    def last():
        swaps[0, 0].wait_recv()
        for copy in close.values():
            copy.wait_recv()

        def add_own(span):
            total = wide(mine, 0, place.ctx, span) + wide(other, 0, place.ctx, span)
            for slot in range(len(xs) + len(ctxs)):
                total = total + wide(near, slot, span)
            out[span] = total.astype(out.dtype)

        add_rows(rows, add_own)
        for copy in (*far.values(), *close.values(), *swaps.values()):
            copy.wait_send()

    return [first, second, third, last]


def line_steps(place, sems, part, out, recv, acc):
    rows = part.shape[0]
    size = rows // (2 * Z_CHUNKS)
    line = place.tensors
    me = place.tensor
    left = me < (line + 1) // 2
    hops = jnp.where(left, me, line - 1 - me)
    ahead = jnp.where(left, 1, -1)
    near = jnp.where(left, 0, 1)
    far = 1 - near
    onward = place.to_tensor(lax.clamp(0, me + ahead, line - 1))
    back = place.to_tensor(lax.clamp(0, me - ahead, line - 1))
    base = sems.take(4 * Z_CHUNKS)
    inner = hops > 0

    def span(flow, chunk):
        return pl.ds(pl.multiple_of((flow * Z_CHUNKS + chunk) * size, size), size)

    def summing(flow, chunk, src, device):
        return sems.remote(
            src.at[span(flow, chunk)],
            recv.at[span(flow, chunk)],
            device,
            base + flow * Z_CHUNKS + chunk,
        )

    def sharing(flow, chunk, device):
        return sems.remote(
            out.at[span(flow, chunk)],
            out.at[span(flow, chunk)],
            device,
            base + (2 + flow) * Z_CHUNKS + chunk,
        )

    def add(flow, chunk, into):
        at = span(flow, chunk)
        total = part[at].astype(jnp.float32) + recv[at].astype(jnp.float32)
        into[at] = total.astype(into.dtype)

    def begin():
        @pl.when(hops == 0)
        def _():
            for chunk in range(Z_CHUNKS):
                summing(near, chunk, part, onward).start()

    def step(turn):
        def run():
            chunk = turn + NEAR_LEAD
            if 0 <= chunk < Z_CHUNKS:

                @pl.when(inner)
                def _():
                    summing(near, chunk, part, onward).wait_recv()
                    add(near, chunk, acc)
                    summing(near, chunk, acc, onward).start()

            chunk = turn
            if 0 <= chunk < Z_CHUNKS:
                summing(far, chunk, acc, back).wait_recv()

                @pl.when(inner)
                def _():
                    add(far, chunk, acc)
                    summing(far, chunk, acc, back).start()

                @pl.when(hops == 0)
                def _():
                    add(far, chunk, out)
                    sharing(far, chunk, onward).start()

            chunk = turn - FAR_LAG
            if 0 <= chunk < Z_CHUNKS:

                @pl.when(inner)
                def _():
                    sharing(far, chunk, onward).wait_recv()
                    sharing(far, chunk, onward).start()

            chunk = turn - NEAR_LAG
            if 0 <= chunk < Z_CHUNKS:
                sharing(near, chunk, back).wait_recv()

                @pl.when(inner)
                def _():
                    sharing(near, chunk, back).start()

        return run

    def end():
        for chunk in range(Z_CHUNKS):
            summing(near, chunk, acc, onward).wait_send()
            sharing(far, chunk, onward).wait_send()

            @pl.when(inner)
            def _():
                summing(far, chunk, acc, back).wait_send()
                sharing(near, chunk, back).wait_send()

    return [begin] + [step(turn) for turn in range(-NEAR_LEAD, Z_CHUNKS + NEAR_LAG)] + [end]


class Work:
    def __init__(
        self, body, inputs, outputs, scratch, sems, part, makes=(), shards=(), whole_plane=False
    ):
        self.body, self.inputs, self.outputs = body, inputs, outputs
        self.scratch, self.sems, self.part, self.makes = scratch, sems, part, makes
        self.shards, self.whole_plane = shards, whole_plane


def take(refs, count):
    taken, refs[:count] = refs[:count], []
    return taken


def greet(place, plane, ctx, line, whole_plane=False, whole_line=False):
    barrier = pltpu.get_barrier_semaphore()
    partners = []
    if whole_plane:
        partners += place.plane_partners()
    else:
        if plane:
            partners.append(place.to_core())
            partners += [place.to_x(place.x_at(step)) for step in range(1, place.xs)]
        if ctx:
            partners += [place.to_ctx(place.ctx_at(step)) for step in range(1, place.ctxs)]
    if whole_line:
        partners += place.line_partners()
    for partner in partners:
        pl.semaphore_signal(barrier, inc=1, device_id=partner, device_id_type=MESH)
    arrived = len(partners)
    if line and not whole_line:
        above = place.tensor < place.tensors - 1
        below = place.tensor > 0

        @pl.when(above)
        def _():
            pl.semaphore_signal(
                barrier, inc=1, device_id=place.to_tensor(place.tensor + 1), device_id_type=MESH
            )

        @pl.when(below)
        def _():
            pl.semaphore_signal(
                barrier, inc=1, device_id=place.to_tensor(place.tensor - 1), device_id_type=MESH
            )

        arrived = arrived + above.astype(jnp.int32) + below.astype(jnp.int32)
    pl.semaphore_wait(barrier, arrived)


def transfer_kernel(sizes, counts, layers, plan, work, *refs):
    z_count, g_count, s_count, p_count = counts
    refs = list(refs)
    given = 0 if work else z_count
    own = len(work.makes) + len(work.shards) if work else 0
    ins = take(refs, sum(counts) - z_count + given - own)
    work_ins = take(refs, len(work.inputs)) if work else []
    outs = take(refs, sum(counts))
    work_outs = take(refs, len(work.outputs)) if work else []
    sem_refs = refs[-2:]
    rest = refs[:-2]
    place = Place(sizes)
    sems = Sems(*sem_refs)
    plane = bool(g_count or s_count)
    whole_plane = bool(work) and work.whole_plane
    greet(place, plane, plane or work, z_count, whole_plane, p_count)

    lines, planes = [], []
    parts = take(rest, 1) if work else take(ins, z_count)
    for part in parts:
        recv = rest.pop(0)
        acc = part if work else rest.pop(0)
        lines.append(line_steps(place, sems, part, outs.pop(0), recv, acc))
    shards = take(rest, len(work.shards)) if work else []
    made = take(rest, len(work.makes)) if work else []
    for index in range(g_count):
        shard = shards[index] if index < len(shards) else ins.pop(0).at[layers[index]]
        planes.append(gather_steps(place, sems, shard, outs.pop(0)))
    for index in range(s_count):
        early = index < s_count - len(made)
        source = ins.pop(0) if early else made[index - s_count]
        planes.append(scatter_steps(place, sems, source, outs.pop(0), *take(rest, 5)))
    late = len(planes) - len(made)
    small = []
    for _ in range(p_count):
        src, dst = ins.pop(0), outs.pop(0)
        small.append(sems.local(src, dst.at[place.tensor]))
        for partner in place.line_partners():
            small.append(sems.remote(src, dst.at[place.tensor], partner))
    for copy in small:
        copy.start()
    body, asked = iter(()), set()
    if work:
        body = work.body(place, sems, work_ins, work_outs, rest, parts[0], *shards, *made)
    for request in body:
        if request is None:
            break
        for which, stage in request:
            asked.add((which, stage))
            planes[which][stage]()
    for which in range(late):
        if (which, 0) not in asked:
            planes[which][0]()
    turns, working = max([len(line) for line in lines], default=0), bool(work)
    for turn in range(turns + 1):
        if turn > 0 and working:
            working = next(body, "done") is None
            if not working:
                for steps in planes[late:]:
                    steps[0]()
        for which, (steps, at) in enumerate(zip(planes, plan)):
            for stage in (1, 2):
                if min(at[stage - 1], turns) == turn and (which, stage) not in asked:
                    steps[stage]()
        for line in lines:
            if turn < len(line):
                line[turn]()
    for steps in planes:
        steps[3]()
    for copy in small:
        copy.wait()


def transfer(
    sizes,
    number,
    z_sums=(),
    gathers=(),
    scatters=(),
    line_pieces=(),
    plan=((99, 99),) * 8,
    work=None,
):
    n = sizes[0] * sizes[1]
    any_space = pl.BlockSpec(memory_space=pl.ANY)
    in_vmem = pl.BlockSpec(memory_space=pltpu.VMEM)
    given = () if work else z_sums
    early, given_shards = len(scatters), [array for array, _ in gathers]
    layers = [layer for _, layer in gathers]
    gathers = [jax.ShapeDtypeStruct(array.shape[1:], array.dtype) for array in given_shards]
    if work:
        z_sums = (work.part,)
        gathers = (*work.shards, *gathers)
        layers = [None] * len(work.shards) + layers
        scatters = (*scatters, *work.makes)
    args = (*given, *given_shards, *scatters[:early], *line_pieces)
    in_specs = [in_vmem] * len(given) + [any_space] * (len(args) - len(given))
    out_specs = (
        [in_vmem] * len(z_sums)
        + [any_space] * len(gathers)
        + [in_vmem] * len(scatters)
        + [any_space] * len(line_pieces)
    )
    out_shape = (
        [jax.ShapeDtypeStruct(a.shape, a.dtype) for a in z_sums]
        + [jax.ShapeDtypeStruct((n, *a.shape), a.dtype) for a in gathers]
        + [jax.ShapeDtypeStruct(a.shape[1:], jnp.float32) for a in scatters]
        + [jax.ShapeDtypeStruct((sizes[2], *a.shape), a.dtype) for a in line_pieces]
    )
    scratch = []
    if work:
        args += tuple(work.inputs)
        in_specs += [in_vmem] * len(work.inputs)
        out_specs += [in_vmem] * len(work.outputs)
        out_shape += work.outputs
        scratch.append(pltpu.VMEM(work.part.shape, work.part.dtype))
    for a in z_sums:
        scratch += [pltpu.VMEM(a.shape, a.dtype)] * (1 if work else 2)
    if work:
        scratch += [pltpu.VMEM(a.shape, a.dtype) for a in (*work.shards, *work.makes)]
    for a in scatters:
        scratch += scatter_buffers(sizes, a.shape, a.dtype)
    count = (
        4 * Z_CHUNKS * len(z_sums)
        + gather_sems(sizes) * len(gathers)
        + scatter_sems(sizes) * len(scatters)
        + sizes[2] * len(line_pieces)
    )
    if work:
        scratch += work.scratch
        count += work.sems
    scratch += [pltpu.SemaphoreType.DMA((count,)), pltpu.SemaphoreType.DMA((count,))]
    counts = (len(z_sums), len(gathers), len(scatters), len(line_pieces))
    return pl.pallas_call(
        functools.partial(transfer_kernel, sizes, counts, layers, plan, work),
        out_shape=out_shape,
        in_specs=in_specs,
        out_specs=out_specs,
        scratch_shapes=scratch,
        compiler_params=pltpu.CompilerParams(
            collective_id=number, has_side_effects=True, vmem_limit_bytes=62 << 20
        ),
        cost_estimate=pl.CostEstimate(
            flops=30_000_000_000, bytes_accessed=150_000_000, transcendentals=0
        ),
        name="transfer%d" % number,
    )(*args)


def mm(lhs, rhs, over):
    return lax.dot_general(
        lhs, rhs, (((over[0],), (over[1],)), ((), ())), preferred_element_type=jnp.float32
    )


def turn_heads(values, cosine, sine):
    return values * cosine + pltpu.roll(values, HD // 2, 1) * sine


def allowed_pairs(place, query_segments, key_segments, local_len):
    shape = (local_len, key_segments.shape[1])
    query = place.ctx * local_len + lax.broadcasted_iota(jnp.int32, shape, 0)
    key = lax.broadcasted_iota(jnp.int32, shape, 1)
    return jnp.logical_and(query_segments == key_segments, key <= query)


def sequence_pairs(pairs, sequence, local_len, column):
    block = pairs[:, pl.ds(sequence * local_len, local_len), pl.ds(column * HD, HD)]
    return block.reshape(-1, HD)


def normalize(rows, block, read, gain, write):
    @pl.loop(0, rows // block)
    def _(index):
        span = pl.ds(pl.multiple_of(index * block, block), block)
        values = read(span)
        scale = lax.rsqrt(jnp.mean(values * values, axis=1, keepdims=True) + NORM_EPS)
        write(span, (values * scale * gain).astype(jnp.bfloat16))


def normalize_back(rows, block, values_in, sums, gain, gain_grad, write):
    gain_grad[...] = jnp.zeros_like(gain_grad)

    @pl.loop(0, rows // block)
    def _(index):
        span = pl.ds(pl.multiple_of(index * block, block), block)
        values = values_in[span, :].astype(jnp.float32)
        grads = sums[span, :].astype(jnp.float32)
        scale = lax.rsqrt(jnp.mean(values * values, axis=1, keepdims=True) + NORM_EPS)
        weighted = grads * gain
        inner_mean = jnp.mean(weighted * values, axis=1, keepdims=True)
        gain_grad[...] += jnp.sum(grads * values * scale, axis=0, keepdims=True)
        write(span, scale * weighted - values * (scale * scale * scale) * inner_mean)


def attention_shard(layer, kv_head, query_weight, kv_weight, out_weight, shard):
    q_width = query_weight.shape[2]
    shard[:, pl.ds(0, q_width)] = query_weight[layer]
    for index, head in enumerate((kv_head, KV + kv_head)):
        columns = pl.ds(pl.multiple_of(head * HD, HD), HD)
        shard[:, pl.ds(q_width + index * HD, HD)] = kv_weight[layer, :, columns]
    shard[:, pl.ds(q_width + 2 * HD, q_width)] = out_weight[layer]


def split_pair(layer, weight, gate, up):
    @pl.loop(0, weight.shape[1] // ROW_TILE)
    def _(index):
        span = pl.ds(pl.multiple_of(index * ROW_TILE, ROW_TILE), ROW_TILE)
        both = weight[layer, span, :, :].astype(jnp.float32)
        gate[span, :] = both[:, 0, :].astype(gate.dtype)
        up[span, :] = both[:, 1, :].astype(up.dtype)


def attend(layer, seq_count, place, sems, ins, outs, scratch, part, *shards):
    if layer == 0:
        x_in, own_table, cosine, sine, query_segments, key_segments = ins[:6]
        query_weight, kv_weight, out_weight, gate_up_weight = ins[6:]
        queries, pairs, log_total, mixed, normed, w_attention, table = outs[:7]
        next_shards = outs[7:]
        tables, shard, totals = scratch
        first_head = place.tensor * query_weight.shape[2] // HD // (H // KV)
        attention_shard(0, first_head, query_weight, kv_weight, out_weight, shard)
        here = place.shard(place.x, place.core, place.ctx)
        sent = [
            sems.remote(own_table, tables.at[here], partner) for partner in place.plane_partners()
        ]
        sent.append(sems.local(own_table, tables.at[here]))
        steps = gather_steps(place, sems, shard, w_attention)
        steps[0]()
        for copy in sent:
            copy.start()
        split_pair(0, gate_up_weight, *shards)
        steps[1]()
        yield [(0, 0)]
        for copy in sent:
            copy.wait()
        total = tables[0]
        for index in range(1, tables.shape[0]):
            total = total + tables[index]
        table[...] = total
        read = lambda span: x_in[span, :].astype(jnp.float32)
    else:
        middle, sums, table, w_attention, cosine, sine, query_segments, key_segments = ins
        (totals,) = scratch
        queries, pairs, log_total, mixed, normed, x_out = outs

        def read(span):
            values = middle[span, :] + sums[span, :].astype(jnp.float32)
            x_out[span, :] = values
            return values

    rows = normed.shape[0]
    local_len = rows // seq_count
    q_width = queries.shape[1]
    heads = q_width // HD
    weight = lambda start, size: w_attention[:, :, pl.ds(start, size)].reshape(-1, size)

    def write(span, values):
        normed[span, :] = values

    normalize(rows, 64, read, table[pl.ds(2 * layer, 1), :], write)
    if layer == 0:
        steps[2]()
        steps[3]()
    cos, sin = cosine[...], sine[...]
    kv_head = place.tensor * heads // (H // KV)
    bias_row = pl.ds(3 * LAYERS + layer, 1)
    bias_at = lambda head: table[bias_row, pl.ds(pl.multiple_of(head * HD, HD), HD)]
    lin = mm(normed[...], weight(q_width, 2 * HD), (1, 0))
    me = place.ctx
    pairs[me, :, :HD] = turn_heads(lin[:, :HD] + bias_at(kv_head), cos, sin).astype(jnp.bfloat16)
    pairs[me, :, HD:] = (lin[:, HD:] + bias_at(KV + kv_head)).astype(jnp.bfloat16)
    sent = [
        sems.remote(pairs.at[me], pairs.at[me], place.to_ctx(place.ctx_at(step)))
        for step in range(1, place.ctxs)
    ]
    for copy in sent:
        copy.start()
    yield [(1, 0), (2, 0)] if layer == 0 else [(0, 0), (1, 0)]
    bias = table[pl.ds(2 * LAYERS + layer, 1), pl.ds(0, q_width)]
    lin = mm(normed[...], weight(0, q_width), (1, 0)) + bias
    for index in range(heads):
        columns = slice(index * HD, (index + 1) * HD)
        queries[:, columns] = turn_heads(lin[:, columns], cos, sin).astype(jnp.bfloat16)
    for copy in sent:
        copy.wait()
    totals[...] = jnp.zeros_like(totals)
    for sequence in range(seq_count):
        span = pl.ds(sequence * local_len, local_len)
        allowed = allowed_pairs(
            place, query_segments[span, :], key_segments[pl.ds(sequence, 1), :], local_len
        )
        keys = sequence_pairs(pairs, sequence, local_len, 0)
        values = sequence_pairs(pairs, sequence, local_len, 1)
        for index in range(heads):
            columns = pl.ds(index * HD, HD)
            scores = mm(queries[span, columns], keys, (1, 1)) * HD ** (-0.5)
            scores = jnp.where(allowed, scores, MASK_FILL)
            row_max = jnp.max(scores, axis=1, keepdims=True)
            exp_scores = jnp.exp(scores - row_max)
            row_total = jnp.sum(exp_scores, axis=1, keepdims=True)
            weights = (exp_scores / row_total).astype(jnp.bfloat16)
            totals[span, pl.ds(index, 1)] = row_max + jnp.log(row_total)
            mixed[span, columns] = mm(weights, values, (1, 0)).astype(jnp.bfloat16)
    part[...] = mm(mixed[...], weight(q_width + 2 * HD, q_width), (1, 1)).astype(part.dtype)
    yield None
    log_total[...] = totals[...].T[: log_total.shape[0], :]
    if layer == 0:
        for other in range(1, LAYERS):
            yield None
            shard, gate, up = next_shards[3 * other - 3 : 3 * other]
            attention_shard(other, first_head, query_weight, kv_weight, out_weight, shard)
            split_pair(other, gate_up_weight, gate, up)


def attend_back(layer, seq_count, place, sems, ins, outs, scratch, part, out_grad, in_grad):
    sums, middle, base, table, normed, w_attention, cosine, sine = ins[:8]
    query_segments, key_segments, queries, pairs, log_total, mixed = ins[8:]
    lin_grad, middle_grad, gain_grad = outs
    mixed_grad, pair_grad, got = scratch
    grad = part
    rows = grad.shape[0]
    local_len = rows // seq_count
    q_width = queries.shape[1]
    heads = q_width // HD
    scale = HD ** (-0.5)
    yield [(0, 0), (1, 0)]

    def write(span, back):
        total = base[span, :].astype(jnp.float32) + back
        middle_grad[span, :] = total
        grad[span, :] = total.astype(grad.dtype)

    gain = table[pl.ds(2 * layer + 1, 1), :]
    normalize_back(rows, 64, middle, sums, gain, gain_grad, write)
    cos, sin = cosine[...], -sine[...]
    weight = lambda start, size: w_attention[:, :, pl.ds(start, size)].reshape(-1, size)
    w_out = weight(q_width + 2 * HD, q_width)
    mixed_grad[...] = mm(grad[...], w_out, (1, 0)).astype(jnp.bfloat16)
    totals = log_total[...]
    for sequence in range(seq_count):
        first = sequence * local_len
        span = pl.ds(first, local_len)
        keys = sequence_pairs(pairs, sequence, local_len, 0)
        values = sequence_pairs(pairs, sequence, local_len, 1)
        shape = (keys.shape[0], local_len)
        key = lax.broadcasted_iota(jnp.int32, shape, 0)
        query = place.ctx * local_len + lax.broadcasted_iota(jnp.int32, shape, 1)
        same = key_segments[:, pl.ds(sequence, 1)] == query_segments[:, span]
        allowed = jnp.logical_and(same, key <= query)
        key_grad = value_grad = None
        for index in range(heads):
            columns = pl.ds(index * HD, HD)
            query_rows = queries[span, columns]
            grad_rows = mixed_grad[span, columns]
            scores = mm(keys, query_rows, (1, 1)) * scale
            scores = jnp.where(allowed, scores, MASK_FILL)
            weights = jnp.exp(scores - totals[index : index + 1, first : first + local_len])
            weight_grads = mm(values, grad_rows, (1, 1))
            row_delta = jnp.sum(weights * weight_grads, axis=0, keepdims=True)
            score_grads = (weights * (weight_grads - row_delta)).astype(jnp.bfloat16)
            for_keys = mm(score_grads, query_rows, (1, 0))
            for_values = mm(weights.astype(jnp.bfloat16), grad_rows, (1, 0))
            key_grad = for_keys if key_grad is None else key_grad + for_keys
            value_grad = for_values if value_grad is None else value_grad + for_values
            query_grad = mm(score_grads, keys, (0, 0)) * scale
            lin_grad[span, columns] = turn_heads(
                query_grad, cosine[span, :], -sine[span, :]
            ).astype(jnp.bfloat16)
        pieces = (place.ctxs, local_len, HD)
        pair_grad[:, span, :HD] = (key_grad * scale).astype(jnp.bfloat16).reshape(pieces)
        pair_grad[:, span, HD:] = value_grad.astype(jnp.bfloat16).reshape(pieces)
    sent = []
    for step in range(1, place.ctxs):
        to = place.ctx_at(step)
        sent.append(sems.remote(pair_grad.at[to], got.at[step - 1], place.to_ctx(to)))
        sent[-1].start()
    yield [(0, 1), (1, 1)]
    product = mm(grad[...], mixed[...], (0, 0)).astype(out_grad.dtype)
    out_grad[...] = product.reshape(out_grad.shape)
    total = pair_grad[place.ctx].astype(jnp.float32)
    for step, copy in enumerate(sent):
        copy.wait()
        total = total + got[step].astype(jnp.float32)
    lin_grad[:, pl.ds(q_width, HD)] = turn_heads(total[:, :HD], cos, sin).astype(jnp.bfloat16)
    lin_grad[:, pl.ds(q_width + HD, HD)] = total[:, HD:].astype(jnp.bfloat16)
    part[...] = mm(lin_grad[...], weight(0, q_width + 2 * HD), (1, 1)).astype(part.dtype)
    yield None
    product = mm(normed[...], lin_grad[...], (0, 0)).astype(in_grad.dtype)
    in_grad[...] = product.reshape(in_grad.shape)


def finish_kernel(sizes, *refs):
    refs = list(refs)
    gain_grads = take(refs, 2 * LAYERS)
    lin_grads = take(refs, LAYERS)
    (in_grad,) = take(refs, 1)
    sums, kv_parts, kv_rows, rows, send, recv = refs
    place = Place(sizes)
    sems = Sems(send, recv)
    width = in_grad.shape[1]
    q_width = width - 2 * HD
    group = H // KV
    heads = q_width // HD
    dps, ctxs, tensors = sizes
    line, plane = place.line_partners(), place.plane_partners()
    barrier = pltpu.get_barrier_semaphore()
    for device in line + plane:
        pl.semaphore_signal(barrier, inc=1, device_id=device, device_id_type=MESH)

    me = place.tensor
    here = place.dp * ctxs + place.ctx
    kv_rows[me] = jnp.zeros(kv_rows.shape[1:], jnp.float32)
    rows[here] = jnp.zeros(rows.shape[1:], jnp.float32)
    kv_parts[me] = in_grad[:, q_width:].astype(kv_parts.dtype)
    for layer in range(LAYERS):
        bias = jnp.sum(lin_grads[layer][...].astype(jnp.float32), axis=0, keepdims=True)
        kv_rows[me, pl.ds(layer, 1), :] = bias[:, q_width:]
        rows[here, pl.ds(2 * LAYERS + layer, 1), pl.ds(0, q_width)] = bias[:, :q_width]
    for index, gain in enumerate(gain_grads):
        rows[here, pl.ds(index, 1), :] = gain[...]
    pl.semaphore_wait(barrier, len(line) + len(plane))

    big = [sems.remote(kv_parts.at[me], kv_parts.at[me], device) for device in line]
    first = [sems.remote(kv_rows.at[me], kv_rows.at[me], device) for device in line]
    for copy in first + big:
        copy.start()
    for copy in first:
        copy.wait()
    for head in range(KV):
        owners = [t for t in range(tensors) if t * heads // group == head]
        total = sum(kv_rows[t, pl.ds(0, LAYERS), :] for t in owners)
        span = pl.ds(3 * LAYERS, LAYERS)
        rows[here, span, pl.ds(head * HD, HD)] = total[:, :HD]
        rows[here, span, pl.ds((KV + head) * HD, HD)] = total[:, HD:]
    second = [sems.remote(rows.at[here], rows.at[here], device) for device in plane]
    for copy in second:
        copy.start()
    for copy in second:
        copy.wait()
    total = rows[0]
    for index in range(1, dps * ctxs):
        total = total + rows[index]
    sums[...] = total
    for copy in big:
        copy.wait()


def finish(sizes, number, gain_grads, lin_grads, in_grad):
    dps, ctxs, tensors = sizes
    in_vmem = pl.BlockSpec(memory_space=pltpu.VMEM)
    args = (*[gain[None] for gain in gain_grads], *lin_grads, in_grad)
    height, width = -(-4 * LAYERS // 8) * 8, gain_grads[0].shape[0]
    count = 2 * (tensors - 1) + dps * ctxs - 1
    return pl.pallas_call(
        functools.partial(finish_kernel, sizes),
        out_shape=[
            jax.ShapeDtypeStruct((height, width), jnp.float32),
            jax.ShapeDtypeStruct((tensors, in_grad.shape[0], 2 * HD), jnp.bfloat16),
        ],
        in_specs=[in_vmem] * len(args),
        out_specs=[in_vmem] * 2,
        scratch_shapes=[
            pltpu.VMEM((tensors, 8, 2 * HD), jnp.float32),
            pltpu.VMEM((dps * ctxs, height, width), jnp.float32),
            pltpu.SemaphoreType.DMA((count,)),
            pltpu.SemaphoreType.DMA((count,)),
        ],
        compiler_params=pltpu.CompilerParams(
            collective_id=number, has_side_effects=True, vmem_limit_bytes=32 << 20
        ),
        name="finish",
    )(*args)


def adam_update(weight, gradient, first_old, second_old, decayed, step_rate):
    first_new = beta_first * first_old + (1.0 - beta_first) * gradient
    second_new = beta_second * second_old + (1.0 - beta_second) * gradient * gradient
    mean_hat = first_new / (1.0 - beta_first**adam_step)
    square_hat = second_new / (1.0 - beta_second**adam_step)
    new_weight = weight - step_rate * (
        mean_hat / (jnp.sqrt(square_hat) + adam_eps) + decayed * decay_rate * weight
    )
    return (first_new, second_new, new_weight)


def pair_adam_block(step_rate, weight, first, second, *rest):
    grads, outs = rest[: 2 * LAYERS], rest[2 * LAYERS :]
    for layer in range(LAYERS):

        @pl.when(pl.program_id(0) == layer)
        def _():
            gate, up = grads[2 * layer], grads[2 * layer + 1]
            grad = jnp.stack([gate[...], up[...]], axis=1)[None]
            moved = adam_update(
                weight[...].astype(jnp.float32), grad, first[...], second[...], 1.0, step_rate
            )
            for out, value in zip(outs, (grad, *moved)):
                out[...] = value


def pair_adam(weight, first, second, grads, step_rate):
    layers, rows, _, columns = weight.shape
    size = rows // (4 if rows % 64 == 0 else 3)
    last = rows // size - 1
    block = pl.BlockSpec((1, size, 2, columns), lambda layer, i: (layer, i, 0, 0))

    def grad_block(own):
        at = lambda layer, i: (jnp.where(layer == own, i, jnp.where(layer < own, 0, last)), 0)
        return pl.BlockSpec((size, columns), at)

    return pl.pallas_call(
        functools.partial(pair_adam_block, step_rate),
        grid=(layers, rows // size),
        in_specs=[block] * 3 + [grad_block(own) for own in range(layers) for _ in range(2)],
        out_specs=[block] * 4,
        out_shape=[jax.ShapeDtypeStruct(weight.shape, jnp.float32)] * 4,
        compiler_params=pltpu.CompilerParams(vmem_limit_bytes=56 << 20),
        name="pair_adam",
    )(weight, first, second, *grads)


TILE = 256
DOWN_TILES = 6


def in_width(block, width):
    column = pl.program_id(0) * TILE + lax.broadcasted_iota(jnp.int32, block.shape, 1)
    return jnp.where(column < width, block, jnp.zeros_like(block))


def forward_tile(
    width, layer, x_in, sums, table, w_gate, w_up, w_down, middle, n2, gate_out, up_out, inner_out, part_out, total
):
    tile = pl.program_id(0)

    @pl.when(tile == 0)
    def _():
        def read(span):
            values = x_in[span, :].astype(jnp.float32) + sums[span, :].astype(jnp.float32)
            middle[span, :] = values
            return values

        def write(span, values):
            n2[span, :] = values

        normalize(n2.shape[0], 64, read, table[pl.ds(2 * layer + 1, 1), :], write)

    gate = mm(n2[...], w_gate[...], (1, 0))
    up = mm(n2[...], w_up[...], (1, 0))
    gate_out[...] = gate
    up_out[...] = up
    inner = in_width(gate * jax.nn.sigmoid(gate) * up, width).astype(jnp.bfloat16)
    inner_out[...] = inner
    product = mm(inner, in_width(w_down[...], width), (1, 1))

    @pl.when(tile == 0)
    def _():
        total[...] = product

    @pl.when(tile > 0)
    def _():
        total[...] += product

    @pl.when(tile == pl.num_programs(0) - 1)
    def _():
        part_out[...] = total[...].astype(part_out.dtype)


def forward_ffn(layer, x_in, sums, table, w_gate, w_up, w_down):
    rows, model_width = x_in.shape
    width = w_gate.shape[1]
    whole = pl.BlockSpec((rows, model_width), lambda j: (0, 0))
    weight = pl.BlockSpec((model_width, TILE), lambda j: (0, j))
    units = pl.BlockSpec((rows, TILE), lambda j: (0, j))
    return pl.pallas_call(
        functools.partial(forward_tile, width, layer),
        grid=(pl.cdiv(width, TILE),),
        in_specs=[whole, whole, pl.BlockSpec(table.shape, lambda j: (0, 0)), weight, weight, weight],
        out_specs=[whole, whole, units, units, units, whole],
        out_shape=[
            jax.ShapeDtypeStruct((rows, model_width), jnp.float32),
            jax.ShapeDtypeStruct((rows, model_width), jnp.bfloat16),
            jax.ShapeDtypeStruct((rows, width), jnp.float32),
            jax.ShapeDtypeStruct((rows, width), jnp.float32),
            jax.ShapeDtypeStruct((rows, width), jnp.bfloat16),
            jax.ShapeDtypeStruct((rows, model_width), jnp.bfloat16),
        ],
        scratch_shapes=[pltpu.VMEM((rows, model_width), jnp.float32)],
        compiler_params=pltpu.CompilerParams(vmem_limit_bytes=56 << 20),
        name="forward_ffn",
    )(x_in, sums, table, w_gate, w_up, w_down)


def backward_tile(width, layer, *refs):
    refs = list(refs)
    if layer is None:
        grad = refs.pop(0)
    else:
        base, values, sums, table = take(refs, 4)
        *refs, grad_out, gain_grad, grad_t, n2_t, total, grad = refs
        refs += [grad_t, n2_t, total]

        @pl.when(pl.program_id(0) == 0)
        def _():
            def write(span, back):
                made = base[span, :] + back
                grad_out[span, :] = made
                grad[span, :] = made.astype(grad.dtype)

            gain = table[pl.ds(2 * layer, 1), :]
            normalize_back(grad.shape[0], 64, values, sums, gain, gain_grad, write)

    backward_work(width, grad, *refs)


def backward_work(
    width,
    grad,
    n2,
    gate_in,
    up_in,
    inner,
    w_gate,
    w_up,
    w_down,
    down_out,
    down_rest,
    gate_out,
    up_out,
    part_out,
    grad_t,
    n2_t,
    total,
):
    tile = pl.program_id(0)

    @pl.when(tile == 0)
    def _():
        grad_t[...] = grad[...].T
        n2_t[...] = n2[...].T

    gate = gate_in[...]
    slope = jax.nn.sigmoid(gate)
    grad_inner = mm(grad[...], w_down[...], (1, 0))
    down_grad = mm(grad_t[...], inner[...], (1, 0)).astype(down_out.dtype)

    @pl.when(tile < DOWN_TILES)
    def _():
        down_out[...] = down_grad

    @pl.when(tile >= DOWN_TILES)
    def _():
        down_rest[...] = down_grad

    grad_gate = grad_inner * up_in[...] * slope * (1.0 + gate * (1.0 - slope))
    grad_gate = in_width(grad_gate, width).astype(jnp.bfloat16)
    grad_up = in_width(grad_inner * gate * slope, width).astype(jnp.bfloat16)
    product = mm(grad_gate, in_width(w_gate[...], width), (1, 1))
    product += mm(grad_up, in_width(w_up[...], width), (1, 1))

    @pl.when(tile == 0)
    def _():
        total[...] = product

    @pl.when(tile > 0)
    def _():
        total[...] += product

    gate_out[...] = mm(n2_t[...], grad_gate, (1, 0)).astype(gate_out.dtype)
    up_out[...] = mm(n2_t[...], grad_up, (1, 0)).astype(up_out.dtype)

    @pl.when(tile == pl.num_programs(0) - 1)
    def _():
        part_out[...] = total[...].astype(part_out.dtype)


def backward_ffn(grad, n2, gate, up, inner, w_gate, w_up, w_down, layer=None):
    rows, model_width = n2.shape
    width = w_gate.shape[1]
    whole = pl.BlockSpec((rows, model_width), lambda j: (0, 0))
    weight = pl.BlockSpec((model_width, TILE), lambda j: (0, j))
    units = pl.BlockSpec((rows, TILE), lambda j: (0, j))
    like = lambda size: jax.ShapeDtypeStruct((model_width, size), jnp.bfloat16)
    cut = DOWN_TILES * TILE
    scratch = [
        pltpu.VMEM((model_width, rows), jnp.bfloat16),
        pltpu.VMEM((model_width, rows), jnp.bfloat16),
        pltpu.VMEM((rows, model_width), jnp.float32),
    ]
    grads, given, made, made_shapes = [grad], [whole], [], []
    if layer is not None:
        grads = grad
        table_block = pl.BlockSpec(grad[3].shape, lambda j: (0, 0))
        given = [whole, whole, whole, table_block]
        made = [whole, pl.BlockSpec((1, model_width), lambda j: (0, 0))]
        made_shapes = [
            jax.ShapeDtypeStruct((rows, model_width), jnp.float32),
            jax.ShapeDtypeStruct((1, model_width), jnp.float32),
        ]
        scratch.append(pltpu.VMEM((rows, model_width), jnp.bfloat16))
    before = pl.BlockSpec((model_width, TILE), lambda j: (0, jnp.minimum(j, DOWN_TILES - 1)))
    behind = pl.BlockSpec((model_width, TILE), lambda j: (0, jnp.maximum(j - DOWN_TILES, 0)))
    return pl.pallas_call(
        functools.partial(backward_tile, width, layer),
        grid=(pl.cdiv(width, TILE),),
        in_specs=given + [whole, units, units, units, weight, weight, weight],
        out_specs=[before, behind, weight, weight, whole] + made,
        out_shape=[
            like(cut),
            like(width - cut),
            like(width),
            like(width),
            jax.ShapeDtypeStruct((rows, model_width), jnp.bfloat16),
        ]
        + made_shapes,
        scratch_shapes=scratch,
        compiler_params=pltpu.CompilerParams(vmem_limit_bytes=56 << 20),
        name="backward_ffn",
    )(*grads, n2, gate, up, inner, w_gate, w_up, w_down)


def rotate(values, cosine, sine):
    half_width = values.shape[-1] // 2
    first_half = values[..., :half_width]
    second_half = values[..., half_width:]
    return jnp.concatenate(
        [first_half * cosine - second_half * sine, second_half * cosine + first_half * sine],
        axis=-1,
    )


def rotate_back(grad_rows, cosine, sine):
    return rotate(grad_rows, cosine, -sine)


def norm_back(values, gain, grad_rows):
    norm_scale = lax.rsqrt(jnp.mean(values * values, axis=-1, keepdims=True) + NORM_EPS)
    weighted = grad_rows * gain
    inner_mean = jnp.mean(weighted * values, axis=-1, keepdims=True)
    grad_values = (
        norm_scale * weighted - values * (norm_scale * norm_scale * norm_scale) * inner_mean
    )
    return (grad_values, jnp.sum(grad_rows * values * norm_scale, axis=0))


def local(
    sizes,
    hidden_in,
    segment_ids,
    out_grad,
    norm_gains,
    query_weight,
    query_bias,
    kv_weight,
    kv_bias,
    out_weight,
    gate_up_weight,
    down_weight,
    *moments,
):
    low = jnp.bfloat16
    wide = jnp.float32
    dps, ctxs, tensors = sizes
    n = dps * ctxs
    seq_count, local_len, model_width = hidden_in.shape
    seq_length = segment_ids.shape[1]
    row_count = seq_count * local_len
    shard_rows = query_weight.shape[1]
    heads_here = query_weight.shape[2] // HD
    q_width = heads_here * HD
    hidden_units = down_weight.shape[1]
    local_start = lax.axis_index("ctx") * local_len
    kv_head = lax.axis_index("tensor") * heads_here // (H // KV)
    score_scale = HD ** (-0.5)
    numbers = iter(range(1, 100))

    def move(**what):
        return transfer(sizes, next(numbers), **what)

    down_shards = down_weight.transpose(0, 2, 1)

    def after(array, *earlier):
        return lax.optimization_barrier((array, *earlier))[0]

    head_part, bias_part = query_bias.shape[2], kv_bias.shape[1]
    shard = lax.axis_index("dp") * ctxs + lax.axis_index("ctx")

    def placed(part, width):
        zeros = jnp.zeros((*part.shape[:-1], width), wide)
        return lax.dynamic_update_slice_in_dim(
            zeros, part.astype(wide), shard * part.shape[-1], part.ndim - 1
        )

    own_table = jnp.concatenate(
        [
            placed(norm_gains, model_width).reshape(2 * LAYERS, model_width),
            jnp.pad(
                placed(query_bias, HD).reshape(LAYERS, q_width),
                ((0, 0), (0, model_width - q_width)),
            ),
            jnp.pad(
                placed(kv_bias, 2 * KV * HD), ((0, 0), (0, model_width - 2 * KV * HD))
            ),
        ]
    )
    own_table = jnp.pad(own_table, ((0, -own_table.shape[0] % 8), (0, 0)))
    own_segments = lax.dynamic_slice_in_dim(segment_ids, local_start, local_len, 1)
    earlier = jnp.sum(
        (segment_ids[:, None, :] < own_segments[:, :, None]).astype(jnp.int32), axis=-1
    )
    token_index = local_start + jnp.arange(local_len, dtype=jnp.int32)
    position = (token_index[None, :] - earlier).astype(wide)
    frequency = ROPE_BASE ** (-jnp.arange(HD // 2, dtype=wide) / (HD // 2))
    angles = position[..., None] * frequency
    cosine = jnp.cos(angles).reshape(row_count, 1, HD // 2)
    sine = jnp.sin(angles).reshape(row_count, 1, HD // 2)
    cos_wide = jnp.concatenate([cosine[:, 0], cosine[:, 0]], axis=1)
    sin_wide = jnp.concatenate([-sine[:, 0], sine[:, 0]], axis=1)
    hidden = hidden_in.reshape(row_count, model_width)
    stored = []
    for layer in range(LAYERS):
        sides = [cos_wide, sin_wide, own_segments.reshape(row_count, 1), segment_ids]
        outputs = [
            jax.ShapeDtypeStruct((row_count, q_width), low),
            jax.ShapeDtypeStruct((ctxs, row_count, 2 * HD), low),
            jax.ShapeDtypeStruct((-(-heads_here // 8) * 8, row_count), wide),
            jax.ShapeDtypeStruct((row_count, q_width), low),
            jax.ShapeDtypeStruct((row_count, model_width), low),
        ]
        if layer == 0:
            unit_shard = jax.ShapeDtypeStruct((shard_rows, hidden_units), low)
            attention_shard = jax.ShapeDtypeStruct((shard_rows, 2 * q_width + 2 * HD), low)
            outputs.append(jax.ShapeDtypeStruct((n, *attention_shard.shape), low))
            outputs.append(jax.ShapeDtypeStruct(own_table.shape, wide))
            outputs += [attention_shard, unit_shard, unit_shard] * (LAYERS - 1)
            weights = [query_weight, kv_weight, out_weight.transpose(0, 2, 1), gate_up_weight]
            work = Work(
                functools.partial(attend, layer, seq_count),
                [hidden, own_table, *sides, *weights],
                outputs,
                [
                    pltpu.VMEM((n, *own_table.shape), wide),
                    pltpu.VMEM(attention_shard.shape, low),
                    pltpu.VMEM((row_count, HD), wide),
                ],
                n + gather_sems(sizes) + ctxs,
                jax.ShapeDtypeStruct((row_count, model_width), low),
                shards=[unit_shard, unit_shard],
                whole_plane=True,
            )
            total, *moved = move(
                work=work, gathers=[(down_shards, 0)], plan=((8, 14), (12, 18), (14, 99))
            )
            w_gate, w_up, down_weights = moved[:3]
            queries, pairs, log_total, mixed_low, normed, w_attention, table = moved[3:10]
            later_shards = moved[10:]
        else:
            outputs.append(jax.ShapeDtypeStruct((row_count, model_width), wide))
            work = Work(
                functools.partial(attend, layer, seq_count),
                [middle, total, table, w_attention, *sides],
                outputs,
                [pltpu.VMEM((row_count, HD), wide)],
                ctxs,
                jax.ShapeDtypeStruct((row_count, model_width), low),
            )
            total, w_gate, w_up, queries, pairs, log_total, mixed_low, normed, hidden = move(
                work=work,
                gathers=[(shard[None], 0) for shard in later_shards[3 * layer - 2 : 3 * layer]],
                plan=((8, 14), (12, 18)),
            )
        w_gate, w_up, w_down = [
            a.reshape(model_width, hidden_units) for a in (w_gate, w_up, down_weights)
        ]
        middle, normed_two, gate, up, inner_low, part = forward_ffn(
            layer, hidden, total, table, w_gate, w_up, w_down
        )
        stored.append(
            (
                hidden,
                normed,
                queries,
                pairs,
                log_total,
                mixed_low,
                middle,
                normed_two,
                gate,
                up,
                inner_low,
                w_attention,
                w_gate,
                w_up,
                w_down,
            )
        )
        if layer + 1 < LAYERS:
            total, w_attention, down_weights = move(
                z_sums=[part],
                gathers=[(later_shards[3 * layer][None], 0), (down_shards, layer + 1)],
                plan=((8, 15), (13, 18)),
            )
        else:
            last_part = part

    def split(gradient):
        return gradient.astype(low).reshape(n, shard_rows, gradient.shape[1])

    grad_hidden = out_grad.reshape(row_count, model_width)
    total = None
    done = [{} for _ in range(LAYERS)]
    small_grads = [None] * LAYERS
    for layer in reversed(range(LAYERS)):
        (
            layer_input,
            normed,
            queries,
            pairs,
            log_total,
            mixed_low,
            middle,
            normed_two,
            gate,
            up,
            inner_low,
            w_attention,
            w_gate,
            w_up,
            w_down,
        ) = stored[layer]
        if layer + 1 == LAYERS:
            *ffn_grads, part = backward_ffn(
                grad_hidden, normed_two, gate, up, inner_low, w_gate, w_up, w_down
            )
        else:
            above = (grad_middle, above_input, total, table)
            *ffn_grads, part, grad_hidden, gain_grad = backward_ffn(
                above, normed_two, gate, up, inner_low, w_gate, w_up, w_down, layer + 1
            )
            small_grads[layer + 1].insert(0, gain_grad[0])
        down_first, down_rest, grad_gate_w, grad_up_w = (split(grad) for grad in ffn_grads)
        total, done[layer]["gate"], done[layer]["down_first"] = move(
            z_sums=[part], scatters=[grad_gate_w, down_first], plan=((2, 9), (3, 11))
        )
        work = Work(
            functools.partial(attend_back, layer, seq_count),
            [
                total,
                middle,
                grad_hidden,
                table,
                normed,
                w_attention,
                cos_wide,
                sin_wide,
                own_segments.reshape(1, row_count),
                segment_ids.T,
                queries,
                pairs,
                log_total,
                mixed_low,
            ],
            [
                jax.ShapeDtypeStruct((row_count, q_width + 2 * HD), low),
                jax.ShapeDtypeStruct((row_count, model_width), wide),
                jax.ShapeDtypeStruct((1, model_width), wide),
            ],
            [
                pltpu.VMEM((row_count, q_width), low),
                pltpu.VMEM((ctxs, row_count, 2 * HD), low),
                pltpu.VMEM((max(1, ctxs - 1), row_count, 2 * HD), low),
            ],
            ctxs,
            jax.ShapeDtypeStruct((row_count, model_width), low),
            [
                jax.ShapeDtypeStruct((n, shard_rows, q_width), low),
                jax.ShapeDtypeStruct((n, shard_rows, q_width + 2 * HD), low),
            ],
        )
        extra = [kv_part] if layer + 1 < LAYERS else []
        total, *results, grad_lin, grad_middle, gain_grad = move(
            work=work,
            line_pieces=extra,
            scatters=[grad_up_w, down_rest],
            plan=((-1, 2), (-1, 4), (3, 13), (3, 13)),
        )
        for name, result in zip(("up", "down_rest", "out", "in"), results):
            done[layer][name] = result
        done[layer]["lin"] = grad_lin
        kv_part = done[layer]["in"][:, q_width:].astype(low)
        if extra:
            done[layer + 1]["kv"] = results[-1]
        small_grads[layer] = [gain_grad[0]]
        above_input = layer_input
        if layer + 1 == LAYERS:
            last_total = lax.psum(after(last_part, total), "tensor")

    back_one, grad_gain_one = norm_back(above_input.astype(wide), table[0], total.astype(wide))
    small_grads[0].insert(0, grad_gain_one)
    grad_hidden = grad_middle + back_one
    sums, kv_parts = finish(
        sizes,
        next(numbers),
        [gain for layer in range(LAYERS) for gain in small_grads[layer]],
        [done[layer]["lin"] for layer in range(LAYERS)],
        done[0]["in"],
    )
    done[0]["kv"] = kv_parts
    cut = lambda a, size: lax.dynamic_slice_in_dim(a, shard * size, size, a.ndim - 1)
    last_total = after(last_total, sums)
    block_out = (stored[-1][6] + last_total.astype(wide)).astype(low)
    block_out = block_out.reshape(seq_count, local_len, model_width)
    input_grad = grad_hidden.reshape(seq_count, local_len, model_width)

    gains_grad = cut(sums[: 2 * LAYERS], shard_rows).reshape(LAYERS, 2, shard_rows)
    q_rows = sums[2 * LAYERS : 3 * LAYERS, :q_width].reshape(LAYERS, heads_here, HD)
    query_bias_grad = cut(q_rows, head_part)
    kv_bias_grad = cut(sums[3 * LAYERS : 4 * LAYERS, : 2 * KV * HD], bias_part)
    kv_weight_grad = []
    for layer in range(LAYERS):
        heads = []
        for head in range(KV):
            owners = [t for t in range(tensors) if t * heads_here // (H // KV) == head]
            heads.append(sum(done[layer]["kv"][t].astype(wide) for t in owners))
        kv_weight_grad.append(
            jnp.concatenate([a[:, :HD] for a in heads] + [a[:, HD:] for a in heads], axis=1)
        )
    kv_weight_grad = jnp.stack(kv_weight_grad)

    stack = lambda name, f=lambda a: a: jnp.stack([f(done[layer][name]) for layer in range(LAYERS)])
    down_grad = jnp.concatenate([stack("down_first"), stack("down_rest")], axis=2)
    grads = [
        gains_grad,
        stack("in", lambda a: a[:, :q_width]),
        query_bias_grad,
        kv_weight_grad,
        kv_bias_grad,
        stack("out", lambda a: a.T),
        None,
        down_grad.transpose(0, 2, 1),
    ]
    params = (
        norm_gains,
        query_weight,
        query_bias,
        kv_weight,
        kv_bias,
        out_weight,
        gate_up_weight,
        down_weight,
    )
    firsts, seconds = moments[:8], moments[8:]
    decays = (0.0, 1.0, 0.0, 1.0, 0.0, 1.0, 1.0, 1.0)
    rates = (0.5, 0.02, 0.5, 0.02, 0.5, 0.1, 0.02, 0.02)
    moved = []
    for i in range(8):
        if grads[i] is None:
            pair = [done[layer][name] for layer in range(LAYERS) for name in ("gate", "up")]
            grads[i], *new = pair_adam(params[i], firsts[i], seconds[i], pair, rates[i])
        else:
            new = adam_update(
                params[i].astype(wide), grads[i], firsts[i], seconds[i], decays[i], rates[i]
            )
        moved.append(new)
    return (
        block_out,
        input_grad,
        *grads,
        *[moved[i][0] for i in range(8)],
        *[moved[i][1] for i in range(8)],
        *[moved[i][2] for i in range(8)],
    )


def solution(mesh):
    params = (
        P(None, None, ("dp", "ctx")),
        P(None, ("dp", "ctx"), "tensor"),
        P(None, "tensor", ("dp", "ctx")),
        P(None, ("dp", "ctx"), None),
        P(None, ("dp", "ctx")),
        P(None, "tensor", ("dp", "ctx")),
        P(None, ("dp", "ctx"), None, "tensor"),
        P(None, "tensor", ("dp", "ctx")),
    )
    rows = P("dp", "ctx", None)
    sizes = (mesh.shape["dp"], mesh.shape["ctx"], mesh.shape["tensor"])
    return jax.shard_map(
        functools.partial(local, sizes),
        mesh=mesh,
        in_specs=(rows, P("dp", None), rows, *params, *params, *params),
        out_specs=(rows, rows, *params, *params, *params, *params),
        check_vma=False,
    )
```

```python
import functools

import jax
import jax.numpy as jnp
from jax import lax
from jax.experimental import pallas as pl
from jax.experimental.layout import Layout, with_layout_constraint
from jax.experimental.pallas import tpu as pltpu
from jax.sharding import PartitionSpec as P

H = 12
KV = 2
HD = 128
LAYERS = 2

NORM_EPS = 1e-06
ROPE_BASE = 1000000.0
MASK_FILL = -1e30
beta_first = 0.9
beta_second = 0.95
adam_eps = 1e-08
decay_rate = 0.1
adam_step = 3.0

MESH = pl.DeviceIdType.MESH
ROW_TILE = 16
Z_CHUNKS = 8
NEAR_LEAD, FAR_LAG, NEAR_LAG = 2, 6, 8


class Place:
    def __init__(self, sizes):
        self.dps, self.ctxs, self.tensors = sizes
        self.xs = self.dps // 2
        self.dp = lax.axis_index("dp")
        self.ctx = lax.axis_index("ctx")
        self.tensor = lax.axis_index("tensor")
        self.x = self.dp // 2
        self.core = self.dp % 2

    def x_at(self, step):
        return lax.rem(self.x + step, self.xs)

    def ctx_at(self, step):
        return lax.rem(self.ctx + step, self.ctxs)

    def shard(self, x, core, ctx):
        return (x * 2 + core) * self.ctxs + ctx

    def to_x(self, x):
        return {"dp": x * 2 + self.core}

    def to_ctx(self, ctx):
        return {"ctx": ctx}

    def to_core(self):
        return {"dp": self.x * 2 + 1 - self.core}

    def to_tensor(self, tensor):
        return {"tensor": tensor}

    def plane_partners(self):
        return [
            {"dp": lax.rem(self.dp + step, self.dps), "ctx": self.ctx_at(turn)}
            for step in range(self.dps)
            for turn in range(self.ctxs)
            if step or turn
        ]

    def line_partners(self):
        return [
            self.to_tensor(lax.rem(self.tensor + step, self.tensors))
            for step in range(1, self.tensors)
        ]


class Sems:
    def __init__(self, send, recv):
        self.send, self.recv, self.used = send, recv, 0

    def take(self, count=1):
        first = self.used
        self.used += count
        return first

    def remote(self, src, dst, device, slot=None):
        slot = self.take() if slot is None else slot
        return pltpu.make_async_remote_copy(
            src_ref=src,
            dst_ref=dst,
            send_sem=self.send.at[slot],
            recv_sem=self.recv.at[slot],
            device_id=device,
            device_id_type=MESH,
        )

    def local(self, src, dst):
        return pltpu.make_async_copy(src, dst, self.send.at[self.take()])


def half_rows(rows):
    return min(rows, (rows // 2 + ROW_TILE - 1) // ROW_TILE * ROW_TILE)


def gather_steps(place, sems, shard, whole):
    rows = shard.shape[0]
    cut = half_rows(rows)
    spans = [(0, cut), (cut, rows - cut)]
    xs, ctxs = range(1, place.xs), range(1, place.ctxs)
    me = place.shard(place.x, place.core, place.ctx)
    sent, kept = [], {}

    def part(index, span):
        return whole.at[index, pl.ds(span[0], span[1])]

    def first():
        for step in xs:
            kept["x", step] = sems.remote(shard, whole.at[me], place.to_x(place.x_at(step)))
        for step in ctxs:
            kept["ctx", step] = sems.remote(shard, whole.at[me], place.to_ctx(place.ctx_at(step)))
        kept["core"] = sems.remote(shard, whole.at[me], place.to_core())
        kept["own"] = sems.local(shard, whole.at[me])
        for copy in kept.values():
            copy.start()

    def forward(index, span, device):
        copy = sems.remote(part(index, span), part(index, span), device)
        copy.start()
        sent.append(copy)
        return copy

    def second():
        for step in xs:
            kept["x", step].wait_recv()
            index = place.shard(place.x_at(place.xs - step), place.core, place.ctx)
            for other in ctxs:
                kept["far", step, other, 0] = forward(index, spans[0], place.to_ctx(place.ctx_at(other)))
            forward(index, (0, rows), place.to_core())
        for step in ctxs:
            kept["ctx", step].wait_recv()
            index = place.shard(place.x, place.core, place.ctx_at(place.ctxs - step))
            if spans[1][1] > 0:
                for other in xs:
                    kept["far", other, step, 1] = forward(
                        index, spans[1], place.to_x(place.x_at(other))
                    )
            forward(index, (0, rows), place.to_core())

    def third():
        for step in xs:
            for other in ctxs:
                index = place.shard(
                    place.x_at(place.xs - step), place.core, place.ctx_at(place.ctxs - other)
                )
                kept["far", step, other, 0].wait_recv()
                if spans[1][1] > 0:
                    kept["far", step, other, 1].wait_recv()
                forward(index, (0, rows), place.to_core())

    def last():
        for name, copy in kept.items():
            if name == "own":
                copy.wait()
            elif name[0] in ("x", "ctx"):
                copy.wait_send()
        kept["core"].wait()
        far = [copy for name, copy in kept.items() if name[0] == "far"]
        for copy in sent:
            if any(copy is other for other in far):
                copy.wait_send()
            else:
                copy.wait()

    return [first, second, third, last]


def gather_sems(sizes):
    xs, ctxs = sizes[0] // 2 - 1, sizes[1] - 1
    return 2 + 2 * (xs + ctxs) + 3 * xs * ctxs


def add_rows(rows, body):
    @pl.loop(0, rows // ROW_TILE)
    def _(block):
        body(pl.ds(pl.multiple_of(block * ROW_TILE, ROW_TILE), ROW_TILE))


def scatter_buffers(sizes, shape, dtype):
    n, rows, cols = shape
    xs, ctxs = sizes[0] // 2, sizes[1]
    cut = half_rows(rows)
    far = max(1, (xs - 1) * (ctxs - 1))
    return [
        pltpu.VMEM((xs, ctxs, rows, cols), dtype),
        pltpu.VMEM((xs, ctxs, rows, cols), dtype),
        pltpu.VMEM((far, cut, cols), dtype),
        pltpu.VMEM((far, max(ROW_TILE, rows - cut), cols), dtype),
        pltpu.VMEM((max(1, xs - 1 + ctxs - 1), rows, cols), dtype),
    ]


def scatter_sems(sizes):
    xs, ctxs = sizes[0] // 2 - 1, sizes[1] - 1
    return (xs + 1) * (ctxs + 2) + (xs + ctxs) + 2 * xs * ctxs


def scatter_steps(place, sems, whole, out, mine, other, far_x, far_ctx, near):
    rows = out.shape[0]
    cut = half_rows(rows)
    xs, ctxs = range(1, place.xs), range(1, place.ctxs)
    ahead = lambda step, turn: (step - 1) * len(ctxs) + turn - 1
    loads, swaps, sent = {}, {}, []
    far, close = {}, {}
    wide = lambda ref, *at: ref[at].astype(jnp.float32)

    def first():
        order = [(step, turn) for step in xs for turn in ctxs]
        order += [(0, turn) for turn in ctxs] + [(step, 0) for step in xs] + [(0, 0)]
        for step, turn in order:
            ctx = place.ctx_at(turn)
            at = place.shard(place.x_at(step), 1 - place.core, ctx)
            swaps[step, turn] = sems.remote(whole.at[at], other.at[step, ctx], place.to_core())
            swaps[step, turn].start()
        for step in list(xs) + [0]:
            at = place.shard(place.x_at(step), place.core, 0)
            loads[step] = sems.local(whole.at[pl.ds(at, place.ctxs)], mine.at[step])
            loads[step].start()

    def second():
        for step in xs:
            loads[step].wait()
            for turn in ctxs:
                ctx = place.ctx_at(turn)
                swaps[step, turn].wait_recv()

                def add(span):
                    total = wide(mine, step, ctx, span) + wide(other, step, ctx, span)
                    mine[step, ctx, span] = total.astype(mine.dtype)

                add_rows(rows, add)
                slot = ahead(step, turn)
                far[step, turn, 0] = sems.remote(
                    mine.at[step, ctx, pl.ds(0, cut)], far_x.at[slot], place.to_ctx(ctx)
                )
                far[step, turn, 0].start()
                if rows > cut:
                    far[step, turn, 1] = sems.remote(
                        mine.at[step, ctx, pl.ds(cut, rows - cut)],
                        far_ctx.at[slot],
                        place.to_x(place.x_at(step)),
                    )
                    far[step, turn, 1].start()

    def third():
        loads[0].wait()
        for turn in ctxs:
            ctx = place.ctx_at(turn)
            swaps[0, turn].wait_recv()
            if rows > cut:
                for step in xs:
                    far[step, turn, 1].wait_recv()

            def add_near(span):
                total = wide(mine, 0, ctx, span) + wide(other, 0, ctx, span)
                mine[0, ctx, span] = total.astype(mine.dtype)

            def add_far(block):
                span = pl.ds(pl.multiple_of(cut + block * ROW_TILE, ROW_TILE), ROW_TILE)
                here = pl.ds(pl.multiple_of(block * ROW_TILE, ROW_TILE), ROW_TILE)
                total = wide(mine, 0, ctx, span) + wide(other, 0, ctx, span)
                for step in xs:
                    total = total + wide(far_ctx, ahead(step, turn), here)
                mine[0, ctx, span] = total.astype(mine.dtype)

            add_rows(cut, add_near)
            if rows > cut:
                pl.loop(0, (rows - cut) // ROW_TILE)(add_far)
            slot = len(xs) + turn - 1
            close["ctx", turn] = sems.remote(mine.at[0, ctx], near.at[slot], place.to_ctx(ctx))
            close["ctx", turn].start()
        for step in xs:
            swaps[step, 0].wait_recv()
            for turn in ctxs:
                far[step, turn, 0].wait_recv()

            def add_cut(span):
                total = wide(mine, step, place.ctx, span) + wide(other, step, place.ctx, span)
                for turn in ctxs:
                    total = total + wide(far_x, ahead(step, turn), span)
                mine[step, place.ctx, span] = total.astype(mine.dtype)

            def add_rest(block):
                span = pl.ds(pl.multiple_of(cut + block * ROW_TILE, ROW_TILE), ROW_TILE)
                total = wide(mine, step, place.ctx, span) + wide(other, step, place.ctx, span)
                mine[step, place.ctx, span] = total.astype(mine.dtype)

            add_rows(cut, add_cut)
            if rows > cut:
                pl.loop(0, (rows - cut) // ROW_TILE)(add_rest)
            close["x", step] = sems.remote(
                mine.at[step, place.ctx], near.at[step - 1], place.to_x(place.x_at(step))
            )
            close["x", step].start()

    def last():
        swaps[0, 0].wait_recv()
        for copy in close.values():
            copy.wait_recv()

        def add_own(span):
            total = wide(mine, 0, place.ctx, span) + wide(other, 0, place.ctx, span)
            for slot in range(len(xs) + len(ctxs)):
                total = total + wide(near, slot, span)
            out[span] = total.astype(out.dtype)

        add_rows(rows, add_own)
        for copy in (*far.values(), *close.values(), *swaps.values()):
            copy.wait_send()

    return [first, second, third, last]


def line_steps(place, sems, part, out, recv, acc):
    rows = part.shape[0]
    size = rows // (2 * Z_CHUNKS)
    line = place.tensors
    me = place.tensor
    left = me < (line + 1) // 2
    hops = jnp.where(left, me, line - 1 - me)
    ahead = jnp.where(left, 1, -1)
    near = jnp.where(left, 0, 1)
    far = 1 - near
    onward = place.to_tensor(lax.clamp(0, me + ahead, line - 1))
    back = place.to_tensor(lax.clamp(0, me - ahead, line - 1))
    base = sems.take(4 * Z_CHUNKS)
    inner = hops > 0

    def span(flow, chunk):
        return pl.ds(pl.multiple_of((flow * Z_CHUNKS + chunk) * size, size), size)

    def summing(flow, chunk, src, device):
        return sems.remote(
            src.at[span(flow, chunk)],
            recv.at[span(flow, chunk)],
            device,
            base + flow * Z_CHUNKS + chunk,
        )

    def sharing(flow, chunk, device):
        return sems.remote(
            out.at[span(flow, chunk)],
            out.at[span(flow, chunk)],
            device,
            base + (2 + flow) * Z_CHUNKS + chunk,
        )

    def add(flow, chunk, into):
        at = span(flow, chunk)
        total = part[at].astype(jnp.float32) + recv[at].astype(jnp.float32)
        into[at] = total.astype(into.dtype)

    def begin():
        @pl.when(hops == 0)
        def _():
            for chunk in range(Z_CHUNKS):
                summing(near, chunk, part, onward).start()

    def step(turn):
        def run():
            chunk = turn + NEAR_LEAD
            if 0 <= chunk < Z_CHUNKS:

                @pl.when(inner)
                def _():
                    summing(near, chunk, part, onward).wait_recv()
                    add(near, chunk, acc)
                    summing(near, chunk, acc, onward).start()

            chunk = turn
            if 0 <= chunk < Z_CHUNKS:
                summing(far, chunk, acc, back).wait_recv()

                @pl.when(inner)
                def _():
                    add(far, chunk, acc)
                    summing(far, chunk, acc, back).start()

                @pl.when(hops == 0)
                def _():
                    add(far, chunk, out)
                    sharing(far, chunk, onward).start()

            chunk = turn - FAR_LAG
            if 0 <= chunk < Z_CHUNKS:

                @pl.when(inner)
                def _():
                    sharing(far, chunk, onward).wait_recv()
                    sharing(far, chunk, onward).start()

            chunk = turn - NEAR_LAG
            if 0 <= chunk < Z_CHUNKS:
                sharing(near, chunk, back).wait_recv()

                @pl.when(inner)
                def _():
                    sharing(near, chunk, back).start()

        return run

    def end():
        for chunk in range(Z_CHUNKS):
            summing(near, chunk, acc, onward).wait_send()
            sharing(far, chunk, onward).wait_send()

            @pl.when(inner)
            def _():
                summing(far, chunk, acc, back).wait_send()
                sharing(near, chunk, back).wait_send()

    return [begin] + [step(turn) for turn in range(-NEAR_LEAD, Z_CHUNKS + NEAR_LAG)] + [end]


class Work:
    def __init__(
        self, body, inputs, outputs, scratch, sems, part, makes=(), shards=(), whole_plane=False
    ):
        self.body, self.inputs, self.outputs = body, inputs, outputs
        self.scratch, self.sems, self.part, self.makes = scratch, sems, part, makes
        self.shards, self.whole_plane = shards, whole_plane


def take(refs, count):
    taken, refs[:count] = refs[:count], []
    return taken


def greet(place, plane, ctx, line, whole_plane=False, whole_line=False):
    barrier = pltpu.get_barrier_semaphore()
    partners = []
    if whole_plane:
        partners += place.plane_partners()
    else:
        if plane:
            partners.append(place.to_core())
            partners += [place.to_x(place.x_at(step)) for step in range(1, place.xs)]
        if ctx:
            partners += [place.to_ctx(place.ctx_at(step)) for step in range(1, place.ctxs)]
    if whole_line:
        partners += place.line_partners()
    for partner in partners:
        pl.semaphore_signal(barrier, inc=1, device_id=partner, device_id_type=MESH)
    arrived = len(partners)
    if line and not whole_line:
        above = place.tensor < place.tensors - 1
        below = place.tensor > 0

        @pl.when(above)
        def _():
            pl.semaphore_signal(
                barrier, inc=1, device_id=place.to_tensor(place.tensor + 1), device_id_type=MESH
            )

        @pl.when(below)
        def _():
            pl.semaphore_signal(
                barrier, inc=1, device_id=place.to_tensor(place.tensor - 1), device_id_type=MESH
            )

        arrived = arrived + above.astype(jnp.int32) + below.astype(jnp.int32)
    pl.semaphore_wait(barrier, arrived)


def transfer_kernel(sizes, counts, layers, plan, work, *refs):
    z_count, g_count, s_count, p_count = counts
    refs = list(refs)
    given = 0 if work else z_count
    own = len(work.makes) + len(work.shards) if work else 0
    ins = take(refs, sum(counts) - z_count + given - own)
    work_ins = take(refs, len(work.inputs)) if work else []
    outs = take(refs, sum(counts))
    work_outs = take(refs, len(work.outputs)) if work else []
    sem_refs = refs[-2:]
    rest = refs[:-2]
    place = Place(sizes)
    sems = Sems(*sem_refs)
    plane = bool(g_count or s_count)
    whole_plane = bool(work) and work.whole_plane
    greet(place, plane, plane or work, z_count, whole_plane, p_count)

    lines, planes = [], []
    parts = take(rest, 1) if work else take(ins, z_count)
    for part in parts:
        recv = rest.pop(0)
        acc = part if work else rest.pop(0)
        lines.append(line_steps(place, sems, part, outs.pop(0), recv, acc))
    shards = take(rest, len(work.shards)) if work else []
    made = take(rest, len(work.makes)) if work else []
    for index in range(g_count):
        shard = shards[index] if index < len(shards) else ins.pop(0).at[layers[index]]
        planes.append(gather_steps(place, sems, shard, outs.pop(0)))
    for index in range(s_count):
        early = index < s_count - len(made)
        source = ins.pop(0) if early else made[index - s_count]
        planes.append(scatter_steps(place, sems, source, outs.pop(0), *take(rest, 5)))
    late = len(planes) - len(made)
    small = []
    for _ in range(p_count):
        src, dst = ins.pop(0), outs.pop(0)
        small.append(sems.local(src, dst.at[place.tensor]))
        for partner in place.line_partners():
            small.append(sems.remote(src, dst.at[place.tensor], partner))
    for copy in small:
        copy.start()
    body, asked = iter(()), set()
    if work:
        body = work.body(place, sems, work_ins, work_outs, rest, parts[0], *shards, *made)
    for request in body:
        if request is None:
            break
        for which, stage in request:
            asked.add((which, stage))
            planes[which][stage]()
    for which in range(late):
        if (which, 0) not in asked:
            planes[which][0]()
    turns, working = max([len(line) for line in lines], default=0), bool(work)
    for turn in range(turns + 1):
        if turn > 0 and working:
            working = next(body, "done") is None
            if not working:
                for steps in planes[late:]:
                    steps[0]()
        for which, (steps, at) in enumerate(zip(planes, plan)):
            for stage in (1, 2):
                if min(at[stage - 1], turns) == turn and (which, stage) not in asked:
                    steps[stage]()
        for line in lines:
            if turn < len(line):
                line[turn]()
    for steps in planes:
        steps[3]()
    for copy in small:
        copy.wait()


def transfer(
    sizes,
    number,
    z_sums=(),
    gathers=(),
    scatters=(),
    line_pieces=(),
    plan=((99, 99),) * 8,
    work=None,
):
    n = sizes[0] * sizes[1]
    any_space = pl.BlockSpec(memory_space=pl.ANY)
    in_vmem = pl.BlockSpec(memory_space=pltpu.VMEM)
    given = () if work else z_sums
    early, given_shards = len(scatters), [array for array, _ in gathers]
    layers = [layer for _, layer in gathers]
    gathers = [jax.ShapeDtypeStruct(array.shape[1:], array.dtype) for array in given_shards]
    if work:
        z_sums = (work.part,)
        gathers = (*work.shards, *gathers)
        layers = [None] * len(work.shards) + layers
        scatters = (*scatters, *work.makes)
    args = (*given, *given_shards, *scatters[:early], *line_pieces)
    in_specs = [in_vmem] * len(given) + [any_space] * (len(args) - len(given))
    out_specs = (
        [in_vmem] * len(z_sums)
        + [any_space] * len(gathers)
        + [in_vmem] * len(scatters)
        + [any_space] * len(line_pieces)
    )
    out_shape = (
        [jax.ShapeDtypeStruct(a.shape, a.dtype) for a in z_sums]
        + [jax.ShapeDtypeStruct((n, *a.shape), a.dtype) for a in gathers]
        + [jax.ShapeDtypeStruct(a.shape[1:], jnp.float32) for a in scatters]
        + [jax.ShapeDtypeStruct((sizes[2], *a.shape), a.dtype) for a in line_pieces]
    )
    scratch = []
    if work:
        args += tuple(work.inputs)
        in_specs += [in_vmem] * len(work.inputs)
        out_specs += [in_vmem] * len(work.outputs)
        out_shape += work.outputs
        scratch.append(pltpu.VMEM(work.part.shape, work.part.dtype))
    for a in z_sums:
        scratch += [pltpu.VMEM(a.shape, a.dtype)] * (1 if work else 2)
    if work:
        scratch += [pltpu.VMEM(a.shape, a.dtype) for a in (*work.shards, *work.makes)]
    for a in scatters:
        scratch += scatter_buffers(sizes, a.shape, a.dtype)
    count = (
        4 * Z_CHUNKS * len(z_sums)
        + gather_sems(sizes) * len(gathers)
        + scatter_sems(sizes) * len(scatters)
        + sizes[2] * len(line_pieces)
    )
    if work:
        scratch += work.scratch
        count += work.sems
    scratch += [pltpu.SemaphoreType.DMA((count,)), pltpu.SemaphoreType.DMA((count,))]
    counts = (len(z_sums), len(gathers), len(scatters), len(line_pieces))
    return pl.pallas_call(
        functools.partial(transfer_kernel, sizes, counts, layers, plan, work),
        out_shape=out_shape,
        in_specs=in_specs,
        out_specs=out_specs,
        scratch_shapes=scratch,
        compiler_params=pltpu.CompilerParams(
            collective_id=number, has_side_effects=True, vmem_limit_bytes=62 << 20
        ),
        cost_estimate=pl.CostEstimate(
            flops=30_000_000_000, bytes_accessed=150_000_000, transcendentals=0
        ),
        name="transfer%d" % number,
    )(*args)


def mm(lhs, rhs, over):
    return lax.dot_general(
        lhs, rhs, (((over[0],), (over[1],)), ((), ())), preferred_element_type=jnp.float32
    )


def turn_heads(values, cosine, sine):
    return values * cosine + pltpu.roll(values, HD // 2, 1) * sine


def allowed_pairs(place, query_segments, key_segments, local_len):
    shape = (local_len, key_segments.shape[1])
    query = place.ctx * local_len + lax.broadcasted_iota(jnp.int32, shape, 0)
    key = lax.broadcasted_iota(jnp.int32, shape, 1)
    return jnp.logical_and(query_segments == key_segments, key <= query)


def sequence_pairs(pairs, sequence, local_len, column):
    block = pairs[:, pl.ds(sequence * local_len, local_len), pl.ds(column * HD, HD)]
    return block.reshape(-1, HD)


def normalize(rows, block, read, gain, write):
    @pl.loop(0, rows // block)
    def _(index):
        span = pl.ds(pl.multiple_of(index * block, block), block)
        values = read(span)
        scale = lax.rsqrt(jnp.mean(values * values, axis=1, keepdims=True) + NORM_EPS)
        write(span, (values * scale * gain).astype(jnp.bfloat16))


def normalize_back(rows, block, values_in, sums, gain, gain_grad, write):
    gain_grad[...] = jnp.zeros_like(gain_grad)

    @pl.loop(0, rows // block)
    def _(index):
        span = pl.ds(pl.multiple_of(index * block, block), block)
        values = values_in[span, :].astype(jnp.float32)
        grads = sums[span, :].astype(jnp.float32)
        scale = lax.rsqrt(jnp.mean(values * values, axis=1, keepdims=True) + NORM_EPS)
        weighted = grads * gain
        inner_mean = jnp.mean(weighted * values, axis=1, keepdims=True)
        gain_grad[...] += jnp.sum(grads * values * scale, axis=0, keepdims=True)
        write(span, scale * weighted - values * (scale * scale * scale) * inner_mean)


def attention_shard(layer, kv_head, query_weight, kv_weight, out_weight, shard):
    q_width = query_weight.shape[2]
    shard[:, pl.ds(0, q_width)] = query_weight[layer]
    for index, head in enumerate((kv_head, KV + kv_head)):
        columns = pl.ds(pl.multiple_of(head * HD, HD), HD)
        shard[:, pl.ds(q_width + index * HD, HD)] = kv_weight[layer, :, columns]
    shard[:, pl.ds(q_width + 2 * HD, q_width)] = out_weight[layer]


def split_pair(layer, weight, gate, up):
    @pl.loop(0, weight.shape[1] // ROW_TILE)
    def _(index):
        span = pl.ds(pl.multiple_of(index * ROW_TILE, ROW_TILE), ROW_TILE)
        both = weight[layer, span, :, :].astype(jnp.float32)
        gate[span, :] = both[:, 0, :].astype(gate.dtype)
        up[span, :] = both[:, 1, :].astype(up.dtype)


def attend(layer, seq_count, place, sems, ins, outs, scratch, part, *shards):
    if layer == 0:
        x_in, own_table, cosine, sine, query_segments, key_segments = ins[:6]
        query_weight, kv_weight, out_weight, gate_up_weight = ins[6:]
        queries, pairs, log_total, mixed, normed, w_attention, table = outs[:7]
        next_shards = outs[7:]
        tables, shard, totals = scratch
        first_head = place.tensor * query_weight.shape[2] // HD // (H // KV)
        attention_shard(0, first_head, query_weight, kv_weight, out_weight, shard)
        here = place.shard(place.x, place.core, place.ctx)
        sent = [
            sems.remote(own_table, tables.at[here], partner) for partner in place.plane_partners()
        ]
        sent.append(sems.local(own_table, tables.at[here]))
        steps = gather_steps(place, sems, shard, w_attention)
        steps[0]()
        for copy in sent:
            copy.start()
        split_pair(0, gate_up_weight, *shards)
        steps[1]()
        yield [(0, 0)]
        for copy in sent:
            copy.wait()
        total = tables[0]
        for index in range(1, tables.shape[0]):
            total = total + tables[index]
        table[...] = total
        read = lambda span: x_in[span, :].astype(jnp.float32)
    else:
        middle, sums, table, w_attention, cosine, sine, query_segments, key_segments = ins
        (totals,) = scratch
        queries, pairs, log_total, mixed, normed, x_out = outs

        def read(span):
            values = middle[span, :] + sums[span, :].astype(jnp.float32)
            x_out[span, :] = values
            return values

    rows = normed.shape[0]
    local_len = rows // seq_count
    q_width = queries.shape[1]
    heads = q_width // HD
    weight = lambda start, size: w_attention[:, :, pl.ds(start, size)].reshape(-1, size)

    def write(span, values):
        normed[span, :] = values

    normalize(rows, 64, read, table[pl.ds(2 * layer, 1), :], write)
    if layer == 0:
        steps[2]()
        steps[3]()
    cos, sin = cosine[...], sine[...]
    kv_head = place.tensor * heads // (H // KV)
    bias_row = pl.ds(3 * LAYERS + layer, 1)
    bias_at = lambda head: table[bias_row, pl.ds(pl.multiple_of(head * HD, HD), HD)]
    lin = mm(normed[...], weight(q_width, 2 * HD), (1, 0))
    me = place.ctx
    pairs[me, :, :HD] = turn_heads(lin[:, :HD] + bias_at(kv_head), cos, sin).astype(jnp.bfloat16)
    pairs[me, :, HD:] = (lin[:, HD:] + bias_at(KV + kv_head)).astype(jnp.bfloat16)
    sent = [
        sems.remote(pairs.at[me], pairs.at[me], place.to_ctx(place.ctx_at(step)))
        for step in range(1, place.ctxs)
    ]
    for copy in sent:
        copy.start()
    yield [(1, 0), (2, 0)] if layer == 0 else [(0, 0), (1, 0)]
    bias = table[pl.ds(2 * LAYERS + layer, 1), pl.ds(0, q_width)]
    lin = mm(normed[...], weight(0, q_width), (1, 0)) + bias
    for index in range(heads):
        columns = slice(index * HD, (index + 1) * HD)
        queries[:, columns] = turn_heads(lin[:, columns], cos, sin).astype(jnp.bfloat16)
    for copy in sent:
        copy.wait()
    totals[...] = jnp.zeros_like(totals)
    for sequence in range(seq_count):
        span = pl.ds(sequence * local_len, local_len)
        allowed = allowed_pairs(
            place, query_segments[span, :], key_segments[pl.ds(sequence, 1), :], local_len
        )
        keys = sequence_pairs(pairs, sequence, local_len, 0)
        values = sequence_pairs(pairs, sequence, local_len, 1)
        for index in range(heads):
            columns = pl.ds(index * HD, HD)
            scores = mm(queries[span, columns], keys, (1, 1)) * HD ** (-0.5)
            scores = jnp.where(allowed, scores, MASK_FILL)
            row_max = jnp.max(scores, axis=1, keepdims=True)
            exp_scores = jnp.exp(scores - row_max)
            row_total = jnp.sum(exp_scores, axis=1, keepdims=True)
            weights = (exp_scores / row_total).astype(jnp.bfloat16)
            totals[span, pl.ds(index, 1)] = row_max + jnp.log(row_total)
            mixed[span, columns] = mm(weights, values, (1, 0)).astype(jnp.bfloat16)
    part[...] = mm(mixed[...], weight(q_width + 2 * HD, q_width), (1, 1)).astype(part.dtype)
    yield None
    log_total[...] = totals[...].T[: log_total.shape[0], :]
    if layer == 0:
        for other in range(1, LAYERS):
            yield None
            shard, gate, up = next_shards[3 * other - 3 : 3 * other]
            attention_shard(other, first_head, query_weight, kv_weight, out_weight, shard)
            split_pair(other, gate_up_weight, gate, up)


def attend_back(layer, seq_count, place, sems, ins, outs, scratch, part, out_grad, in_grad):
    sums, middle, base, table, normed, w_attention, cosine, sine = ins[:8]
    query_segments, key_segments, queries, pairs, log_total, mixed = ins[8:]
    lin_grad, middle_grad, gain_grad = outs
    mixed_grad, pair_grad, got = scratch
    grad = part
    rows = grad.shape[0]
    local_len = rows // seq_count
    q_width = queries.shape[1]
    heads = q_width // HD
    scale = HD ** (-0.5)
    yield [(0, 0), (1, 0)]

    def write(span, back):
        total = base[span, :].astype(jnp.float32) + back
        middle_grad[span, :] = total
        grad[span, :] = total.astype(grad.dtype)

    gain = table[pl.ds(2 * layer + 1, 1), :]
    normalize_back(rows, 64, middle, sums, gain, gain_grad, write)
    cos, sin = cosine[...], -sine[...]
    weight = lambda start, size: w_attention[:, :, pl.ds(start, size)].reshape(-1, size)
    w_out = weight(q_width + 2 * HD, q_width)
    mixed_grad[...] = mm(grad[...], w_out, (1, 0)).astype(jnp.bfloat16)
    totals = log_total[...]
    for sequence in range(seq_count):
        first = sequence * local_len
        span = pl.ds(first, local_len)
        keys = sequence_pairs(pairs, sequence, local_len, 0)
        values = sequence_pairs(pairs, sequence, local_len, 1)
        shape = (keys.shape[0], local_len)
        key = lax.broadcasted_iota(jnp.int32, shape, 0)
        query = place.ctx * local_len + lax.broadcasted_iota(jnp.int32, shape, 1)
        same = key_segments[:, pl.ds(sequence, 1)] == query_segments[:, span]
        allowed = jnp.logical_and(same, key <= query)
        key_grad = value_grad = None
        for index in range(heads):
            columns = pl.ds(index * HD, HD)
            query_rows = queries[span, columns]
            grad_rows = mixed_grad[span, columns]
            scores = mm(keys, query_rows, (1, 1)) * scale
            scores = jnp.where(allowed, scores, MASK_FILL)
            weights = jnp.exp(scores - totals[index : index + 1, first : first + local_len])
            weight_grads = mm(values, grad_rows, (1, 1))
            row_delta = jnp.sum(weights * weight_grads, axis=0, keepdims=True)
            score_grads = (weights * (weight_grads - row_delta)).astype(jnp.bfloat16)
            for_keys = mm(score_grads, query_rows, (1, 0))
            for_values = mm(weights.astype(jnp.bfloat16), grad_rows, (1, 0))
            key_grad = for_keys if key_grad is None else key_grad + for_keys
            value_grad = for_values if value_grad is None else value_grad + for_values
            query_grad = mm(score_grads, keys, (0, 0)) * scale
            lin_grad[span, columns] = turn_heads(
                query_grad, cosine[span, :], -sine[span, :]
            ).astype(jnp.bfloat16)
        pieces = (place.ctxs, local_len, HD)
        pair_grad[:, span, :HD] = (key_grad * scale).astype(jnp.bfloat16).reshape(pieces)
        pair_grad[:, span, HD:] = value_grad.astype(jnp.bfloat16).reshape(pieces)
    sent = []
    for step in range(1, place.ctxs):
        to = place.ctx_at(step)
        sent.append(sems.remote(pair_grad.at[to], got.at[step - 1], place.to_ctx(to)))
        sent[-1].start()
    yield [(0, 1), (1, 1)]
    product = mm(grad[...], mixed[...], (0, 0)).astype(out_grad.dtype)
    out_grad[...] = product.reshape(out_grad.shape)
    total = pair_grad[place.ctx].astype(jnp.float32)
    for step, copy in enumerate(sent):
        copy.wait()
        total = total + got[step].astype(jnp.float32)
    lin_grad[:, pl.ds(q_width, HD)] = turn_heads(total[:, :HD], cos, sin).astype(jnp.bfloat16)
    lin_grad[:, pl.ds(q_width + HD, HD)] = total[:, HD:].astype(jnp.bfloat16)
    part[...] = mm(lin_grad[...], weight(0, q_width + 2 * HD), (1, 1)).astype(part.dtype)
    yield None
    product = mm(normed[...], lin_grad[...], (0, 0)).astype(in_grad.dtype)
    in_grad[...] = product.reshape(in_grad.shape)


def finish_kernel(sizes, *refs):
    refs = list(refs)
    gain_grads = take(refs, 2 * LAYERS)
    lin_grads = take(refs, LAYERS)
    (in_grad,) = take(refs, 1)
    sums, kv_parts, kv_rows, rows, send, recv = refs
    place = Place(sizes)
    sems = Sems(send, recv)
    width = in_grad.shape[1]
    q_width = width - 2 * HD
    group = H // KV
    heads = q_width // HD
    dps, ctxs, tensors = sizes
    line, plane = place.line_partners(), place.plane_partners()
    barrier = pltpu.get_barrier_semaphore()
    for device in line + plane:
        pl.semaphore_signal(barrier, inc=1, device_id=device, device_id_type=MESH)

    me = place.tensor
    here = place.dp * ctxs + place.ctx
    kv_rows[me] = jnp.zeros(kv_rows.shape[1:], jnp.float32)
    rows[here] = jnp.zeros(rows.shape[1:], jnp.float32)
    kv_parts[me] = in_grad[:, q_width:].astype(kv_parts.dtype)
    for layer in range(LAYERS):
        bias = jnp.sum(lin_grads[layer][...].astype(jnp.float32), axis=0, keepdims=True)
        kv_rows[me, pl.ds(layer, 1), :] = bias[:, q_width:]
        rows[here, pl.ds(2 * LAYERS + layer, 1), pl.ds(0, q_width)] = bias[:, :q_width]
    for index, gain in enumerate(gain_grads):
        rows[here, pl.ds(index, 1), :] = gain[...]
    pl.semaphore_wait(barrier, len(line) + len(plane))

    big = [sems.remote(kv_parts.at[me], kv_parts.at[me], device) for device in line]
    first = [sems.remote(kv_rows.at[me], kv_rows.at[me], device) for device in line]
    for copy in first + big:
        copy.start()
    for copy in first:
        copy.wait()
    for head in range(KV):
        owners = [t for t in range(tensors) if t * heads // group == head]
        total = sum(kv_rows[t, pl.ds(0, LAYERS), :] for t in owners)
        span = pl.ds(3 * LAYERS, LAYERS)
        rows[here, span, pl.ds(head * HD, HD)] = total[:, :HD]
        rows[here, span, pl.ds((KV + head) * HD, HD)] = total[:, HD:]
    second = [sems.remote(rows.at[here], rows.at[here], device) for device in plane]
    for copy in second:
        copy.start()
    for copy in second:
        copy.wait()
    total = rows[0]
    for index in range(1, dps * ctxs):
        total = total + rows[index]
    sums[...] = total
    for copy in big:
        copy.wait()


def finish(sizes, number, gain_grads, lin_grads, in_grad):
    dps, ctxs, tensors = sizes
    in_vmem = pl.BlockSpec(memory_space=pltpu.VMEM)
    args = (*[gain[None] for gain in gain_grads], *lin_grads, in_grad)
    height, width = -(-4 * LAYERS // 8) * 8, gain_grads[0].shape[0]
    count = 2 * (tensors - 1) + dps * ctxs - 1
    return pl.pallas_call(
        functools.partial(finish_kernel, sizes),
        out_shape=[
            jax.ShapeDtypeStruct((height, width), jnp.float32),
            jax.ShapeDtypeStruct((tensors, in_grad.shape[0], 2 * HD), jnp.bfloat16),
        ],
        in_specs=[in_vmem] * len(args),
        out_specs=[in_vmem] * 2,
        scratch_shapes=[
            pltpu.VMEM((tensors, 8, 2 * HD), jnp.float32),
            pltpu.VMEM((dps * ctxs, height, width), jnp.float32),
            pltpu.SemaphoreType.DMA((count,)),
            pltpu.SemaphoreType.DMA((count,)),
        ],
        compiler_params=pltpu.CompilerParams(
            collective_id=number, has_side_effects=True, vmem_limit_bytes=32 << 20
        ),
        name="finish",
    )(*args)


def adam_update(weight, gradient, first_old, second_old, decayed, step_rate):
    first_new = beta_first * first_old + (1.0 - beta_first) * gradient
    second_new = beta_second * second_old + (1.0 - beta_second) * gradient * gradient
    mean_hat = first_new / (1.0 - beta_first**adam_step)
    square_hat = second_new / (1.0 - beta_second**adam_step)
    new_weight = weight - step_rate * (
        mean_hat / (jnp.sqrt(square_hat) + adam_eps) + decayed * decay_rate * weight
    )
    return (first_new, second_new, new_weight)


def pair_adam_block(step_rate, weight, first, second, *rest):
    grads, outs = rest[: 2 * LAYERS], rest[2 * LAYERS :]
    for layer in range(LAYERS):

        @pl.when(pl.program_id(0) == layer)
        def _():
            gate, up = grads[2 * layer], grads[2 * layer + 1]
            grad = jnp.stack([gate[...], up[...]], axis=1)[None]
            moved = adam_update(
                weight[...].astype(jnp.float32), grad, first[...], second[...], 1.0, step_rate
            )
            for out, value in zip(outs, (grad, *moved)):
                out[...] = value


def pair_adam(weight, first, second, grads, step_rate):
    layers, rows, _, columns = weight.shape
    size = rows // (4 if rows % 64 == 0 else 3)
    last = rows // size - 1
    block = pl.BlockSpec((1, size, 2, columns), lambda layer, i: (layer, i, 0, 0))

    def grad_block(own):
        at = lambda layer, i: (jnp.where(layer == own, i, jnp.where(layer < own, 0, last)), 0)
        return pl.BlockSpec((size, columns), at)

    return pl.pallas_call(
        functools.partial(pair_adam_block, step_rate),
        grid=(layers, rows // size),
        in_specs=[block] * 3 + [grad_block(own) for own in range(layers) for _ in range(2)],
        out_specs=[block] * 4,
        out_shape=[jax.ShapeDtypeStruct(weight.shape, jnp.float32)] * 4,
        compiler_params=pltpu.CompilerParams(vmem_limit_bytes=56 << 20),
        name="pair_adam",
    )(weight, first, second, *grads)


TILE = 256
DOWN_TILES = 6


def in_width(block, width):
    column = pl.program_id(0) * TILE + lax.broadcasted_iota(jnp.int32, block.shape, 1)
    return jnp.where(column < width, block, jnp.zeros_like(block))


def forward_tile(
    width, layer, x_in, sums, table, w_gate, w_up, w_down, middle, n2, gate_out, up_out, inner_out, part_out, total
):
    tile = pl.program_id(0)

    @pl.when(tile == 0)
    def _():
        def read(span):
            values = x_in[span, :].astype(jnp.float32) + sums[span, :].astype(jnp.float32)
            middle[span, :] = values
            return values

        def write(span, values):
            n2[span, :] = values

        normalize(n2.shape[0], 64, read, table[pl.ds(2 * layer + 1, 1), :], write)

    gate = mm(n2[...], w_gate[...], (1, 0))
    up = mm(n2[...], w_up[...], (1, 0))
    gate_out[...] = gate
    up_out[...] = up
    inner = in_width(gate * jax.nn.sigmoid(gate) * up, width).astype(jnp.bfloat16)
    inner_out[...] = inner
    product = mm(inner, in_width(w_down[...], width), (1, 1))

    @pl.when(tile == 0)
    def _():
        total[...] = product

    @pl.when(tile > 0)
    def _():
        total[...] += product

    @pl.when(tile == pl.num_programs(0) - 1)
    def _():
        part_out[...] = total[...].astype(part_out.dtype)


def forward_ffn(layer, x_in, sums, table, w_gate, w_up, w_down):
    rows, model_width = x_in.shape
    width = w_gate.shape[1]
    whole = pl.BlockSpec((rows, model_width), lambda j: (0, 0))
    weight = pl.BlockSpec((model_width, TILE), lambda j: (0, j))
    units = pl.BlockSpec((rows, TILE), lambda j: (0, j))
    return pl.pallas_call(
        functools.partial(forward_tile, width, layer),
        grid=(pl.cdiv(width, TILE),),
        in_specs=[whole, whole, pl.BlockSpec(table.shape, lambda j: (0, 0)), weight, weight, weight],
        out_specs=[whole, whole, units, units, units, whole],
        out_shape=[
            jax.ShapeDtypeStruct((rows, model_width), jnp.float32),
            jax.ShapeDtypeStruct((rows, model_width), jnp.bfloat16),
            jax.ShapeDtypeStruct((rows, width), jnp.float32),
            jax.ShapeDtypeStruct((rows, width), jnp.float32),
            jax.ShapeDtypeStruct((rows, width), jnp.bfloat16),
            jax.ShapeDtypeStruct((rows, model_width), jnp.bfloat16),
        ],
        scratch_shapes=[pltpu.VMEM((rows, model_width), jnp.float32)],
        compiler_params=pltpu.CompilerParams(vmem_limit_bytes=56 << 20),
        name="forward_ffn",
    )(x_in, sums, table, w_gate, w_up, w_down)


def backward_tile(width, layer, *refs):
    refs = list(refs)
    if layer is None:
        grad = refs.pop(0)
    else:
        base, values, sums, table = take(refs, 4)
        *refs, grad_out, gain_grad, grad_t, n2_t, total, grad = refs
        refs += [grad_t, n2_t, total]

        @pl.when(pl.program_id(0) == 0)
        def _():
            def write(span, back):
                made = base[span, :] + back
                grad_out[span, :] = made
                grad[span, :] = made.astype(grad.dtype)

            gain = table[pl.ds(2 * layer, 1), :]
            normalize_back(grad.shape[0], 64, values, sums, gain, gain_grad, write)

    backward_work(width, grad, *refs)


def backward_work(
    width,
    grad,
    n2,
    gate_in,
    up_in,
    inner,
    w_gate,
    w_up,
    w_down,
    down_out,
    down_rest,
    gate_out,
    up_out,
    part_out,
    grad_t,
    n2_t,
    total,
):
    tile = pl.program_id(0)

    @pl.when(tile == 0)
    def _():
        grad_t[...] = grad[...].T
        n2_t[...] = n2[...].T

    gate = gate_in[...]
    slope = jax.nn.sigmoid(gate)
    grad_inner = mm(grad[...], w_down[...], (1, 0))
    down_grad = mm(grad_t[...], inner[...], (1, 0)).astype(down_out.dtype)

    @pl.when(tile < DOWN_TILES)
    def _():
        down_out[...] = down_grad

    @pl.when(tile >= DOWN_TILES)
    def _():
        down_rest[...] = down_grad

    grad_gate = grad_inner * up_in[...] * slope * (1.0 + gate * (1.0 - slope))
    grad_gate = in_width(grad_gate, width).astype(jnp.bfloat16)
    grad_up = in_width(grad_inner * gate * slope, width).astype(jnp.bfloat16)
    product = mm(grad_gate, in_width(w_gate[...], width), (1, 1))
    product += mm(grad_up, in_width(w_up[...], width), (1, 1))

    @pl.when(tile == 0)
    def _():
        total[...] = product

    @pl.when(tile > 0)
    def _():
        total[...] += product

    gate_out[...] = mm(n2_t[...], grad_gate, (1, 0)).astype(gate_out.dtype)
    up_out[...] = mm(n2_t[...], grad_up, (1, 0)).astype(up_out.dtype)

    @pl.when(tile == pl.num_programs(0) - 1)
    def _():
        part_out[...] = total[...].astype(part_out.dtype)


def backward_ffn(grad, n2, gate, up, inner, w_gate, w_up, w_down, layer=None):
    rows, model_width = n2.shape
    width = w_gate.shape[1]
    whole = pl.BlockSpec((rows, model_width), lambda j: (0, 0))
    weight = pl.BlockSpec((model_width, TILE), lambda j: (0, j))
    units = pl.BlockSpec((rows, TILE), lambda j: (0, j))
    like = lambda size: jax.ShapeDtypeStruct((model_width, size), jnp.bfloat16)
    cut = DOWN_TILES * TILE
    scratch = [
        pltpu.VMEM((model_width, rows), jnp.bfloat16),
        pltpu.VMEM((model_width, rows), jnp.bfloat16),
        pltpu.VMEM((rows, model_width), jnp.float32),
    ]
    grads, given, made, made_shapes = [grad], [whole], [], []
    if layer is not None:
        grads = grad
        table_block = pl.BlockSpec(grad[3].shape, lambda j: (0, 0))
        given = [whole, whole, whole, table_block]
        made = [whole, pl.BlockSpec((1, model_width), lambda j: (0, 0))]
        made_shapes = [
            jax.ShapeDtypeStruct((rows, model_width), jnp.float32),
            jax.ShapeDtypeStruct((1, model_width), jnp.float32),
        ]
        scratch.append(pltpu.VMEM((rows, model_width), jnp.bfloat16))
    before = pl.BlockSpec((model_width, TILE), lambda j: (0, jnp.minimum(j, DOWN_TILES - 1)))
    behind = pl.BlockSpec((model_width, TILE), lambda j: (0, jnp.maximum(j - DOWN_TILES, 0)))
    return pl.pallas_call(
        functools.partial(backward_tile, width, layer),
        grid=(pl.cdiv(width, TILE),),
        in_specs=given + [whole, units, units, units, weight, weight, weight],
        out_specs=[before, behind, weight, weight, whole] + made,
        out_shape=[
            like(cut),
            like(width - cut),
            like(width),
            like(width),
            jax.ShapeDtypeStruct((rows, model_width), jnp.bfloat16),
        ]
        + made_shapes,
        scratch_shapes=scratch,
        compiler_params=pltpu.CompilerParams(vmem_limit_bytes=56 << 20),
        name="backward_ffn",
    )(*grads, n2, gate, up, inner, w_gate, w_up, w_down)


def rotate(values, cosine, sine):
    half_width = values.shape[-1] // 2
    first_half = values[..., :half_width]
    second_half = values[..., half_width:]
    return jnp.concatenate(
        [first_half * cosine - second_half * sine, second_half * cosine + first_half * sine],
        axis=-1,
    )


def rotate_back(grad_rows, cosine, sine):
    return rotate(grad_rows, cosine, -sine)


def norm_back(values, gain, grad_rows):
    norm_scale = lax.rsqrt(jnp.mean(values * values, axis=-1, keepdims=True) + NORM_EPS)
    weighted = grad_rows * gain
    inner_mean = jnp.mean(weighted * values, axis=-1, keepdims=True)
    grad_values = (
        norm_scale * weighted - values * (norm_scale * norm_scale * norm_scale) * inner_mean
    )
    return (grad_values, jnp.sum(grad_rows * values * norm_scale, axis=0))


def local(
    sizes,
    hidden_in,
    segment_ids,
    out_grad,
    norm_gains,
    query_weight,
    query_bias,
    kv_weight,
    kv_bias,
    out_weight,
    gate_up_weight,
    down_weight,
    *moments,
):
    low = jnp.bfloat16
    wide = jnp.float32
    dps, ctxs, tensors = sizes
    n = dps * ctxs
    seq_count, local_len, model_width = hidden_in.shape
    seq_length = segment_ids.shape[1]
    row_count = seq_count * local_len
    shard_rows = query_weight.shape[1]
    heads_here = query_weight.shape[2] // HD
    q_width = heads_here * HD
    hidden_units = down_weight.shape[1]
    local_start = lax.axis_index("ctx") * local_len
    kv_head = lax.axis_index("tensor") * heads_here // (H // KV)
    score_scale = HD ** (-0.5)
    numbers = iter(range(1, 100))

    def move(**what):
        return transfer(sizes, next(numbers), **what)

    down_shards = down_weight.transpose(0, 2, 1)

    def after(array, *earlier):
        return lax.optimization_barrier((array, *earlier))[0]

    head_part, bias_part = query_bias.shape[2], kv_bias.shape[1]
    shard = lax.axis_index("dp") * ctxs + lax.axis_index("ctx")

    def placed(part, width):
        zeros = jnp.zeros((*part.shape[:-1], width), wide)
        return lax.dynamic_update_slice_in_dim(
            zeros, part.astype(wide), shard * part.shape[-1], part.ndim - 1
        )

    own_table = jnp.concatenate(
        [
            placed(norm_gains, model_width).reshape(2 * LAYERS, model_width),
            jnp.pad(
                placed(query_bias, HD).reshape(LAYERS, q_width),
                ((0, 0), (0, model_width - q_width)),
            ),
            jnp.pad(
                placed(kv_bias, 2 * KV * HD), ((0, 0), (0, model_width - 2 * KV * HD))
            ),
        ]
    )
    own_table = jnp.pad(own_table, ((0, -own_table.shape[0] % 8), (0, 0)))
    own_segments = lax.dynamic_slice_in_dim(segment_ids, local_start, local_len, 1)
    earlier = jnp.sum(
        (segment_ids[:, None, :] < own_segments[:, :, None]).astype(jnp.int32), axis=-1
    )
    token_index = local_start + jnp.arange(local_len, dtype=jnp.int32)
    position = (token_index[None, :] - earlier).astype(wide)
    frequency = ROPE_BASE ** (-jnp.arange(HD // 2, dtype=wide) / (HD // 2))
    angles = position[..., None] * frequency
    cosine = jnp.cos(angles).reshape(row_count, 1, HD // 2)
    sine = jnp.sin(angles).reshape(row_count, 1, HD // 2)
    cos_wide = jnp.concatenate([cosine[:, 0], cosine[:, 0]], axis=1)
    sin_wide = jnp.concatenate([-sine[:, 0], sine[:, 0]], axis=1)
    hidden = hidden_in.reshape(row_count, model_width)
    stored = []
    for layer in range(LAYERS):
        sides = [cos_wide, sin_wide, own_segments.reshape(row_count, 1), segment_ids]
        outputs = [
            jax.ShapeDtypeStruct((row_count, q_width), low),
            jax.ShapeDtypeStruct((ctxs, row_count, 2 * HD), low),
            jax.ShapeDtypeStruct((-(-heads_here // 8) * 8, row_count), wide),
            jax.ShapeDtypeStruct((row_count, q_width), low),
            jax.ShapeDtypeStruct((row_count, model_width), low),
        ]
        if layer == 0:
            unit_shard = jax.ShapeDtypeStruct((shard_rows, hidden_units), low)
            attention_shard = jax.ShapeDtypeStruct((shard_rows, 2 * q_width + 2 * HD), low)
            outputs.append(jax.ShapeDtypeStruct((n, *attention_shard.shape), low))
            outputs.append(jax.ShapeDtypeStruct(own_table.shape, wide))
            outputs += [attention_shard, unit_shard, unit_shard] * (LAYERS - 1)
            weights = [query_weight, kv_weight, out_weight.transpose(0, 2, 1), gate_up_weight]
            work = Work(
                functools.partial(attend, layer, seq_count),
                [hidden, own_table, *sides, *weights],
                outputs,
                [
                    pltpu.VMEM((n, *own_table.shape), wide),
                    pltpu.VMEM(attention_shard.shape, low),
                    pltpu.VMEM((row_count, HD), wide),
                ],
                n + gather_sems(sizes) + ctxs,
                jax.ShapeDtypeStruct((row_count, model_width), low),
                shards=[unit_shard, unit_shard],
                whole_plane=True,
            )
            total, *moved = move(
                work=work, gathers=[(down_shards, 0)], plan=((8, 14), (12, 18), (14, 99))
            )
            w_gate, w_up, down_weights = moved[:3]
            queries, pairs, log_total, mixed_low, normed, w_attention, table = moved[3:10]
            later_shards = moved[10:]
        else:
            outputs.append(jax.ShapeDtypeStruct((row_count, model_width), wide))
            work = Work(
                functools.partial(attend, layer, seq_count),
                [middle, total, table, w_attention, *sides],
                outputs,
                [pltpu.VMEM((row_count, HD), wide)],
                ctxs,
                jax.ShapeDtypeStruct((row_count, model_width), low),
            )
            total, w_gate, w_up, queries, pairs, log_total, mixed_low, normed, hidden = move(
                work=work,
                gathers=[(shard[None], 0) for shard in later_shards[3 * layer - 2 : 3 * layer]],
                plan=((8, 14), (12, 18)),
            )
        w_gate, w_up, w_down = [
            a.reshape(model_width, hidden_units) for a in (w_gate, w_up, down_weights)
        ]
        middle, normed_two, gate, up, inner_low, part = forward_ffn(
            layer, hidden, total, table, w_gate, w_up, w_down
        )
        stored.append(
            (
                hidden,
                normed,
                queries,
                pairs,
                log_total,
                mixed_low,
                middle,
                normed_two,
                gate,
                up,
                inner_low,
                w_attention,
                w_gate,
                w_up,
                w_down,
            )
        )
        if layer + 1 < LAYERS:
            total, w_attention, down_weights = move(
                z_sums=[part],
                gathers=[(later_shards[3 * layer][None], 0), (down_shards, layer + 1)],
                plan=((8, 15), (13, 18)),
            )
        else:
            last_part, half = part, row_count // 2
            last_first = lax.psum(last_part[:half], "tensor")

    def split(gradient):
        return gradient.astype(low).reshape(n, shard_rows, gradient.shape[1])

    grad_hidden = out_grad.reshape(row_count, model_width)
    total = None
    done = [{} for _ in range(LAYERS)]
    small_grads = [None] * LAYERS
    for layer in reversed(range(LAYERS)):
        (
            layer_input,
            normed,
            queries,
            pairs,
            log_total,
            mixed_low,
            middle,
            normed_two,
            gate,
            up,
            inner_low,
            w_attention,
            w_gate,
            w_up,
            w_down,
        ) = stored[layer]
        if layer + 1 == LAYERS:
            *ffn_grads, part = backward_ffn(
                grad_hidden, normed_two, gate, up, inner_low, w_gate, w_up, w_down
            )
        else:
            above = (grad_middle, above_input, total, table)
            *ffn_grads, part, grad_hidden, gain_grad = backward_ffn(
                above, normed_two, gate, up, inner_low, w_gate, w_up, w_down, layer + 1
            )
            small_grads[layer + 1].insert(0, gain_grad[0])
        down_first, down_rest, grad_gate_w, grad_up_w = (split(grad) for grad in ffn_grads)
        total, done[layer]["gate"], done[layer]["down_first"] = move(
            z_sums=[part], scatters=[grad_gate_w, down_first], plan=((2, 9), (3, 11))
        )
        if layer + 2 >= LAYERS:
            normed = after(normed, last_first if layer + 1 == LAYERS else last_rest)
        work = Work(
            functools.partial(attend_back, layer, seq_count),
            [
                total,
                middle,
                grad_hidden,
                table,
                normed,
                w_attention,
                cos_wide,
                sin_wide,
                own_segments.reshape(1, row_count),
                segment_ids.T,
                queries,
                pairs,
                log_total,
                mixed_low,
            ],
            [
                jax.ShapeDtypeStruct((row_count, q_width + 2 * HD), low),
                jax.ShapeDtypeStruct((row_count, model_width), wide),
                jax.ShapeDtypeStruct((1, model_width), wide),
            ],
            [
                pltpu.VMEM((row_count, q_width), low),
                pltpu.VMEM((ctxs, row_count, 2 * HD), low),
                pltpu.VMEM((max(1, ctxs - 1), row_count, 2 * HD), low),
            ],
            ctxs,
            jax.ShapeDtypeStruct((row_count, model_width), low),
            [
                jax.ShapeDtypeStruct((n, shard_rows, q_width), low),
                jax.ShapeDtypeStruct((n, shard_rows, q_width + 2 * HD), low),
            ],
        )
        extra = [kv_part] if layer + 1 < LAYERS else []
        total, *results, grad_lin, grad_middle, gain_grad = move(
            work=work,
            line_pieces=extra,
            scatters=[grad_up_w, down_rest],
            plan=((-1, 2), (-1, 4), (3, 13), (3, 13)),
        )
        for name, result in zip(("up", "down_rest", "out", "in"), results):
            done[layer][name] = result
        done[layer]["lin"] = grad_lin
        kv_part = done[layer]["in"][:, q_width:].astype(low)
        if extra:
            done[layer + 1]["kv"] = results[-1]
        small_grads[layer] = [gain_grad[0]]
        above_input = layer_input
        if layer + 1 == LAYERS:
            last_rest = lax.psum(after(last_part[half:], total), "tensor")

    back_one, grad_gain_one = norm_back(above_input.astype(wide), table[0], total.astype(wide))
    small_grads[0].insert(0, grad_gain_one)
    grad_hidden = grad_middle + back_one
    sums, kv_parts = finish(
        sizes,
        next(numbers),
        [gain for layer in range(LAYERS) for gain in small_grads[layer]],
        [done[layer]["lin"] for layer in range(LAYERS)],
        done[0]["in"],
    )
    done[0]["kv"] = kv_parts
    cut = lambda a, size: lax.dynamic_slice_in_dim(a, shard * size, size, a.ndim - 1)
    last_total = after(jnp.concatenate([last_first, last_rest]), sums)
    block_out = (stored[-1][6] + last_total.astype(wide)).astype(low)
    block_out = block_out.reshape(seq_count, local_len, model_width)
    input_grad = grad_hidden.reshape(seq_count, local_len, model_width)

    gains_grad = cut(sums[: 2 * LAYERS], shard_rows).reshape(LAYERS, 2, shard_rows)
    q_rows = sums[2 * LAYERS : 3 * LAYERS, :q_width].reshape(LAYERS, heads_here, HD)
    query_bias_grad = cut(q_rows, head_part)
    kv_bias_grad = cut(sums[3 * LAYERS : 4 * LAYERS, : 2 * KV * HD], bias_part)
    kv_weight_grad = []
    for layer in range(LAYERS):
        heads = []
        for head in range(KV):
            owners = [t for t in range(tensors) if t * heads_here // (H // KV) == head]
            heads.append(sum(done[layer]["kv"][t].astype(wide) for t in owners))
        kv_weight_grad.append(
            jnp.concatenate([a[:, :HD] for a in heads] + [a[:, HD:] for a in heads], axis=1)
        )
    kv_weight_grad = jnp.stack(kv_weight_grad)

    stack = lambda name, f=lambda a: a: jnp.stack([f(done[layer][name]) for layer in range(LAYERS)])
    down_grad = jnp.concatenate([stack("down_first"), stack("down_rest")], axis=2)
    grads = [
        gains_grad,
        stack("in", lambda a: a[:, :q_width]),
        query_bias_grad,
        kv_weight_grad,
        kv_bias_grad,
        stack("out", lambda a: a.T),
        None,
        down_grad.transpose(0, 2, 1),
    ]
    params = (
        norm_gains,
        query_weight,
        query_bias,
        kv_weight,
        kv_bias,
        out_weight,
        gate_up_weight,
        down_weight,
    )
    firsts, seconds = moments[:8], moments[8:]
    decays = (0.0, 1.0, 0.0, 1.0, 0.0, 1.0, 1.0, 1.0)
    rates = (0.5, 0.02, 0.5, 0.02, 0.5, 0.1, 0.02, 0.02)
    moved = []
    for i in range(8):
        if grads[i] is None:
            pair = [done[layer][name] for layer in range(LAYERS) for name in ("gate", "up")]
            grads[i], *new = pair_adam(params[i], firsts[i], seconds[i], pair, rates[i])
        else:
            new = adam_update(
                params[i].astype(wide), grads[i], firsts[i], seconds[i], decays[i], rates[i]
            )
        moved.append(new)
    return (
        block_out,
        input_grad,
        *grads,
        *[moved[i][0] for i in range(8)],
        *[moved[i][1] for i in range(8)],
        *[moved[i][2] for i in range(8)],
    )


def solution(mesh):
    params = (
        P(None, None, ("dp", "ctx")),
        P(None, ("dp", "ctx"), "tensor"),
        P(None, "tensor", ("dp", "ctx")),
        P(None, ("dp", "ctx"), None),
        P(None, ("dp", "ctx")),
        P(None, "tensor", ("dp", "ctx")),
        P(None, ("dp", "ctx"), None, "tensor"),
        P(None, "tensor", ("dp", "ctx")),
    )
    rows = P("dp", "ctx", None)
    sizes = (mesh.shape["dp"], mesh.shape["ctx"], mesh.shape["tensor"])
    return jax.shard_map(
        functools.partial(local, sizes),
        mesh=mesh,
        in_specs=(rows, P("dp", None), rows, *params, *params, *params),
        out_specs=(rows, rows, *params, *params, *params, *params),
        check_vma=False,
    )
```
